256 devices in a mesh: dp: 128 (over z, x, y), shard: 2 (over core).
Axes of the slice: x: 4, y: 4, z: 8, core: 2. Of those that a mesh axis runs over, the one named last changes fastest.
Arguments:
- features: bfloat16 [32768, 512], P(('dp', 'shard')), may hold values from -1.5 to 1.5
- norm_gain: float32 [512], replicated, may hold values from 0.25 to 1.75
- w_in: bfloat16 [512, 512], replicated, may hold values from -0.25 to 0.25
- w_out: bfloat16 [512, 512], replicated, may hold values from -1 to 1
- cotangent: bfloat16 [32768, 512], P(('dp', 'shard')), may hold values from -6 to 6
- positions: bfloat16 [3, 32768], P(None, ('dp', 'shard')), may hold values from 0 to 1
- crystal_of_atom: int32 [32768], P(('dp', 'shard')), may hold values from 0 to 7
- atom_owner: int32 [32768, 1], P(('dp', 'shard')), may hold values from 0 to 127; in each aligned block of 128 rows (0 to 127, 128 to 255, ...) at most 2 rows name the same one
- k_index: int32 [3, 131072], P(None, 'dp'), may hold values from -4 to 4
- k_crystal: int32 [131072], P('dp'), may hold values from 0 to 7
- damping: float32 [512], replicated, may hold values from 0.005 to 0.2
Outputs:
- updated: bfloat16 [32768, 512], P(('dp', 'shard'))
- grad_w_in: float32 [512, 512], replicated
- grad_w_out: float32 [512, 512], replicated
The draws below stay inside these ranges and needn't reach their ends.
Inputs may be any that keep to these rules, and one draw needn't show every extreme that they name: `atom_owner`: among the rows of one device, at most 2 atoms name the same packing group, a bound that some block reaches.
All inputs are finite; a program needn't handle non-finite values.
Results may differ from the reference program's by a relative error of at most 0.015.
Values may be sent and summed in bfloat16 or wider, within the bound.
No kernel may reach another device: no remote copies, remote signals or barrier semaphores. Data moves between devices by JAX's collectives and lax.ppermute only.
A program may use at most 64 MiB of HBM per device.

```python
import math
import jax
import jax.numpy as jnp
import numpy as np
from jax import lax

C = 512
ATOM_DEV = 128
K_DEV = 1024
CRY_DEV = 8
CAP = 2
SLOTS = 256
ATOMS = 32768
KTOT = 131072
N_DP = 128
N_SHARD = 2


def place_ends(drawn, rng, smallest, high):
    place = [jax.random.randint(jax.random.fold_in(rng, axis), (), 0, length) for axis, length in enumerate(drawn.shape)]
    main_axis = drawn.shape.index(max(drawn.shape))
    beside = place[:main_axis] + [(place[main_axis] + 1) % drawn.shape[main_axis]] + place[main_axis + 1:]
    return drawn.at[tuple(place)].set(smallest).at[tuple(beside)].set(high)


def levels(key, dims, split, smallest, largest):
    level = 1.0
    for dim, blocks in split:
        heights = jax.random.uniform(jax.random.fold_in(jax.random.fold_in(key, 6), dim), (blocks,), jnp.float32, smallest / len(split), largest / len(split))
        level = level * jnp.repeat(jnp.exp(heights), dims[dim] // blocks).reshape((-1,) + (1,) * (len(dims) - 1 - dim))
    return level


def deal_out(own_key, own, number, rows, number_of, top, reach, lean):
    order = jax.random.permutation(own_key, number_of)
    crowded, ordinary = portions_of(number_of, rows * top, reach, lean, True), portions_of(number_of, rows * top, reach, lean, False)
    places = jnp.arange(number_of)

    def named(tallies, offset_by):
        used = int((tallies > 0).sum())
        fixed = max(1, used // 4)
        moved = fixed + (places - fixed + offset_by * (used - fixed)) % max(1, number_of - fixed)
        return jnp.zeros((number_of,), jnp.int32).at[order[jnp.where(places < fixed, places, moved)]].set(jnp.asarray(tallies, jnp.int32))

    tallies = jnp.where(number % 4 == 0, named(crowded, number // 4), named(ordinary, number - number // 4 - 1))
    mixed = jax.random.permutation(jax.random.fold_in(own, 3), number_of)
    donor, sink = mixed[0:number_of // 2 * 2:2], mixed[1:number_of // 2 * 2:2]
    room = jnp.minimum(tallies[donor] - 1, reach - tallies[sink]) // 2
    room = jnp.where((donor == order[0]) | (sink == order[0]) | (tallies[sink] == 0), 0, jnp.maximum(room, 0))
    moved = jax.random.randint(jax.random.fold_in(own, 4), (number_of // 2,), 0, 1 << 20) % (room + 1)
    tallies = tallies.at[donor].add(-moved).at[sink].add(moved)
    items = jnp.searchsorted(jnp.cumsum(tallies), jnp.arange(rows * top), side="right").astype(jnp.int32)
    listing = items.reshape(top, rows).T
    listing = listing[jax.random.permutation(jax.random.fold_in(own, 1), rows)]
    offset_by = jax.random.randint(jax.random.fold_in(own, 2), (rows, 1), 0, top)
    return jnp.take_along_axis(listing, (jnp.arange(top)[None, :] + offset_by) % top, axis=1)


def portions_of(count, total, bound, lean, full):
    weights = [(1 << 20) // math.isqrt(rank ** lean) + 1 for rank in range(1, count + 1)]
    largest = bound if full else min(bound, max(-(-total // count), total * weights[0] // sum(weights)))
    least = 1 if total - largest >= count - 1 else 0
    given, spare = [largest] + [least] * (count - 1), total - largest - least * (count - 1)
    while spare > 0:
        candidates = [i for i in range(1, count) if given[i] < largest] or [i for i in range(1, count) if given[i] < bound]
        whole, left = sum([weights[i] for i in candidates]), spare
        for i in candidates:
            addition = min(bound - given[i], max(1, left * weights[i] // whole), spare)
            given[i] = given[i] + addition
            spare = spare - addition
    return np.array(given)


def bell_draw(stream_key, shape, width, limit, pieces=(), kind=jnp.bfloat16):
    level = levels(stream_key, shape, pieces, -0.22, 0.18) if pieces else 1.0
    drawn = jax.random.normal(stream_key, shape, jnp.float32) * width * level
    return jnp.minimum(jnp.maximum(drawn, -limit), limit).astype(kind)


def setup_inputs(seed: int = 0) -> dict:
    key_of = jax.random.split(jax.random.key(seed), 12)
    features = bell_draw(key_of[0], (ATOMS, C), 0.25, 1.5, ((0, 256),))
    norm_gain = jnp.clip(1.0 + 0.15 * jax.random.normal(key_of[1], (C,), jnp.float32), 0.25, 1.75)
    w_in = bell_draw(key_of[2], (C, C), C ** -0.5, 0.25)
    w_out = bell_draw(key_of[3], (C, C), (C // 16) ** -0.5, 1.0)
    cotangent = bell_draw(key_of[4], (ATOMS, C), 1.0, 6.0, ((0, 256),))
    positions = jnp.clip(1.0 * jax.random.uniform(key_of[5], (3, ATOMS), jnp.float32) ** levels(key_of[5], (3, ATOMS), ((1, 256),), -0.2, 0.2), 0.0, 1.0).astype(jnp.bfloat16)
    crystal_of_atom = place_ends(jax.random.randint(key_of[6], (ATOMS,), 0, CRY_DEV), jax.random.fold_in(key_of[6], 1), 0, CRY_DEV - 1).astype(jnp.int32)
    atom_owner_keys = jax.random.split(jax.random.fold_in(key_of[7], 1), ATOMS // ATOM_DEV)
    atom_owner_turns = jax.random.permutation(jax.random.fold_in(key_of[7], 3), ATOMS // ATOM_DEV)
    atom_owner = jax.vmap(lambda own, number: deal_out(jax.random.fold_in(key_of[7], 2), own, number, ATOM_DEV, N_DP, 1, CAP, 2))(atom_owner_keys, atom_owner_turns).reshape((ATOMS, 1))
    k_index = place_ends(jax.random.randint(key_of[8], (3, KTOT), -4, 5), jax.random.fold_in(key_of[8], 1), -4, 4).astype(jnp.int32)
    k_crystal = place_ends(jax.random.randint(key_of[9], (KTOT,), 0, CRY_DEV), jax.random.fold_in(key_of[9], 1), 0, CRY_DEV - 1).astype(jnp.int32)
    damping = jnp.clip(jnp.exp(jax.random.uniform(key_of[10], (C,), jnp.float32, math.log(0.005), math.log(0.2))), 0.005, 0.2)
    return dict(features=features, norm_gain=norm_gain, w_in=w_in, w_out=w_out, cotangent=cotangent, positions=positions, crystal_of_atom=crystal_of_atom, atom_owner=atom_owner, k_index=k_index, k_crystal=k_crystal, damping=damping)


def phase_matrix(k_float, k_group, coords, crystal_ids):
    theta = 2.0 * math.pi * (k_float[0][:, None] * coords[0][None, :] + k_float[1][:, None] * coords[1][None, :] + k_float[2][:, None] * coords[2][None, :])
    matched = k_group[:, None] == crystal_ids[None, :]
    cosine = jnp.where(matched, jnp.cos(theta), 0.0).astype(jnp.bfloat16)
    sine = jnp.where(matched, jnp.sin(theta), 0.0).astype(jnp.bfloat16)
    return jnp.concatenate([cosine, sine], axis=0)

def reference(features, norm_gain, w_in, w_out, cotangent, positions, crystal_of_atom, atom_owner, k_index, k_crystal, damping):
    hidden = features.astype(jnp.float32)
    normed = (hidden * lax.rsqrt(lax.optimization_barrier(jnp.mean(hidden * hidden, axis=-1, keepdims=True)) + 1e-06) * norm_gain[None, :]).astype(jnp.bfloat16)
    owner_group = atom_owner[:, 0]
    devices_all = N_DP * N_SHARD
    owner_block = owner_group.reshape(devices_all, ATOM_DEV)
    owner_hits = (owner_block[:, :, None] == jnp.arange(N_DP, dtype=jnp.int32)[None, None, :]).astype(jnp.int32)
    slot_rank = lax.optimization_barrier(jnp.sum((jnp.cumsum(owner_hits, axis=1) - owner_hits) * owner_hits, axis=2)).reshape(-1)
    device_of = jnp.arange(ATOMS, dtype=jnp.int32) // ATOM_DEV
    shard_of = device_of % N_SHARD
    source_dp = device_of // N_SHARD
    slot_index = ((owner_group * N_SHARD + shard_of) * N_DP + source_dp) * CAP + slot_rank
    total = N_DP * N_SHARD * SLOTS
    recv_x = jnp.zeros((total, C), jnp.bfloat16).at[slot_index].set(normed).reshape(N_DP, N_SHARD, SLOTS, C)
    recv_g = jnp.zeros((total, C), jnp.bfloat16).at[slot_index].set(cotangent).reshape(N_DP, N_SHARD, SLOTS, C)
    recv_pos = jnp.zeros((3, total), jnp.float32).at[:, slot_index].set(positions.astype(jnp.float32))
    recv_pos = recv_pos.reshape(3, N_DP, N_SHARD, SLOTS).transpose(1, 2, 0, 3)
    recv_cry = jnp.zeros((total,), jnp.int32).at[slot_index].set(crystal_of_atom).reshape(N_DP, N_SHARD, SLOTS)
    k_float = k_index.astype(jnp.float32).reshape(3, N_DP, K_DEV).transpose(1, 0, 2)
    k_group = k_crystal.reshape(N_DP, K_DEV)
    scale_s = (SLOTS * N_SHARD / CRY_DEV) ** (-0.5)
    scale_m = (K_DEV / CRY_DEV) ** (-0.5)

    def one_group(items):
        xg, gg, pg, cg, kf, kg = items
        ksq = kf[0] * kf[0] + kf[1] * kf[1] + kf[2] * kf[2]
        filter_k = jnp.exp(-ksq[:, None] * damping[None, :]) / (1.0 + ksq[:, None])
        filter_two = jnp.concatenate([filter_k, filter_k], axis=0)
        phases = [phase_matrix(kf, kg, pg[m], cg[m]) for m in range(N_SHARD)]
        downs = [jnp.dot(xg[m], w_in, preferred_element_type=jnp.float32).astype(jnp.bfloat16) for m in range(N_SHARD)]
        structure = jnp.zeros((2 * K_DEV, C), jnp.float32)
        for m in range(N_SHARD):
            partial_sum = lax.optimization_barrier(jnp.dot(phases[m], downs[m], preferred_element_type=jnp.float32).astype(jnp.bfloat16))
            structure = structure + partial_sum.astype(jnp.float32)
        scaled = (structure * filter_two * scale_s).astype(jnp.bfloat16)
        messages = [(scale_m * jnp.dot(phases[m].T, scaled, preferred_element_type=jnp.float32)).astype(jnp.bfloat16) for m in range(N_SHARD)]
        changes = jnp.stack([jnp.dot(messages[m], w_out, preferred_element_type=jnp.float32).astype(jnp.bfloat16) for m in range(N_SHARD)])
        grad_msgs = [jnp.dot(gg[m], w_out.T, preferred_element_type=jnp.float32).astype(jnp.bfloat16) for m in range(N_SHARD)]
        back = jnp.zeros((2 * K_DEV, C), jnp.float32)
        for m in range(N_SHARD):
            partial_back = lax.optimization_barrier(jnp.dot(phases[m], grad_msgs[m], preferred_element_type=jnp.float32).astype(jnp.bfloat16))
            back = back + partial_back.astype(jnp.float32)
        back_scaled = (back * filter_two * scale_s).astype(jnp.bfloat16)
        grad_out = jnp.zeros((C, C), jnp.float32)
        grad_in = jnp.zeros((C, C), jnp.float32)
        for m in range(N_SHARD):
            grad_down = (scale_m * jnp.dot(phases[m].T, back_scaled, preferred_element_type=jnp.float32)).astype(jnp.bfloat16)
            grad_out = grad_out + jnp.dot(messages[m].T, gg[m], preferred_element_type=jnp.float32)
            grad_in = grad_in + jnp.dot(xg[m].T, grad_down, preferred_element_type=jnp.float32)
        return (changes, grad_out, grad_in)
    changes, grad_outs, grad_ins = lax.map(one_group, (recv_x, recv_g, recv_pos, recv_cry, k_float, k_group))
    change_rows = changes.reshape(total, C)[slot_index]
    updated = (hidden + change_rows.astype(jnp.float32)).astype(jnp.bfloat16)
    norm_factor = ATOMS ** (-0.5)
    grad_w_in = lax.optimization_barrier(jnp.sum(grad_ins, axis=0)) * norm_factor
    grad_w_out = lax.optimization_barrier(jnp.sum(grad_outs, axis=0)) * norm_factor
    return (updated, grad_w_in, grad_w_out)
```

```python
import functools
import math

import jax
import jax.numpy as jnp
from jax import lax
from jax.experimental import pallas as pl
from jax.experimental.pallas import tpu as pltpu
from jax.sharding import PartitionSpec as P

CRY_DEV = 8
BF = jnp.bfloat16
F32 = jnp.float32
VMEM_LIMIT = 48 * 1024 * 1024
META = 128

COS_POLY = (
    1.0,
    -19.73920440673828,
    64.93911743164062,
    -85.45014190673828,
    60.16762924194336,
    -25.967599868774414,
    6.528658390045166,
)
SIN_POLY = (
    6.283185005187988,
    -41.341590881347656,
    81.59994506835938,
    -76.61447143554688,
    41.3428840637207,
    -12.471243858337402,
)

VM = pl.BlockSpec(memory_space=pltpu.VMEM)
SM = pl.BlockSpec(memory_space=pltpu.SMEM)


def call(body, out_shape, inputs, scratch=(), specs=None):
    return pl.pallas_call(
        body,
        out_shape=out_shape,
        in_specs=specs if specs is not None else [VM] * len(inputs),
        out_specs=jax.tree.map(lambda _: VM, out_shape),
        scratch_shapes=list(scratch),
        compiler_params=pltpu.CompilerParams(vmem_limit_bytes=VMEM_LIMIT),
    )(*inputs)


def dot(a, b, ca, cb):
    return lax.dot_general(a, b, (((ca,), (cb,)), ((), ())), preferred_element_type=F32)


def prep_kernel(feat_ref, gain_ref, cot_ref, meta_ref, col_ref, row_ref, out_ref):
    rows = feat_ref.shape[0]
    peers = out_ref.shape[1]
    width = feat_ref.shape[1]
    hidden = feat_ref[...].astype(F32)
    normed = (
        hidden
        * lax.rsqrt(jnp.mean(hidden * hidden, axis=-1, keepdims=True) + 1e-06)
        * gain_ref[...]
    ).astype(BF)
    owner = row_ref[...]
    first = lax.broadcasted_iota(jnp.int32, (rows, rows), 0)
    second = lax.broadcasted_iota(jnp.int32, (rows, rows), 1)
    earlier = (col_ref[...] == owner) & (first < second)
    rank = jnp.sum(jnp.where(earlier, 1.0, 0.0), axis=0, keepdims=True)
    peer = lax.broadcasted_iota(jnp.int32, (peers, rows), 0)
    for r in range(2):
        place = jnp.where((owner == peer) & (rank == float(r)), 1.0, 0.0).astype(BF)
        out_ref[r, :, 0:width] = dot(place, normed, 1, 0).astype(BF)
        out_ref[r, :, width : 2 * width] = dot(place, cot_ref[...], 1, 0).astype(BF)
        out_ref[r, :, 2 * width : 2 * width + META] = dot(place, meta_ref[...], 1, 1).astype(BF)


def static_kernel(shard_ref, k_ref, damp_ref, w_in_ref, kmat_ref, filt_ref, w_in_t_ref, scale_s):
    half = filt_ref.shape[0]
    start = pl.multiple_of(shard_ref[0] * half, half)
    kf = k_ref[...].astype(F32)
    kmat_ref[...] = jnp.zeros(kmat_ref.shape, BF)
    kmat_ref[0:16, :] = jnp.concatenate([kf, jnp.zeros((13, kf.shape[1]), F32)], axis=0).astype(BF)
    ksq = kf[0:1] * kf[0:1] + kf[1:2] * kf[1:2] + kf[2:3] * kf[2:3]
    damp = damp_ref[pl.ds(start, half), :]
    scale = scale_s / (1.0 + ksq)
    step = 32

    def rows(i, carry):
        at = pl.multiple_of(i * step, step)
        d = damp_ref[pl.ds(pl.multiple_of(start + at, step), step), :]
        filt_ref[pl.ds(at, step), :] = jnp.exp(-(d * ksq)) * scale
        return carry

    lax.fori_loop(0, half // step, rows, 0)
    w_in_t_ref[...] = w_in_ref[:, pl.ds(start, half)].T


def main_kernel(
    shard_ref, own_ref, oth_ref, kmat_ref, kc_ref, filt_ref, w_in_t_ref, w_out_ref,
    msg_ref, grad_ref,
    turn_ref, phase_ref, stack_ref, scaled_ref, scale_m,
):
    slots = own_ref.shape[0]
    width = w_out_ref.shape[1]
    half = w_in_t_ref.shape[0]
    kcount = kc_ref.shape[1]
    start = pl.multiple_of(shard_ref[0] * half, half)
    w_out_half = w_out_ref[pl.ds(start, half), :]
    tile_rows, tile_cols = 16, 512
    for m, ref in enumerate((own_ref, oth_ref)):
        cols = slice(m * slots, (m + 1) * slots)
        turn_ref[cols, :] = dot(ref[:, 2 * width :], kmat_ref[...], 1, 0)
        stack_ref[0:half, cols] = dot(w_in_t_ref[...], ref[:, 0:width], 1, 1).astype(BF)
        stack_ref[half:, cols] = dot(w_out_half, ref[:, width : 2 * width], 1, 1).astype(BF)

        def tile(i, carry):
            at = pl.multiple_of(i * tile_rows, tile_rows)
            dst = pl.ds(pl.multiple_of(m * slots + at, tile_rows), tile_rows)
            crystal = ref[pl.ds(at, tile_rows), 2 * width :].astype(F32)[:, 3:4]
            for j in range(kcount // tile_cols):
                span = slice(j * tile_cols, (j + 1) * tile_cols)
                turn = turn_ref[dst, span]
                rest = turn - jnp.floor(turn + 0.5)
                square = rest * rest
                cosine = jnp.full(square.shape, COS_POLY[-1], F32)
                for c in COS_POLY[-2::-1]:
                    cosine = cosine * square + c
                sine = jnp.full(square.shape, SIN_POLY[-1], F32)
                for c in SIN_POLY[-2::-1]:
                    sine = sine * square + c
                matched = crystal == kc_ref[:, span]
                phase_ref[dst, span] = jnp.where(matched, cosine, 0.0).astype(BF)
                phase_ref[dst, kcount + j * tile_cols : kcount + (j + 1) * tile_cols] = jnp.where(
                    matched, sine * rest, 0.0
                ).astype(BF)
            return carry

        lax.fori_loop(0, slots // tile_rows, tile, 0)
    block = 512
    for j in range(2 * kcount // block):
        span = slice(j * block, (j + 1) * block)
        lo = (j * block) % kcount
        filt = filt_ref[:, lo : lo + block]
        for part in range(2):
            rows = slice(part * half, (part + 1) * half)
            structure = dot(stack_ref[rows, :], phase_ref[:, span], 1, 0)
            scaled_ref[rows, span] = (structure * filt).astype(BF)
    for part, first in ((0, width), (1, 0)):
        rows = slice(part * half, (part + 1) * half)
        back = (scale_m * dot(scaled_ref[rows, :], phase_ref[...], 1, 1)).astype(BF)
        if part == 0:
            msg_ref[...] = back
        total = dot(back[:, 0:slots], own_ref[:, first : first + width], 1, 0)
        total += dot(back[:, slots:], oth_ref[:, first : first + width], 1, 0)
        grad_ref[rows, :] = total.astype(BF)


def change_kernel(shard_ref, msg_ref, got_ref, w_out_ref, grad_ref, out_ref):
    half = msg_ref.shape[0]
    slots = msg_ref.shape[1]
    rows = out_ref.shape[1]
    mine = pl.multiple_of(shard_ref[0] * half, half)
    other = pl.multiple_of((1 - shard_ref[0]) * half, half)
    change = dot(msg_ref[...], w_out_ref[pl.ds(mine, half), :], 0, 0)
    change += dot(got_ref[...], w_out_ref[pl.ds(other, half), :], 0, 0)
    change = change.astype(BF)
    for r in range(slots // rows):
        out_ref[r] = change[r * rows : (r + 1) * rows]
    for r in range(grad_ref.shape[0] // rows):
        out_ref[slots // rows + r] = grad_ref[r * rows : (r + 1) * rows]


def sum_kernel(recv_ref, out_ref, norm_factor):
    for j in range(out_ref.shape[0]):
        total = jnp.sum(recv_ref[2 + j].astype(F32), axis=0, keepdims=True) * norm_factor
        out_ref[j] = jnp.broadcast_to(total.astype(BF), out_ref.shape[1:])


def update_kernel(feat_ref, recv_ref, col_ref, row_ref, out_ref):
    rows = feat_ref.shape[0]
    peers = recv_ref.shape[1]
    owner = col_ref[...]
    first = lax.broadcasted_iota(jnp.int32, (rows, rows), 0)
    second = lax.broadcasted_iota(jnp.int32, (rows, rows), 1)
    earlier = (owner == row_ref[...]) & (second < first)
    rank = jnp.sum(jnp.where(earlier, 1.0, 0.0), axis=1, keepdims=True)
    peer = lax.broadcasted_iota(jnp.int32, (rows, peers), 1)
    total = feat_ref[...].astype(F32)
    for r in range(2):
        pick = jnp.where((owner == peer) & (rank == float(r)), 1.0, 0.0).astype(BF)
        total += dot(pick, recv_ref[r], 1, 0)
    out_ref[...] = total.astype(BF)


def final_kernel(shard_ref, own_ref, oth_ref, grad_in_ref, grad_out_ref):
    half = own_ref.shape[1] * 2
    for ref, member in ((own_ref, shard_ref[0]), (oth_ref, 1 - shard_ref[0])):
        start = pl.multiple_of(member * half, half)
        out = jnp.concatenate([ref[0], ref[1]], axis=0).astype(F32)
        grad_out_ref[pl.ds(start, half), :] = out
        into = jnp.concatenate([ref[2], ref[3]], axis=0).astype(F32)
        grad_in_ref[:, pl.ds(start, half)] = into.T


def local(
    features,
    norm_gain,
    w_in,
    w_out,
    cotangent,
    positions,
    crystal_of_atom,
    atom_owner,
    k_index,
    k_crystal,
    damping,
):
    rows, width = features.shape
    groups = lax.axis_size("dp")
    members = lax.axis_size("shard")
    capacity = 2 * rows // groups
    slots = groups * capacity
    half = width // members
    kcount = k_index.shape[1]
    scale_s = (slots * members / CRY_DEV) ** (-0.5)
    scale_m = (kcount / CRY_DEV) ** (-0.5)
    norm_factor = (rows * groups * members) ** (-0.5)
    shard = lax.axis_index("shard").astype(jnp.int32).reshape(1)
    swap = [(0, 1), (1, 0)]

    meta = jnp.concatenate(
        [
            positions,
            crystal_of_atom.astype(BF)[None, :],
            jnp.zeros((META - 4, rows), BF),
        ],
        axis=0,
    )
    owner_row = atom_owner.reshape(1, rows)
    send = call(
        prep_kernel,
        jax.ShapeDtypeStruct((2, groups, 2 * width + META), BF),
        [features, norm_gain.reshape(1, width), cotangent, meta, atom_owner, owner_row],
    )
    recv = lax.all_to_all(send, "dp", split_axis=1, concat_axis=1, tiled=True)
    own = recv.reshape(slots, 2 * width + META)
    kmat, filt, w_in_t = call(
        functools.partial(static_kernel, scale_s=scale_s),
        (
            jax.ShapeDtypeStruct((META, kcount), BF),
            jax.ShapeDtypeStruct((half, kcount), F32),
            jax.ShapeDtypeStruct((half, width), BF),
        ),
        [shard, k_index, damping.reshape(width, 1), w_in],
        specs=[SM, VM, VM, VM],
    )
    other = lax.ppermute(own, "shard", swap)
    message, grads = call(
        functools.partial(main_kernel, scale_m=scale_m),
        (
            jax.ShapeDtypeStruct((half, 2 * slots), BF),
            jax.ShapeDtypeStruct((2 * half, width), BF),
        ),
        [shard, own, other, kmat, k_crystal.astype(F32).reshape(1, kcount), filt, w_in_t, w_out],
        scratch=[
            pltpu.VMEM((2 * slots, kcount), F32),
            pltpu.VMEM((2 * slots, 2 * kcount), BF),
            pltpu.VMEM((2 * half, 2 * slots), BF),
            pltpu.VMEM((2 * half, 2 * kcount), BF),
        ],
        specs=[SM] + [VM] * 7,
    )
    got = lax.ppermute(message[:, slots:], "shard", swap)
    back = call(
        change_kernel,
        jax.ShapeDtypeStruct((6, groups, width), BF),
        [shard, message[:, :slots], got, w_out, grads],
        specs=[SM] + [VM] * 4,
    )
    recv_back = lax.all_to_all(back, "dp", split_axis=1, concat_axis=1, tiled=True)
    share = call(
        functools.partial(sum_kernel, norm_factor=norm_factor),
        jax.ShapeDtypeStruct((4, groups, width), BF),
        [recv_back],
    )
    mine = lax.all_to_all(share, "dp", split_axis=1, concat_axis=1, tiled=True)
    updated = call(
        update_kernel,
        jax.ShapeDtypeStruct((rows, width), BF),
        [features, recv_back, atom_owner, owner_row],
    )
    theirs = lax.ppermute(mine, "shard", swap)
    grad_w_in, grad_w_out = call(
        final_kernel,
        (jax.ShapeDtypeStruct((width, width), F32), jax.ShapeDtypeStruct((width, width), F32)),
        [shard, mine, theirs],
        specs=[SM, VM, VM],
    )
    return (updated, grad_w_in, grad_w_out)


def solution(mesh):
    in_specs = (
        P(("dp", "shard"), None),
        P(),
        P(),
        P(),
        P(("dp", "shard"), None),
        P(None, ("dp", "shard")),
        P(("dp", "shard")),
        P(("dp", "shard"), None),
        P(None, "dp"),
        P("dp"),
        P(),
    )
    out_specs = (P(("dp", "shard"), None), P(), P())
    return jax.shard_map(local, mesh=mesh, in_specs=in_specs, out_specs=out_specs, check_vma=False)
```

```python
import functools
import math

import jax
import jax.numpy as jnp
from jax import lax
from jax.experimental import pallas as pl
from jax.experimental.pallas import tpu as pltpu
from jax.sharding import Mesh
from jax.sharding import PartitionSpec as P

CRY_DEV = 8
BF = jnp.bfloat16
F32 = jnp.float32
VMEM_LIMIT = 48 * 1024 * 1024
META = 128

COS_POLY = (
    1.0,
    -19.73920440673828,
    64.93911743164062,
    -85.45014190673828,
    60.16762924194336,
    -25.967599868774414,
    6.528658390045166,
)
SIN_POLY = (
    6.283185005187988,
    -41.341590881347656,
    81.59994506835938,
    -76.61447143554688,
    41.3428840637207,
    -12.471243858337402,
)

VM = pl.BlockSpec(memory_space=pltpu.VMEM)
SM = pl.BlockSpec(memory_space=pltpu.SMEM)
HB = pl.BlockSpec(memory_space=pl.ANY)
PLANE = 16


def call(body, out_shape, inputs, scratch=(), specs=None, flops=1_000_000):
    return pl.pallas_call(
        body,
        out_shape=out_shape,
        in_specs=specs if specs is not None else [VM] * len(inputs),
        out_specs=jax.tree.map(lambda _: VM, out_shape),
        scratch_shapes=list(scratch),
        compiler_params=pltpu.CompilerParams(vmem_limit_bytes=VMEM_LIMIT),
        cost_estimate=pl.CostEstimate(flops=flops, bytes_accessed=1_000_000, transcendentals=0),
    )(*inputs)


def dot(a, b, ca, cb):
    return lax.dot_general(a, b, (((ca,), (cb,)), ((), ())), preferred_element_type=F32)


def plane_major(owner):
    return (owner & 15) * 8 + (owner >> 4)


def as_column(row):
    n = row.shape[1]
    diagonal = lax.broadcasted_iota(jnp.int32, (n, n), 0) == lax.broadcasted_iota(
        jnp.int32, (n, n), 1
    )
    return jnp.sum(jnp.where(diagonal, row, 0.0), axis=1, keepdims=True)


def fetch(pairs, sems):
    copies = [pltpu.make_async_copy(src, dst, sems.at[i]) for i, (src, dst) in enumerate(pairs)]
    for copy in copies:
        copy.start()
    for copy in copies:
        copy.wait()


def prep_kernel(
    feat_hbm, gain_hbm, cot_hbm, pos_hbm, cry_hbm, own_hbm, out_ref,
    feat_ref, gain_ref, cot_ref, pos_ref, cry_ref, own_ref, sems,
):
    fetch(
        (
            (own_hbm, own_ref),
            (feat_hbm, feat_ref),
            (cot_hbm, cot_ref),
            (gain_hbm, gain_ref),
            (pos_hbm, pos_ref),
            (cry_hbm, cry_ref),
        ),
        sems,
    )
    rows, width = feat_ref.shape
    slots = out_ref.shape[0]
    hidden = feat_ref[...].astype(F32)
    normed = (
        hidden
        * lax.rsqrt(jnp.mean(hidden * hidden, axis=-1, keepdims=True) + 1e-06)
        * gain_ref[...]
    ).astype(BF)
    owner = plane_major(own_ref[...]).astype(F32)
    first = lax.broadcasted_iota(jnp.int32, (rows, rows), 0)
    second = lax.broadcasted_iota(jnp.int32, (rows, rows), 1)
    earlier = (as_column(owner) == owner) & (first < second)
    rank = jnp.sum(jnp.where(earlier, 1.0, 0.0), axis=0, keepdims=True)
    slot = (owner * 2.0 + rank).astype(jnp.int32)
    place = jnp.where(
        slot == lax.broadcasted_iota(jnp.int32, (slots, rows), 0), 1.0, 0.0
    ).astype(BF)
    meta = jnp.concatenate(
        [
            pos_ref[...].astype(F32),
            cry_ref[...].astype(F32),
            jnp.zeros((META - 4, rows), F32),
        ],
        axis=0,
    ).astype(BF)
    out_ref[:, 0:width] = dot(place, normed, 1, 0).astype(BF)
    out_ref[:, width : 2 * width] = dot(place, cot_ref[...], 1, 0).astype(BF)
    out_ref[:, 2 * width : 2 * width + META] = dot(place, meta, 1, 1).astype(BF)


def static_kernel(shard_ref, k_ref, damp_ref, w_in_ref, kmat_ref, filt_ref, w_in_t_ref, scale_s):
    half = filt_ref.shape[0]
    start = pl.multiple_of(shard_ref[0] * half, half)
    kf = k_ref[...].astype(F32)
    kmat_ref[...] = jnp.zeros(kmat_ref.shape, BF)
    kmat_ref[0:16, :] = jnp.concatenate([kf, jnp.zeros((13, kf.shape[1]), F32)], axis=0).astype(BF)
    ksq = kf[0:1] * kf[0:1] + kf[1:2] * kf[1:2] + kf[2:3] * kf[2:3]
    damp = damp_ref[pl.ds(start, half), :]
    scale = scale_s / (1.0 + ksq)
    step = 32

    def rows(i, carry):
        at = pl.multiple_of(i * step, step)
        d = damp_ref[pl.ds(pl.multiple_of(start + at, step), step), :]
        filt_ref[pl.ds(at, step), :] = jnp.exp(-(d * ksq)) * scale
        return carry

    lax.fori_loop(0, half // step, rows, 0)
    w_in_t_ref[...] = w_in_ref[:, pl.ds(start, half)].T


def main_kernel(
    shard_ref, own_ref, oth_ref, kmat_ref, kc_ref, filt_ref, w_in_t_ref, w_out_ref,
    msg_ref, grad_ref,
    turn_ref, phase_ref, stack_ref, scaled_ref, scale_m,
):
    slots = own_ref.shape[0]
    width = w_out_ref.shape[1]
    half = w_in_t_ref.shape[0]
    kcount = kc_ref.shape[1]
    start = pl.multiple_of(shard_ref[0] * half, half)
    w_out_half = w_out_ref[pl.ds(start, half), :]
    tile_rows, tile_cols = 16, 512
    for m, ref in enumerate((own_ref, oth_ref)):
        cols = slice(m * slots, (m + 1) * slots)
        turn_ref[cols, :] = dot(ref[:, 2 * width :], kmat_ref[...], 1, 0)
        stack_ref[0:half, cols] = dot(w_in_t_ref[...], ref[:, 0:width], 1, 1).astype(BF)
        stack_ref[half:, cols] = dot(w_out_half, ref[:, width : 2 * width], 1, 1).astype(BF)

        def tile(i, carry):
            at = pl.multiple_of(i * tile_rows, tile_rows)
            dst = pl.ds(pl.multiple_of(m * slots + at, tile_rows), tile_rows)
            crystal = ref[pl.ds(at, tile_rows), 2 * width :].astype(F32)[:, 3:4]
            for j in range(kcount // tile_cols):
                span = slice(j * tile_cols, (j + 1) * tile_cols)
                turn = turn_ref[dst, span]
                rest = turn - jnp.floor(turn + 0.5)
                square = rest * rest
                cosine = jnp.full(square.shape, COS_POLY[-1], F32)
                for c in COS_POLY[-2::-1]:
                    cosine = cosine * square + c
                sine = jnp.full(square.shape, SIN_POLY[-1], F32)
                for c in SIN_POLY[-2::-1]:
                    sine = sine * square + c
                matched = crystal == kc_ref[:, span]
                phase_ref[dst, span] = jnp.where(matched, cosine, 0.0).astype(BF)
                phase_ref[dst, kcount + j * tile_cols : kcount + (j + 1) * tile_cols] = jnp.where(
                    matched, sine * rest, 0.0
                ).astype(BF)
            return carry

        lax.fori_loop(0, slots // tile_rows, tile, 0)
    block = 512
    for j in range(2 * kcount // block):
        span = slice(j * block, (j + 1) * block)
        lo = (j * block) % kcount
        filt = filt_ref[:, lo : lo + block]
        for part in range(2):
            rows = slice(part * half, (part + 1) * half)
            structure = dot(stack_ref[rows, :], phase_ref[:, span], 1, 0)
            scaled_ref[rows, span] = (structure * filt).astype(BF)
    for part, first in ((0, width), (1, 0)):
        rows = slice(part * half, (part + 1) * half)
        back = (scale_m * dot(scaled_ref[rows, :], phase_ref[...], 1, 1)).astype(BF)
        if part == 0:
            msg_ref[...] = back
        total = dot(back[:, 0:slots], own_ref[:, first : first + width], 1, 0)
        total += dot(back[:, slots:], oth_ref[:, first : first + width], 1, 0)
        grad_ref[rows, :] = total.astype(BF)


def change_kernel(shard_ref, msg_ref, got_ref, w_out_ref, grad_ref, out_ref):
    half = msg_ref.shape[0]
    mine = pl.multiple_of(shard_ref[0] * half, half)
    other = pl.multiple_of((1 - shard_ref[0]) * half, half)
    change = dot(msg_ref[...], w_out_ref[pl.ds(mine, half), :], 0, 0)
    change += dot(got_ref[...], w_out_ref[pl.ds(other, half), :], 0, 0)
    change = change.astype(BF)
    step = half // PLANE
    for q in range(PLANE):
        out_ref[q, 0:step] = change[q * step : (q + 1) * step]
        out_ref[q, step : 2 * step] = grad_ref[q * step : (q + 1) * step]
        out_ref[q, 2 * step :] = grad_ref[half + q * step : half + (q + 1) * step]


def plane_sum_kernel(recv_ref, out_ref):
    planes, block = out_ref.shape[0], recv_ref.shape[1] // 3
    slots = PLANE * block
    change = jnp.concatenate([recv_ref[q, 0:block] for q in range(PLANE)], axis=0)
    to = lax.broadcasted_iota(jnp.int32, (slots, slots), 0)
    of = lax.broadcasted_iota(jnp.int32, (slots, slots), 1)
    width = 2 * PLANE
    source = ((to & 31) >> 1) * block + (to >> 5) * 2 + (to & 1)
    move = jnp.where(source == of, 1.0, 0.0).astype(BF)
    change = dot(move, change, 1, 0).astype(BF)
    total = recv_ref[0, block:].astype(F32)
    for q in range(1, PLANE):
        total += recv_ref[q, block:].astype(F32)
    total = total.astype(BF)
    for z in range(planes):
        out_ref[z, 0:width] = change[z * width : (z + 1) * width]
        out_ref[z, width:] = total


def column_sum_kernel(recv_ref, out_ref, norm_factor):
    first = recv_ref.shape[1] - out_ref.shape[1]
    total = recv_ref[0, first:].astype(F32)
    for z in range(1, recv_ref.shape[0]):
        total += recv_ref[z, first:].astype(F32)
    total = (total * norm_factor).astype(BF)
    for q in range(out_ref.shape[0]):
        out_ref[q] = total


def update_kernel(feat_ref, recv_ref, own_ref, out_ref):
    rows = feat_ref.shape[0]
    planes = recv_ref.shape[0]
    width = 2 * PLANE
    owner_row = own_ref[...].astype(F32)
    owner = as_column(owner_row)
    first = lax.broadcasted_iota(jnp.int32, (rows, rows), 0)
    second = lax.broadcasted_iota(jnp.int32, (rows, rows), 1)
    earlier = (owner == owner_row) & (second < first)
    rank = jnp.sum(jnp.where(earlier, 1.0, 0.0), axis=1, keepdims=True)
    slot = (owner * 2.0 + rank).astype(jnp.int32)
    pick = jnp.where(
        slot == lax.broadcasted_iota(jnp.int32, (rows, planes * width), 1), 1.0, 0.0
    ).astype(BF)
    change = jnp.concatenate([recv_ref[z, 0:width] for z in range(planes)], axis=0)
    out_ref[...] = (feat_ref[...].astype(F32) + dot(pick, change, 1, 0)).astype(BF)


def final_kernel(shard_ref, own_ref, oth_ref, grad_in_ref, grad_out_ref):
    block = own_ref.shape[1] // 2
    half = PLANE * block
    for ref, member in ((own_ref, shard_ref[0]), (oth_ref, 1 - shard_ref[0])):
        start = pl.multiple_of(member * half, half)
        for q in range(PLANE):
            at = pl.ds(pl.multiple_of(start + q * block, block), block)
            grad_out_ref[at, :] = ref[q, 0:block].astype(F32)
        into = jnp.concatenate([ref[q, block:] for q in range(PLANE)], axis=0).astype(F32)
        grad_in_ref[:, pl.ds(start, half)] = into.T


def local(
    features,
    norm_gain,
    w_in,
    w_out,
    cotangent,
    positions,
    crystal_of_atom,
    atom_owner,
    k_index,
    k_crystal,
    damping,
):
    rows, width = features.shape
    around = ("x", "y", "z")
    plane = ("x", "y")
    groups = lax.axis_size(around)
    planes = lax.axis_size("z")
    members = lax.axis_size("shard")
    capacity = 2 * rows // groups
    slots = groups * capacity
    half = width // members
    kcount = k_index.shape[1]
    scale_s = (slots * members / CRY_DEV) ** (-0.5)
    scale_m = (kcount / CRY_DEV) ** (-0.5)
    norm_factor = (rows * groups * members) ** (-0.5)
    shard = lax.axis_index("shard").astype(jnp.int32).reshape(1)
    swap = [(0, 1), (1, 0)]

    owner_row = atom_owner.reshape(1, rows)
    packed = 2 * width + META
    operands = [
        features,
        norm_gain.reshape(1, width),
        cotangent,
        positions,
        crystal_of_atom.reshape(1, rows),
        owner_row,
    ]
    send = call(
        prep_kernel,
        jax.ShapeDtypeStruct((slots, packed), BF),
        operands,
        scratch=[pltpu.VMEM(a.shape, a.dtype) for a in operands]
        + [pltpu.SemaphoreType.DMA((len(operands),))],
        specs=[HB] * len(operands),
    )
    recv = lax.all_to_all(
        send.reshape(groups, capacity, packed), around, split_axis=0, concat_axis=0, tiled=True
    )
    own = recv.reshape(slots, packed)
    kmat, filt, w_in_t = call(
        functools.partial(static_kernel, scale_s=scale_s),
        (
            jax.ShapeDtypeStruct((META, kcount), BF),
            jax.ShapeDtypeStruct((half, kcount), F32),
            jax.ShapeDtypeStruct((half, width), BF),
        ),
        [shard, k_index, damping.reshape(width, 1), w_in],
        specs=[SM, VM, VM, VM],
        flops=4_000_000_000,
    )
    other = lax.ppermute(own, "shard", swap)
    message, grads = call(
        functools.partial(main_kernel, scale_m=scale_m),
        (
            jax.ShapeDtypeStruct((half, 2 * slots), BF),
            jax.ShapeDtypeStruct((2 * half, width), BF),
        ),
        [shard, own, other, kmat, k_crystal.astype(F32).reshape(1, kcount), filt, w_in_t, w_out],
        scratch=[
            pltpu.VMEM((2 * slots, kcount), F32),
            pltpu.VMEM((2 * slots, 2 * kcount), BF),
            pltpu.VMEM((2 * half, 2 * slots), BF),
            pltpu.VMEM((2 * half, 2 * kcount), BF),
        ],
        specs=[SM] + [VM] * 7,
    )
    got = lax.ppermute(message[:, slots:], "shard", swap)
    block = slots // PLANE
    back = call(
        change_kernel,
        jax.ShapeDtypeStruct((PLANE, 3 * block, width), BF),
        [shard, message[:, :slots], got, w_out, grads],
        specs=[SM] + [VM] * 4,
    )
    recv_plane = lax.all_to_all(back, plane, split_axis=0, concat_axis=0, tiled=True)
    column = call(
        plane_sum_kernel,
        jax.ShapeDtypeStruct((planes, slots // planes + 2 * block, width), BF),
        [recv_plane],
    )
    recv_column = lax.all_to_all(column, "z", split_axis=0, concat_axis=0, tiled=True)
    share = call(
        functools.partial(column_sum_kernel, norm_factor=norm_factor),
        jax.ShapeDtypeStruct((PLANE, 2 * block, width), BF),
        [recv_column],
    )
    mine = lax.all_to_all(share, plane, split_axis=0, concat_axis=0, tiled=True)
    updated = call(
        update_kernel,
        jax.ShapeDtypeStruct((rows, width), BF),
        [features, recv_column, owner_row],
        flops=4_000_000_000,
    )
    theirs = lax.ppermute(mine, "shard", swap)
    grad_w_in, grad_w_out = call(
        final_kernel,
        (jax.ShapeDtypeStruct((width, width), F32), jax.ShapeDtypeStruct((width, width), F32)),
        [shard, mine, theirs],
        specs=[SM, VM, VM],
    )
    return (updated, grad_w_in, grad_w_out)


def solution(mesh):
    axes = Mesh(
        mesh.devices.reshape(mesh.shape["dp"] // PLANE, 4, PLANE // 4, mesh.shape["shard"]),
        ("z", "x", "y", "shard"),
    )
    dp = ("z", "x", "y")
    every = (*dp, "shard")
    in_specs = (
        P(every, None),
        P(),
        P(),
        P(),
        P(every, None),
        P(None, every),
        P(every),
        P(every, None),
        P(None, dp),
        P(dp),
        P(),
    )
    out_specs = (P(every, None), P(), P())
    return jax.shard_map(local, mesh=axes, in_specs=in_specs, out_specs=out_specs, check_vma=False)
```

```python
import functools
import math

import jax
import jax.numpy as jnp
from jax import lax
from jax.experimental import pallas as pl
from jax.experimental.pallas import tpu as pltpu
from jax.sharding import Mesh
from jax.sharding import PartitionSpec as P

CRY_DEV = 8
BF = jnp.bfloat16
F32 = jnp.float32
VMEM_LIMIT = 24 * 1024 * 1024
FULL_VMEM = 63 * 1024 * 1024
META = 128

COS_POLY = (
    0.9999992251396179,
    -19.738981246948242,
    64.92865753173828,
    -85.27162170410156,
    58.79049301147461,
    -21.07110595703125,
)
SIN_POLY = (
    6.283185005187988,
    -41.341590881347656,
    81.59994506835938,
    -76.61447143554688,
    41.3428840637207,
    -12.471243858337402,
)

VM = pl.BlockSpec(memory_space=pltpu.VMEM)
SM = pl.BlockSpec(memory_space=pltpu.SMEM)
HB = pl.BlockSpec(memory_space=pltpu.MemorySpace.HBM)
PLANE = 16


def call(body, out_shape, inputs, scratch=(), specs=None, outs=None, flops=1_000_000, aliases=None,
         limit=VMEM_LIMIT):
    return pl.pallas_call(
        body,
        out_shape=out_shape,
        in_specs=specs if specs is not None else [VM] * len(inputs),
        out_specs=outs if outs is not None else jax.tree.map(lambda _: VM, out_shape),
        scratch_shapes=list(scratch),
        input_output_aliases=aliases or {},
        compiler_params=pltpu.CompilerParams(vmem_limit_bytes=limit),
        cost_estimate=pl.CostEstimate(flops=flops, bytes_accessed=1_000_000, transcendentals=0),
    )(*inputs)


def dot(a, b, ca, cb):
    return lax.dot_general(a, b, (((ca,), (cb,)), ((), ())), preferred_element_type=F32)


def plane_major(owner):
    return (owner & 15) * 8 + (owner >> 4)


def as_column(row):
    n = row.shape[1]
    diagonal = lax.broadcasted_iota(jnp.int32, (n, n), 0) == lax.broadcasted_iota(
        jnp.int32, (n, n), 1
    )
    return jnp.sum(jnp.where(diagonal, row, 0.0), axis=1, keepdims=True)


def fetch(pairs, sems):
    copies = [pltpu.make_async_copy(src, dst, sems.at[i]) for i, (src, dst) in enumerate(pairs)]
    for copy in copies:
        copy.start()
    for copy in copies:
        copy.wait()


def prep_kernel(
    feat_hbm, gain_hbm, cot_hbm, pos_hbm, cry_hbm, own_hbm, out_ref,
    feat_ref, gain_ref, cot_ref, pos_ref, cry_ref, own_ref, sems,
):
    fetch(
        (
            (own_hbm, own_ref),
            (feat_hbm, feat_ref),
            (cot_hbm, cot_ref),
            (gain_hbm, gain_ref),
            (pos_hbm, pos_ref),
            (cry_hbm, cry_ref),
        ),
        sems,
    )
    rows, width = feat_ref.shape
    slots = out_ref.shape[0] * out_ref.shape[1]
    hidden = feat_ref[...].astype(F32)
    normed = (
        hidden
        * lax.rsqrt(jnp.mean(hidden * hidden, axis=-1, keepdims=True) + 1e-06)
        * gain_ref[...]
    ).astype(BF)
    owner = plane_major(own_ref[...]).astype(F32)
    first = lax.broadcasted_iota(jnp.int32, (rows, rows), 0)
    second = lax.broadcasted_iota(jnp.int32, (rows, rows), 1)
    earlier = (as_column(owner) == owner) & (first < second)
    rank = jnp.sum(jnp.where(earlier, 1.0, 0.0), axis=0, keepdims=True)
    slot = (owner * 2.0 + rank).astype(jnp.int32)
    place = jnp.where(
        slot == lax.broadcasted_iota(jnp.int32, (slots, rows), 0), 1.0, 0.0
    ).astype(BF)
    meta = jnp.concatenate(
        [
            pos_ref[...].astype(F32),
            cry_ref[...].astype(F32),
            jnp.zeros((META - 4, rows), F32),
        ],
        axis=0,
    ).astype(BF)
    first = 0
    for part in (dot(place, normed, 1, 0), dot(place, cot_ref[...], 1, 0), dot(place, meta, 1, 1)):
        last = first + part.shape[1]
        out_ref[:, :, first:last] = part.reshape(slots // 2, 2, part.shape[1]).astype(BF)
        first = last


def static_kernel(
    shard_ref, k_ref, kc_ref, damp_ref, w_in_ref, kmat_ref, kcf_ref, filt_ref, w_in_t_ref, scale_s
):
    half = filt_ref.shape[0]
    start = pl.multiple_of(shard_ref[0] * half, half)
    kf = k_ref[...].astype(F32)
    kmat_ref[...] = jnp.zeros(kmat_ref.shape, BF)
    kmat_ref[0:16, :] = jnp.concatenate([kf, jnp.zeros((13, kf.shape[1]), F32)], axis=0).astype(BF)
    kcf_ref[...] = kc_ref[...].astype(F32)
    ksq = kf[0:1] * kf[0:1] + kf[1:2] * kf[1:2] + kf[2:3] * kf[2:3]
    scale = scale_s / (1.0 + ksq)
    step = 32

    def rows(i, carry):
        at = pl.multiple_of(i * step, step)
        d = damp_ref[pl.ds(pl.multiple_of(start + at, step), step), :]
        filt_ref[pl.ds(at, step), :] = jnp.exp(-(d * ksq)) * scale
        return carry

    lax.fori_loop(0, half // step, rows, 0)
    w_in_t_ref[...] = w_in_ref[:, pl.ds(start, half)].T


def fill_phase(rows_ref, kmat_ref, kc_ref, turn_ref, phase_ref):
    slots = rows_ref.shape[0]
    kcount = kc_ref.shape[1]
    first = rows_ref.shape[1] - META
    turn_ref[...] = dot(rows_ref[:, first:], kmat_ref[...], 1, 0)
    tile_rows, tile_cols = 16, 512

    def tile(i, carry):
        at = pl.ds(pl.multiple_of(i * tile_rows, tile_rows), tile_rows)
        crystal = rows_ref[at, first:].astype(F32)[:, 3:4]
        for j in range(kcount // tile_cols):
            span = slice(j * tile_cols, (j + 1) * tile_cols)
            turn = turn_ref[at, span]
            rest = turn - jnp.floor(turn + 0.5)
            square = rest * rest
            cosine = jnp.full(square.shape, COS_POLY[-1], F32)
            for c in COS_POLY[-2::-1]:
                cosine = cosine * square + c
            sine = jnp.full(square.shape, SIN_POLY[-1], F32)
            for c in SIN_POLY[-2::-1]:
                sine = sine * square + c
            matched = crystal == kc_ref[:, span]
            phase_ref[at, span] = jnp.where(matched, cosine, 0.0).astype(BF)
            phase_ref[at, kcount + j * tile_cols : kcount + (j + 1) * tile_cols] = jnp.where(
                matched, sine * rest, 0.0
            ).astype(BF)
        return carry

    lax.fori_loop(0, slots // tile_rows, tile, 0)


def fill_stack(rows_ref, w_in_t_ref, w_out_half, stack_ref):
    half = w_in_t_ref.shape[0]
    width = w_in_t_ref.shape[1]
    stack_ref[0:half, :] = dot(w_in_t_ref[...], rows_ref[:, 0:width], 1, 1).astype(BF)
    stack_ref[half:, :] = dot(w_out_half, rows_ref[:, width : 2 * width], 1, 1).astype(BF)


def half_of(ref, shard_ref, half):
    return ref[pl.ds(pl.multiple_of(shard_ref[0] * half, half), half), :]


def own_kernel(
    shard_ref, own_ref, kmat_ref, kc_ref, w_in_t_ref, w_out_ref, phase_ref, stack_ref, turn_ref
):
    fill_stack(own_ref, w_in_t_ref, half_of(w_out_ref, shard_ref, w_in_t_ref.shape[0]), stack_ref)
    fill_phase(own_ref, kmat_ref, kc_ref, turn_ref, phase_ref)


def there_and_back(stacks, phases, rows, filt_ref, scaled_ref, scale_m):
    kcount = filt_ref.shape[1]
    block = 512
    for j in range(2 * kcount // block):
        span = slice(j * block, (j + 1) * block)
        lo = (j * block) % kcount
        structure = dot(stacks[0][rows, :], phases[0][:, span], 1, 0)
        structure += dot(stacks[1][rows, :], phases[1][:, span], 1, 0)
        scaled_ref[:, span] = (structure * filt_ref[:, lo : lo + block]).astype(BF)
    return [
        (scale_m * dot(scaled_ref[...], phase[...], 1, 1)).astype(BF) for phase in phases
    ]


def forward_kernel(
    shard_ref, oth_ref, phase_own_ref, stack_own_ref, kmat_ref, kc_ref, filt_ref, w_in_t_ref,
    w_out_ref,
    phase_ref, stack_ref, msg_own_ref, msg_oth_ref,
    turn_ref, scaled_ref, scale_m,
):
    half = w_in_t_ref.shape[0]
    fill_stack(oth_ref, w_in_t_ref, half_of(w_out_ref, shard_ref, half), stack_ref)
    fill_phase(oth_ref, kmat_ref, kc_ref, turn_ref, phase_ref)
    msg_own_ref[...], msg_oth_ref[...] = there_and_back(
        (stack_own_ref, stack_ref), (phase_own_ref, phase_ref), slice(0, half), filt_ref,
        scaled_ref, scale_m,
    )


def backward_kernel(
    own_ref, oth_ref, phase_own_ref, phase_oth_ref, stack_own_ref, stack_oth_ref, msg_own_ref,
    msg_oth_ref, filt_ref, grad_ref, scaled_ref, scale_m,
):
    half = msg_own_ref.shape[0]
    width = grad_ref.shape[1]
    total = dot(msg_own_ref[...], own_ref[:, width : 2 * width], 1, 0)
    total += dot(msg_oth_ref[...], oth_ref[:, width : 2 * width], 1, 0)
    grad_ref[0:half, :] = total.astype(BF)
    back_own, back_oth = there_and_back(
        (stack_own_ref, stack_oth_ref), (phase_own_ref, phase_oth_ref), slice(half, 2 * half),
        filt_ref, scaled_ref, scale_m,
    )
    total = dot(back_own, own_ref[:, 0:width], 1, 0)
    total += dot(back_oth, oth_ref[:, 0:width], 1, 0)
    grad_ref[half:, :] = total.astype(BF)


def change_kernel(shard_ref, msg_ref, got_ref, w_out_ref, grad_ref, out_ref):
    half = msg_ref.shape[0]
    mine = pl.multiple_of(shard_ref[0] * half, half)
    other = pl.multiple_of((1 - shard_ref[0]) * half, half)
    change = dot(msg_ref[...], w_out_ref[pl.ds(mine, half), :], 0, 0)
    change += dot(got_ref[...], w_out_ref[pl.ds(other, half), :], 0, 0)
    change = change.astype(BF)
    step = half // PLANE
    for q in range(PLANE):
        out_ref[q, 0:step] = change[q * step : (q + 1) * step]
        out_ref[q, step : 2 * step] = grad_ref[q * step : (q + 1) * step]
        out_ref[q, 2 * step :] = grad_ref[half + q * step : half + (q + 1) * step]


def plane_sum_kernel(recv_ref, out_ref):
    planes, block = out_ref.shape[0], recv_ref.shape[1] // 3
    slots = PLANE * block
    change = jnp.concatenate([recv_ref[q, 0:block] for q in range(PLANE)], axis=0)
    to = lax.broadcasted_iota(jnp.int32, (slots, slots), 0)
    of = lax.broadcasted_iota(jnp.int32, (slots, slots), 1)
    width = 2 * PLANE
    source = ((to & 31) >> 1) * block + (to >> 5) * 2 + (to & 1)
    move = jnp.where(source == of, 1.0, 0.0).astype(BF)
    change = dot(move, change, 1, 0).astype(BF)
    total = recv_ref[0, block:].astype(F32)
    for q in range(1, PLANE):
        total += recv_ref[q, block:].astype(F32)
    total = total.astype(BF)
    for z in range(planes):
        out_ref[z, 0:width] = change[z * width : (z + 1) * width]
        out_ref[z, width:] = total


def column_sum_kernel(recv_ref, out_ref, norm_factor):
    first = recv_ref.shape[1] - out_ref.shape[1]
    total = recv_ref[0, first:].astype(F32)
    for z in range(1, recv_ref.shape[0]):
        total += recv_ref[z, first:].astype(F32)
    total = (total * norm_factor).astype(BF)
    for q in range(out_ref.shape[0]):
        out_ref[q] = total


def update_kernel(feat_ref, recv_ref, own_ref, out_ref):
    rows = feat_ref.shape[0]
    planes = recv_ref.shape[0]
    width = 2 * PLANE
    owner_row = own_ref[...].astype(F32)
    owner = as_column(owner_row)
    first = lax.broadcasted_iota(jnp.int32, (rows, rows), 0)
    second = lax.broadcasted_iota(jnp.int32, (rows, rows), 1)
    earlier = (owner == owner_row) & (second < first)
    rank = jnp.sum(jnp.where(earlier, 1.0, 0.0), axis=1, keepdims=True)
    slot = (owner * 2.0 + rank).astype(jnp.int32)
    pick = jnp.where(
        slot == lax.broadcasted_iota(jnp.int32, (rows, planes * width), 1), 1.0, 0.0
    ).astype(BF)
    change = jnp.concatenate([recv_ref[z, 0:width] for z in range(planes)], axis=0)
    out_ref[...] = (feat_ref[...].astype(F32) + dot(pick, change, 1, 0)).astype(BF)


def final_kernel(*refs, member):
    shard_ref, ref = refs[:2]
    grad_in_hbm, grad_out_hbm, in_ref, out_ref, sems = refs[-5:]
    block = ref.shape[1] // 2
    half = PLANE * block
    which = shard_ref[0] if member == 0 else 1 - shard_ref[0]
    start = pl.multiple_of(which * half, half)
    for q in range(PLANE):
        out_ref[q * block : (q + 1) * block, :] = ref[q, 0:block].astype(F32)
    rows = pltpu.make_async_copy(out_ref, grad_out_hbm.at[pl.ds(start, half), :], sems.at[0])
    rows.start()
    into = jnp.concatenate([ref[q, block:] for q in range(PLANE)], axis=0).astype(F32)
    in_ref[...] = into.T
    cols = pltpu.make_async_copy(in_ref, grad_in_hbm.at[:, pl.ds(start, half)], sems.at[1])
    cols.start()
    rows.wait()
    cols.wait()


def local(
    features,
    norm_gain,
    w_in,
    w_out,
    cotangent,
    positions,
    crystal_of_atom,
    atom_owner,
    k_index,
    k_crystal,
    damping,
):
    rows, width = features.shape
    around = ("x", "y", "z")
    plane = ("x", "y")
    groups = lax.axis_size(around)
    planes = lax.axis_size("z")
    members = lax.axis_size("shard")
    capacity = 2 * rows // groups
    slots = groups * capacity
    half = width // members
    kcount = k_index.shape[1]
    scale_s = (slots * members / CRY_DEV) ** (-0.5)
    scale_m = (kcount / CRY_DEV) ** (-0.5)
    norm_factor = (rows * groups * members) ** (-0.5)
    shard = lax.axis_index("shard").astype(jnp.int32).reshape(1)
    swap = [(0, 1), (1, 0)]

    owner_row = atom_owner.reshape(1, rows)
    packed = 2 * width + META
    operands = [
        features,
        norm_gain.reshape(1, width),
        cotangent,
        positions,
        crystal_of_atom.reshape(1, rows),
        owner_row,
    ]
    send = call(
        prep_kernel,
        jax.ShapeDtypeStruct((groups, capacity, packed), BF),
        operands,
        scratch=[pltpu.VMEM(a.shape, a.dtype) for a in operands]
        + [pltpu.SemaphoreType.DMA((len(operands),))],
        specs=[HB] * len(operands),
        limit=FULL_VMEM,
    )
    recv = lax.all_to_all(send, around, split_axis=0, concat_axis=0, tiled=True)
    own = recv.reshape(slots, packed)
    kmat, kc, filt, w_in_t = call(
        functools.partial(static_kernel, scale_s=scale_s),
        (
            jax.ShapeDtypeStruct((META, kcount), BF),
            jax.ShapeDtypeStruct((1, kcount), F32),
            jax.ShapeDtypeStruct((half, kcount), F32),
            jax.ShapeDtypeStruct((half, width), BF),
        ),
        [shard, k_index, k_crystal.reshape(1, kcount), damping.reshape(width, 1), w_in],
        specs=[SM, VM, VM, VM, VM],
        flops=4_000_000_000,
    )
    own, kmat, kc, filt, w_in_t = lax.optimization_barrier((own, kmat, kc, filt, w_in_t))
    other = lax.ppermute(own, "shard", swap)
    phase_shape = jax.ShapeDtypeStruct((slots, 2 * kcount), BF)
    stack_shape = jax.ShapeDtypeStruct((2 * half, slots), BF)
    message_shape = jax.ShapeDtypeStruct((half, slots), BF)
    turn = pltpu.VMEM((slots, kcount), F32)
    scaled = pltpu.VMEM((half, 2 * kcount), BF)
    phase_own, stack_own = call(
        own_kernel,
        (phase_shape, stack_shape),
        [shard, own, kmat, kc, w_in_t, w_out],
        scratch=[turn],
        specs=[SM] + [VM] * 5,
        flops=4_000_000_000,
    )
    phase_oth, stack_oth, message, message_oth = call(
        functools.partial(forward_kernel, scale_m=scale_m),
        (phase_shape, stack_shape, message_shape, message_shape),
        [shard, other, phase_own, stack_own, kmat, kc, filt, w_in_t, w_out],
        scratch=[turn, scaled],
        specs=[SM] + [VM] * 8,
    )
    got = lax.ppermute(message_oth, "shard", swap)
    grads = call(
        functools.partial(backward_kernel, scale_m=scale_m),
        jax.ShapeDtypeStruct((2 * half, width), BF),
        [own, other, phase_own, phase_oth, stack_own, stack_oth, message, message_oth, filt],
        scratch=[scaled],
        flops=4_000_000_000,
    )
    block = slots // PLANE
    back = call(
        change_kernel,
        jax.ShapeDtypeStruct((PLANE, 3 * block, width), BF),
        [shard, message, got, w_out, grads],
        specs=[SM] + [VM] * 4,
    )
    recv_plane = lax.all_to_all(back, plane, split_axis=0, concat_axis=0, tiled=True)
    column = call(
        plane_sum_kernel,
        jax.ShapeDtypeStruct((planes, slots // planes + 2 * block, width), BF),
        [recv_plane],
    )
    recv_column = lax.all_to_all(column, "z", split_axis=0, concat_axis=0, tiled=True)
    share = call(
        functools.partial(column_sum_kernel, norm_factor=norm_factor),
        jax.ShapeDtypeStruct((PLANE, 2 * block, width), BF),
        [recv_column],
    )
    mine = lax.all_to_all(share, plane, split_axis=0, concat_axis=0, tiled=True)
    updated = call(
        update_kernel,
        jax.ShapeDtypeStruct((rows, width), BF),
        [features, recv_column, owner_row],
        flops=4_000_000_000,
    )
    theirs = lax.ppermute(mine, "shard", swap)
    grads = (jax.ShapeDtypeStruct((width, width), F32),) * 2
    placing = dict(
        outs=(HB, HB),
        scratch=[
            pltpu.VMEM((width, half), F32),
            pltpu.VMEM((half, width), F32),
            pltpu.SemaphoreType.DMA((2,)),
        ],
    )
    first = call(
        functools.partial(final_kernel, member=0),
        grads,
        [shard, mine],
        specs=[SM, VM],
        flops=4_000_000_000,
        **placing,
    )
    grad_w_in, grad_w_out = call(
        functools.partial(final_kernel, member=1),
        grads,
        [shard, theirs, *first],
        specs=[SM, VM, HB, HB],
        aliases={2: 0, 3: 1},
        **placing,
    )
    return (updated, grad_w_in, grad_w_out)


def solution(mesh):
    axes = Mesh(
        mesh.devices.reshape(mesh.shape["dp"] // PLANE, 4, PLANE // 4, mesh.shape["shard"]),
        ("z", "x", "y", "shard"),
    )
    dp = ("z", "x", "y")
    every = (*dp, "shard")
    in_specs = (
        P(every, None),
        P(),
        P(),
        P(),
        P(every, None),
        P(None, every),
        P(every),
        P(every, None),
        P(None, dp),
        P(dp),
        P(),
    )
    out_specs = (P(every, None), P(), P())
    return jax.shard_map(local, mesh=axes, in_specs=in_specs, out_specs=out_specs, check_vma=False)
```

```python
import functools
import math

import jax
import jax.numpy as jnp
from jax import lax
from jax.experimental import pallas as pl
from jax.experimental.pallas import tpu as pltpu
from jax.sharding import PartitionSpec as P

CRY_DEV = 8
BF = jnp.bfloat16
F32 = jnp.float32
VMEM_LIMIT = 24 * 1024 * 1024
FULL_VMEM = 63 * 1024 * 1024
META = 128

COS_POLY = (
    0.9999992251396179,
    -19.738981246948242,
    64.92865753173828,
    -85.27162170410156,
    58.79049301147461,
    -21.07110595703125,
)
SIN_POLY = (
    6.283185005187988,
    -41.341590881347656,
    81.59994506835938,
    -76.61447143554688,
    41.3428840637207,
    -12.471243858337402,
)

VM = pl.BlockSpec(memory_space=pltpu.VMEM)
SM = pl.BlockSpec(memory_space=pltpu.SMEM)
HB = pl.BlockSpec(memory_space=pltpu.MemorySpace.HBM)
PLANE = 16


def place_of(owner, shard):
    first = jnp.where(shard == 0, owner & 15, (owner >> 4) * 2 + (owner & 1))
    second = jnp.where(shard == 0, owner >> 4, (owner >> 1) & 7)
    return first, second


def hop_sets():
    every = [(z, x, y) for z in range(8) for x in range(4) for y in range(4)]

    def split(shard):
        if shard == 0:
            return {(x * 4 + y, z): (z, x, y) for z, x, y in every}
        return {(z * 2 + y % 2, x * 2 + y // 2): (z, x, y) for z, x, y in every}

    around, first, second = [], [], []
    for shard in range(2):
        at = {key: ((z * 4 + x) * 4 + y) * 2 + shard for key, (z, x, y) in split(shard).items()}
        around.append([at[i, j] for i in range(PLANE) for j in range(8)])
        first += [[at[i, j] for i in range(PLANE)] for j in range(8)]
        second += [[at[i, j] for j in range(8)] for i in range(PLANE)]
    return around, first, second


def exchange(array, sets):
    return lax.all_to_all(
        array,
        ("dp", "shard"),
        split_axis=0,
        concat_axis=0,
        axis_index_groups=sets,
        tiled=True,
    )


def call(body, out_shape, inputs, scratch=(), specs=None, outs=None, flops=1_000_000, aliases=None,
         limit=VMEM_LIMIT):
    return pl.pallas_call(
        body,
        out_shape=out_shape,
        in_specs=specs if specs is not None else [VM] * len(inputs),
        out_specs=outs if outs is not None else jax.tree.map(lambda _: VM, out_shape),
        scratch_shapes=list(scratch),
        input_output_aliases=aliases or {},
        compiler_params=pltpu.CompilerParams(vmem_limit_bytes=limit),
        cost_estimate=pl.CostEstimate(flops=flops, bytes_accessed=1_000_000, transcendentals=0),
    )(*inputs)


def dot(a, b, ca, cb):
    return lax.dot_general(a, b, (((ca,), (cb,)), ((), ())), preferred_element_type=F32)


def as_column(row):
    n = row.shape[1]
    diagonal = lax.broadcasted_iota(jnp.int32, (n, n), 0) == lax.broadcasted_iota(
        jnp.int32, (n, n), 1
    )
    return jnp.sum(jnp.where(diagonal, row, 0.0), axis=1, keepdims=True)


def fetch(pairs, sems):
    copies = [pltpu.make_async_copy(src, dst, sems.at[i]) for i, (src, dst) in enumerate(pairs)]
    for copy in copies:
        copy.start()
    for copy in copies:
        copy.wait()


def prep_kernel(
    shard_ref, feat_hbm, gain_hbm, cot_hbm, pos_hbm, cry_hbm, own_hbm, out_ref,
    feat_ref, gain_ref, cot_ref, pos_ref, cry_ref, own_ref, sems,
):
    fetch(
        (
            (own_hbm, own_ref),
            (feat_hbm, feat_ref),
            (cot_hbm, cot_ref),
            (gain_hbm, gain_ref),
            (pos_hbm, pos_ref),
            (cry_hbm, cry_ref),
        ),
        sems,
    )
    rows, width = feat_ref.shape
    slots = out_ref.shape[0] * out_ref.shape[1]
    hidden = feat_ref[...].astype(F32)
    normed = (
        hidden
        * lax.rsqrt(jnp.mean(hidden * hidden, axis=-1, keepdims=True) + 1e-06)
        * gain_ref[...]
    ).astype(BF)
    owner = own_ref[...].astype(F32)
    first = lax.broadcasted_iota(jnp.int32, (rows, rows), 0)
    second = lax.broadcasted_iota(jnp.int32, (rows, rows), 1)
    earlier = (as_column(owner) == owner) & (first < second)
    rank = jnp.sum(jnp.where(earlier, 1.0, 0.0), axis=0, keepdims=True)
    first, second = place_of(own_ref[...], shard_ref[0])
    slot = (first * 8 + second) * 2 + rank.astype(jnp.int32)
    place = jnp.where(
        slot == lax.broadcasted_iota(jnp.int32, (slots, rows), 0), 1.0, 0.0
    ).astype(BF)
    meta = jnp.concatenate(
        [
            pos_ref[...].astype(F32),
            cry_ref[...].astype(F32),
            jnp.zeros((META - 4, rows), F32),
        ],
        axis=0,
    ).astype(BF)
    first = 0
    for part in (dot(place, normed, 1, 0), dot(place, cot_ref[...], 1, 0), dot(place, meta, 1, 1)):
        last = first + part.shape[1]
        out_ref[:, :, first:last] = part.reshape(slots // 2, 2, part.shape[1]).astype(BF)
        first = last


def static_kernel(
    shard_ref, k_ref, kc_ref, damp_ref, w_in_ref, kmat_ref, kcf_ref, filt_ref, w_in_t_ref, scale_s
):
    half = filt_ref.shape[0]
    start = pl.multiple_of(shard_ref[0] * half, half)
    kf = k_ref[...].astype(F32)
    kmat_ref[...] = jnp.zeros(kmat_ref.shape, BF)
    kmat_ref[0:16, :] = jnp.concatenate([kf, jnp.zeros((13, kf.shape[1]), F32)], axis=0).astype(BF)
    kcf_ref[...] = kc_ref[...].astype(F32)
    ksq = kf[0:1] * kf[0:1] + kf[1:2] * kf[1:2] + kf[2:3] * kf[2:3]
    scale = scale_s / (1.0 + ksq)
    step = 32

    def rows(i, carry):
        at = pl.multiple_of(i * step, step)
        d = damp_ref[pl.ds(pl.multiple_of(start + at, step), step), :]
        filt_ref[pl.ds(at, step), :] = jnp.exp(-(d * ksq)) * scale
        return carry

    lax.fori_loop(0, half // step, rows, 0)
    w_in_t_ref[...] = w_in_ref[:, pl.ds(start, half)].T


def fill_phase(rows_ref, kmat_ref, kc_ref, turn_ref, phase_ref):
    slots = rows_ref.shape[0]
    kcount = kc_ref.shape[1]
    first = rows_ref.shape[1] - META
    turn_ref[...] = dot(rows_ref[:, first:], kmat_ref[...], 1, 0)
    tile_rows, tile_cols = 16, 512

    def tile(i, carry):
        at = pl.ds(pl.multiple_of(i * tile_rows, tile_rows), tile_rows)
        crystal = rows_ref[at, first:].astype(F32)[:, 3:4]
        for j in range(kcount // tile_cols):
            span = slice(j * tile_cols, (j + 1) * tile_cols)
            turn = turn_ref[at, span]
            rest = turn - jnp.floor(turn + 0.5)
            square = rest * rest
            cosine = jnp.full(square.shape, COS_POLY[-1], F32)
            for c in COS_POLY[-2::-1]:
                cosine = cosine * square + c
            sine = jnp.full(square.shape, SIN_POLY[-1], F32)
            for c in SIN_POLY[-2::-1]:
                sine = sine * square + c
            matched = crystal == kc_ref[:, span]
            phase_ref[at, span] = jnp.where(matched, cosine, 0.0).astype(BF)
            phase_ref[at, kcount + j * tile_cols : kcount + (j + 1) * tile_cols] = jnp.where(
                matched, sine * rest, 0.0
            ).astype(BF)
        return carry

    lax.fori_loop(0, slots // tile_rows, tile, 0)


def fill_stack(rows_ref, w_in_t_ref, w_out_half, stack_ref):
    half = w_in_t_ref.shape[0]
    width = w_in_t_ref.shape[1]
    stack_ref[0:half, :] = dot(w_in_t_ref[...], rows_ref[:, 0:width], 1, 1).astype(BF)
    stack_ref[half:, :] = dot(w_out_half, rows_ref[:, width : 2 * width], 1, 1).astype(BF)


def half_of(ref, shard_ref, half):
    return ref[pl.ds(pl.multiple_of(shard_ref[0] * half, half), half), :]


def own_kernel(
    shard_ref, own_ref, kmat_ref, kc_ref, w_in_t_ref, w_out_ref, phase_ref, stack_ref, turn_ref
):
    fill_stack(own_ref, w_in_t_ref, half_of(w_out_ref, shard_ref, w_in_t_ref.shape[0]), stack_ref)
    fill_phase(own_ref, kmat_ref, kc_ref, turn_ref, phase_ref)


def there_and_back(stacks, phases, rows, filt_ref, scaled_ref, scale_m):
    kcount = filt_ref.shape[1]
    block = 512
    for j in range(2 * kcount // block):
        span = slice(j * block, (j + 1) * block)
        lo = (j * block) % kcount
        structure = dot(stacks[0][rows, :], phases[0][:, span], 1, 0)
        structure += dot(stacks[1][rows, :], phases[1][:, span], 1, 0)
        scaled_ref[:, span] = (structure * filt_ref[:, lo : lo + block]).astype(BF)
    return [
        (scale_m * dot(scaled_ref[...], phase[...], 1, 1)).astype(BF) for phase in phases
    ]


def forward_kernel(
    shard_ref, oth_ref, phase_own_ref, stack_own_ref, kmat_ref, kc_ref, filt_ref, w_in_t_ref,
    w_out_ref,
    phase_ref, stack_ref, msg_own_ref, msg_oth_ref,
    turn_ref, scaled_ref, scale_m,
):
    half = w_in_t_ref.shape[0]
    fill_stack(oth_ref, w_in_t_ref, half_of(w_out_ref, shard_ref, half), stack_ref)
    fill_phase(oth_ref, kmat_ref, kc_ref, turn_ref, phase_ref)
    msg_own_ref[...], msg_oth_ref[...] = there_and_back(
        (stack_own_ref, stack_ref), (phase_own_ref, phase_ref), slice(0, half), filt_ref,
        scaled_ref, scale_m,
    )


def backward_kernel(
    own_ref, oth_ref, phase_own_ref, phase_oth_ref, stack_own_ref, stack_oth_ref, msg_own_ref,
    msg_oth_ref, filt_ref, grad_ref, scaled_ref, scale_m,
):
    half = msg_own_ref.shape[0]
    width = grad_ref.shape[1]
    total = dot(msg_own_ref[...], own_ref[:, width : 2 * width], 1, 0)
    total += dot(msg_oth_ref[...], oth_ref[:, width : 2 * width], 1, 0)
    grad_ref[0:half, :] = total.astype(BF)
    back_own, back_oth = there_and_back(
        (stack_own_ref, stack_oth_ref), (phase_own_ref, phase_oth_ref), slice(half, 2 * half),
        filt_ref, scaled_ref, scale_m,
    )
    total = dot(back_own, own_ref[:, 0:width], 1, 0)
    total += dot(back_oth, oth_ref[:, 0:width], 1, 0)
    grad_ref[half:, :] = total.astype(BF)


def change_kernel(shard_ref, msg_ref, got_ref, w_out_ref, grad_ref, out_ref):
    half = msg_ref.shape[0]
    mine = pl.multiple_of(shard_ref[0] * half, half)
    other = pl.multiple_of((1 - shard_ref[0]) * half, half)
    change = dot(msg_ref[...], w_out_ref[pl.ds(mine, half), :], 0, 0)
    change += dot(got_ref[...], w_out_ref[pl.ds(other, half), :], 0, 0)
    change = change.astype(BF)
    step = half // PLANE
    for q in range(PLANE):
        out_ref[q, 0:step] = change[q * step : (q + 1) * step]
        out_ref[q, step : 2 * step] = grad_ref[q * step : (q + 1) * step]
        out_ref[q, 2 * step :] = grad_ref[half + q * step : half + (q + 1) * step]


def plane_sum_kernel(recv_ref, out_ref):
    planes, block = out_ref.shape[0], recv_ref.shape[1] // 3
    slots = PLANE * block
    change = jnp.concatenate([recv_ref[q, 0:block] for q in range(PLANE)], axis=0)
    to = lax.broadcasted_iota(jnp.int32, (slots, slots), 0)
    of = lax.broadcasted_iota(jnp.int32, (slots, slots), 1)
    width = 2 * PLANE
    source = ((to & 31) >> 1) * block + (to >> 5) * 2 + (to & 1)
    move = jnp.where(source == of, 1.0, 0.0).astype(BF)
    change = dot(move, change, 1, 0).astype(BF)
    total = recv_ref[0, block:].astype(F32)
    for q in range(1, PLANE):
        total += recv_ref[q, block:].astype(F32)
    total = total.astype(BF)
    for z in range(planes):
        out_ref[z, 0:width] = change[z * width : (z + 1) * width]
        out_ref[z, width:] = total


def column_sum_kernel(recv_ref, out_ref, norm_factor):
    first = recv_ref.shape[1] - out_ref.shape[1]
    total = recv_ref[0, first:].astype(F32)
    for z in range(1, recv_ref.shape[0]):
        total += recv_ref[z, first:].astype(F32)
    total = (total * norm_factor).astype(BF)
    for q in range(out_ref.shape[0]):
        out_ref[q] = total


def update_kernel(shard_ref, feat_ref, recv_ref, own_ref, out_ref):
    rows = feat_ref.shape[0]
    planes = recv_ref.shape[0]
    width = 2 * PLANE
    owner_row = own_ref[...].astype(F32)
    owner = as_column(owner_row)
    first = lax.broadcasted_iota(jnp.int32, (rows, rows), 0)
    second = lax.broadcasted_iota(jnp.int32, (rows, rows), 1)
    earlier = (owner == owner_row) & (second < first)
    rank = jnp.sum(jnp.where(earlier, 1.0, 0.0), axis=1, keepdims=True)
    first, second = place_of(owner.astype(jnp.int32), shard_ref[0])
    slot = (second * PLANE + first) * 2 + rank.astype(jnp.int32)
    pick = jnp.where(
        slot == lax.broadcasted_iota(jnp.int32, (rows, planes * width), 1), 1.0, 0.0
    ).astype(BF)
    change = jnp.concatenate([recv_ref[z, 0:width] for z in range(planes)], axis=0)
    out_ref[...] = (feat_ref[...].astype(F32) + dot(pick, change, 1, 0)).astype(BF)


def final_kernel(*refs, member):
    shard_ref, ref = refs[:2]
    grad_in_hbm, grad_out_hbm, in_ref, out_ref, sems = refs[-5:]
    block = ref.shape[1] // 2
    half = PLANE * block
    which = shard_ref[0] if member == 0 else 1 - shard_ref[0]
    start = pl.multiple_of(which * half, half)
    for q in range(PLANE):
        out_ref[q * block : (q + 1) * block, :] = ref[q, 0:block].astype(F32)
    rows = pltpu.make_async_copy(out_ref, grad_out_hbm.at[pl.ds(start, half), :], sems.at[0])
    rows.start()
    into = jnp.concatenate([ref[q, block:] for q in range(PLANE)], axis=0).astype(F32)
    in_ref[...] = into.T
    cols = pltpu.make_async_copy(in_ref, grad_in_hbm.at[:, pl.ds(start, half)], sems.at[1])
    cols.start()
    rows.wait()
    cols.wait()


def local(
    features,
    norm_gain,
    w_in,
    w_out,
    cotangent,
    positions,
    crystal_of_atom,
    atom_owner,
    k_index,
    k_crystal,
    damping,
):
    rows, width = features.shape
    around, plane, column_set = hop_sets()
    groups = lax.axis_size("dp")
    planes = groups // PLANE
    members = lax.axis_size("shard")
    capacity = 2 * rows // groups
    slots = groups * capacity
    half = width // members
    kcount = k_index.shape[1]
    scale_s = (slots * members / CRY_DEV) ** (-0.5)
    scale_m = (kcount / CRY_DEV) ** (-0.5)
    norm_factor = (rows * groups * members) ** (-0.5)
    shard = lax.axis_index("shard").astype(jnp.int32).reshape(1)
    swap = [(0, 1), (1, 0)]

    owner_row = atom_owner.reshape(1, rows)
    packed = 2 * width + META
    operands = [
        shard,
        features,
        norm_gain.reshape(1, width),
        cotangent,
        positions,
        crystal_of_atom.reshape(1, rows),
        owner_row,
    ]
    send = call(
        prep_kernel,
        jax.ShapeDtypeStruct((groups, capacity, packed), BF),
        operands,
        scratch=[pltpu.VMEM(a.shape, a.dtype) for a in operands[1:]]
        + [pltpu.SemaphoreType.DMA((len(operands) - 1,))],
        specs=[SM] + [HB] * (len(operands) - 1),
        limit=FULL_VMEM,
    )
    recv = exchange(send, around)
    own = recv.reshape(slots, packed)
    kmat, kc, filt, w_in_t = call(
        functools.partial(static_kernel, scale_s=scale_s),
        (
            jax.ShapeDtypeStruct((META, kcount), BF),
            jax.ShapeDtypeStruct((1, kcount), F32),
            jax.ShapeDtypeStruct((half, kcount), F32),
            jax.ShapeDtypeStruct((half, width), BF),
        ),
        [shard, k_index, k_crystal.reshape(1, kcount), damping.reshape(width, 1), w_in],
        specs=[SM, VM, VM, VM, VM],
        flops=4_000_000_000,
    )
    own, kmat, kc, filt, w_in_t = lax.optimization_barrier((own, kmat, kc, filt, w_in_t))
    other = lax.ppermute(own, "shard", swap)
    phase_shape = jax.ShapeDtypeStruct((slots, 2 * kcount), BF)
    stack_shape = jax.ShapeDtypeStruct((2 * half, slots), BF)
    message_shape = jax.ShapeDtypeStruct((half, slots), BF)
    turn = pltpu.VMEM((slots, kcount), F32)
    scaled = pltpu.VMEM((half, 2 * kcount), BF)
    phase_own, stack_own = call(
        own_kernel,
        (phase_shape, stack_shape),
        [shard, own, kmat, kc, w_in_t, w_out],
        scratch=[turn],
        specs=[SM] + [VM] * 5,
        flops=4_000_000_000,
    )
    phase_oth, stack_oth, message, message_oth = call(
        functools.partial(forward_kernel, scale_m=scale_m),
        (phase_shape, stack_shape, message_shape, message_shape),
        [shard, other, phase_own, stack_own, kmat, kc, filt, w_in_t, w_out],
        scratch=[turn, scaled],
        specs=[SM] + [VM] * 8,
    )
    got = lax.ppermute(message_oth, "shard", swap)
    grads = call(
        functools.partial(backward_kernel, scale_m=scale_m),
        jax.ShapeDtypeStruct((2 * half, width), BF),
        [own, other, phase_own, phase_oth, stack_own, stack_oth, message, message_oth, filt],
        scratch=[scaled],
        flops=4_000_000_000,
    )
    block = slots // PLANE
    back = call(
        change_kernel,
        jax.ShapeDtypeStruct((PLANE, 3 * block, width), BF),
        [shard, message, got, w_out, grads],
        specs=[SM] + [VM] * 4,
    )
    recv_plane = exchange(back, plane)
    column = call(
        plane_sum_kernel,
        jax.ShapeDtypeStruct((planes, slots // planes + 2 * block, width), BF),
        [recv_plane],
    )
    recv_column = exchange(column, column_set)
    share = call(
        functools.partial(column_sum_kernel, norm_factor=norm_factor),
        jax.ShapeDtypeStruct((PLANE, 2 * block, width), BF),
        [recv_column],
    )
    mine = exchange(share, plane)
    updated = call(
        update_kernel,
        jax.ShapeDtypeStruct((rows, width), BF),
        [shard, features, recv_column, owner_row],
        specs=[SM, VM, VM, VM],
        flops=4_000_000_000,
    )
    theirs = lax.ppermute(mine, "shard", swap)
    grads = (jax.ShapeDtypeStruct((width, width), F32),) * 2
    placing = dict(
        outs=(HB, HB),
        scratch=[
            pltpu.VMEM((width, half), F32),
            pltpu.VMEM((half, width), F32),
            pltpu.SemaphoreType.DMA((2,)),
        ],
    )
    first = call(
        functools.partial(final_kernel, member=0),
        grads,
        [shard, mine],
        specs=[SM, VM],
        flops=4_000_000_000,
        **placing,
    )
    grad_w_in, grad_w_out = call(
        functools.partial(final_kernel, member=1),
        grads,
        [shard, theirs, *first],
        specs=[SM, VM, HB, HB],
        aliases={2: 0, 3: 1},
        **placing,
    )
    return (updated, grad_w_in, grad_w_out)


def solution(mesh):
    every = ("dp", "shard")
    in_specs = (
        P(every, None),
        P(),
        P(),
        P(),
        P(every, None),
        P(None, every),
        P(every),
        P(every, None),
        P(None, "dp"),
        P("dp"),
        P(),
    )
    out_specs = (P(every, None), P(), P())
    return jax.shard_map(local, mesh=mesh, in_specs=in_specs, out_specs=out_specs, check_vma=False)
```

```python
import functools
import math

import jax
import jax.numpy as jnp
from jax import lax
from jax.experimental import pallas as pl
from jax.experimental.pallas import tpu as pltpu
from jax.sharding import PartitionSpec as P

CRY_DEV = 8
BF = jnp.bfloat16
F32 = jnp.float32
VMEM_LIMIT = 24 * 1024 * 1024
FULL_VMEM = 63 * 1024 * 1024
META = 128

COS_POLY = (
    1.4142135381698608,
    -6.978850841522217,
    5.739460468292236,
    -1.883557915687561,
    0.3106880187988281,
)
SIN_POLY = (
    4.442883014678955,
    -7.308245658874512,
    3.606354236602783,
    -0.8461116552352905,
    0.1098245158791542,
)

VM = pl.BlockSpec(memory_space=pltpu.VMEM)
SM = pl.BlockSpec(memory_space=pltpu.SMEM)
HB = pl.BlockSpec(memory_space=pltpu.MemorySpace.HBM)
PLANE = 16


def place_of(owner, shard):
    first = jnp.where(shard == 0, owner & 15, (owner >> 4) * 2 + (owner & 1))
    second = jnp.where(shard == 0, owner >> 4, (owner >> 1) & 7)
    return first, second


def hop_sets():
    every = [(z, x, y) for z in range(8) for x in range(4) for y in range(4)]

    def split(shard):
        if shard == 0:
            return {(x * 4 + y, z): (z, x, y) for z, x, y in every}
        return {(z * 2 + y % 2, x * 2 + y // 2): (z, x, y) for z, x, y in every}

    around, first, second = [], [], []
    for shard in range(2):
        at = {key: ((z * 4 + x) * 4 + y) * 2 + shard for key, (z, x, y) in split(shard).items()}
        around.append([at[i, j] for i in range(PLANE) for j in range(8)])
        first += [[at[i, j] for i in range(PLANE)] for j in range(8)]
        second += [[at[i, j] for j in range(8)] for i in range(PLANE)]
    return around, first, second


def exchange(array, sets):
    return lax.all_to_all(
        array,
        ("dp", "shard"),
        split_axis=0,
        concat_axis=0,
        axis_index_groups=sets,
        tiled=True,
    )


def call(body, out_shape, inputs, scratch=(), specs=None, outs=None, flops=1_000_000, aliases=None,
         limit=VMEM_LIMIT):
    return pl.pallas_call(
        body,
        out_shape=out_shape,
        in_specs=specs if specs is not None else [VM] * len(inputs),
        out_specs=outs if outs is not None else jax.tree.map(lambda _: VM, out_shape),
        scratch_shapes=list(scratch),
        input_output_aliases=aliases or {},
        compiler_params=pltpu.CompilerParams(vmem_limit_bytes=limit),
        cost_estimate=pl.CostEstimate(flops=flops, bytes_accessed=1_000_000, transcendentals=0),
    )(*inputs)


def dot(a, b, ca, cb):
    return lax.dot_general(a, b, (((ca,), (cb,)), ((), ())), preferred_element_type=F32)


def as_column(row):
    n = row.shape[1]
    diagonal = lax.broadcasted_iota(jnp.int32, (n, n), 0) == lax.broadcasted_iota(
        jnp.int32, (n, n), 1
    )
    return jnp.sum(jnp.where(diagonal, row, 0.0), axis=1, keepdims=True)


def prep_kernel(
    shard_ref, feat_hbm, gain_hbm, cot_hbm, pos_hbm, cry_hbm, own_hbm, out_hbm,
    feat_ref, gain_ref, cot_ref, pos_ref, cry_ref, own_ref, sems, stage_ref, out_sems,
):
    sources = (feat_hbm, gain_hbm, cot_hbm, pos_hbm, cry_hbm, own_hbm)
    targets = (feat_ref, gain_ref, cot_ref, pos_ref, cry_ref, own_ref)
    feat_in, gain_in, cot_in, pos_in, cry_in, own_in = copies = [
        pltpu.make_async_copy(src, dst, sems.at[i])
        for i, (src, dst) in enumerate(zip(sources, targets))
    ]
    for i in (5, 2, 0, 1, 3, 4):
        copies[i].start()
    rows, width = feat_ref.shape
    slots = out_hbm.shape[0] * out_hbm.shape[1]
    own_in.wait()
    owner = own_ref[...].astype(F32)
    first = lax.broadcasted_iota(jnp.int32, (rows, rows), 0)
    second = lax.broadcasted_iota(jnp.int32, (rows, rows), 1)
    earlier = (as_column(owner) == owner) & (first < second)
    rank = jnp.sum(jnp.where(earlier, 1.0, 0.0), axis=0, keepdims=True)
    first, second = place_of(own_ref[...], shard_ref[0])
    slot = (first * 8 + second) * 2 + rank.astype(jnp.int32)
    place = jnp.where(
        slot == lax.broadcasted_iota(jnp.int32, (slots, rows), 0), 1.0, 0.0
    ).astype(BF)
    sent = []

    def send(first, part):
        span = slice(first, first + part.shape[1])
        stage_ref[:, :, span] = part.reshape(slots // 2, 2, part.shape[1]).astype(BF)
        copy = pltpu.make_async_copy(
            stage_ref.at[:, :, span], out_hbm.at[:, :, span], out_sems.at[len(sent)]
        )
        copy.start()
        sent.append(copy)

    cot_in.wait()
    send(width, dot(place, cot_ref[...], 1, 0))
    feat_in.wait()
    gain_in.wait()
    hidden = feat_ref[...].astype(F32)
    normed = (
        hidden
        * lax.rsqrt(jnp.mean(hidden * hidden, axis=-1, keepdims=True) + 1e-06)
        * gain_ref[...]
    ).astype(BF)
    send(0, dot(place, normed, 1, 0))
    pos_in.wait()
    cry_in.wait()
    meta = jnp.concatenate(
        [
            pos_ref[...].astype(F32),
            cry_ref[...].astype(F32),
            jnp.zeros((META - 4, rows), F32),
        ],
        axis=0,
    ).astype(BF)
    send(2 * width, dot(place, meta, 1, 1))
    for copy in sent:
        copy.wait()


def static_kernel(
    shard_ref, k_ref, kc_ref, damp_ref, w_in_ref, kmat_ref, kone_ref, filt_ref, w_in_t_ref, scale_s
):
    half = filt_ref.shape[0]
    start = pl.multiple_of(shard_ref[0] * half, half)
    kf = k_ref[...].astype(F32)
    kmat_ref[...] = jnp.zeros(kmat_ref.shape, BF)
    kmat_ref[0:16, :] = jnp.concatenate([kf, jnp.zeros((13, kf.shape[1]), F32)], axis=0).astype(BF)
    crystal = lax.broadcasted_iota(jnp.int32, kone_ref.shape, 0)
    kone_ref[...] = jnp.where(kc_ref[...] == crystal, 1.0, 0.0).astype(BF)
    ksq = kf[0:1] * kf[0:1] + kf[1:2] * kf[1:2] + kf[2:3] * kf[2:3]
    scale = scale_s / (1.0 + ksq)
    step = 32

    def rows(i, carry):
        at = pl.multiple_of(i * step, step)
        d = damp_ref[pl.ds(pl.multiple_of(start + at, step), step), :]
        filt_ref[pl.ds(at, step), :] = jnp.exp(-(d * ksq)) * scale
        return carry

    lax.fori_loop(0, half // step, rows, 0)
    w_in_t_ref[...] = w_in_ref[:, pl.ds(start, half)].T


def start_phase(rows_ref, kmat_ref, kone_ref, turn_ref, same_ref):
    first = rows_ref.shape[1] - META
    meta = rows_ref[:, first:]
    turn_ref[...] = dot(meta, kmat_ref[...], 1, 0)
    lane = lax.broadcasted_iota(jnp.int32, meta.shape, 1).astype(F32)
    one = jnp.where(meta.astype(F32)[:, 3:4] == lane, 1.0, 0.0).astype(BF)
    same_ref[...] = dot(one, kone_ref[...], 1, 0)


def phase_tile(turn_ref, same_ref, phase_ref, at, first, count):
    span = slice(first, first + count)
    kcount = turn_ref.shape[1]
    turn = turn_ref[at, span]
    same = same_ref[at, span]
    rest = turn - jnp.floor(turn + 0.5)
    square = rest * rest
    cosine = square * COS_POLY[-1] + COS_POLY[-2]
    for c in COS_POLY[-3::-1]:
        cosine = cosine * square + c
    sine = square * SIN_POLY[-1] + SIN_POLY[-2]
    for c in SIN_POLY[-3::-1]:
        sine = sine * square + c
    sine = sine * rest
    held = sine * same
    phase_ref[at, span] = (same - held * sine).astype(BF)
    phase_ref[at, kcount + first : kcount + first + count] = (held * cosine).astype(BF)


def fill_stack(rows_ref, w_in_t_ref, w_out_half, stack_ref):
    half = w_in_t_ref.shape[0]
    width = w_in_t_ref.shape[1]
    stack_ref[0:half, :] = dot(w_in_t_ref[...], rows_ref[:, 0:width], 1, 1).astype(BF)
    stack_ref[half:, :] = dot(w_out_half, rows_ref[:, width : 2 * width], 1, 1).astype(BF)


def half_of(ref, shard_ref, half):
    return ref[pl.ds(pl.multiple_of(shard_ref[0] * half, half), half), :]


def own_kernel(
    shard_ref, own_ref, kmat_ref, kone_ref, w_in_t_ref, w_out_ref, phase_ref, stack_ref, part_ref,
    turn_ref, same_ref,
):
    start_phase(own_ref, kmat_ref, kone_ref, turn_ref, same_ref)
    fill_stack(own_ref, w_in_t_ref, half_of(w_out_ref, shard_ref, w_in_t_ref.shape[0]), stack_ref)
    slots, kcount = turn_ref.shape
    chunk = 256

    def structure(first):
        for at in (first, kcount + first):
            span = slice(at, at + chunk)
            part_ref[:, span] = dot(stack_ref[...], phase_ref[:, span], 1, 0)

    for first in range(0, kcount, chunk):
        if first:
            structure(first - chunk)
        for row in range(0, slots, 16):
            phase_tile(turn_ref, same_ref, phase_ref, slice(row, row + 16), first, chunk)
    structure(kcount - chunk)


def forward_kernel(
    shard_ref, oth_ref, part_ref, phase_own_ref, kmat_ref, kone_ref, filt_ref, w_in_t_ref,
    w_out_ref,
    phase_ref, stack_ref, msg_own_ref, msg_oth_ref,
    turn_ref, same_ref, scaled_ref, scale_m,
):
    half = w_in_t_ref.shape[0]
    fill_stack(oth_ref, w_in_t_ref, half_of(w_out_ref, shard_ref, half), stack_ref)
    start_phase(oth_ref, kmat_ref, kone_ref, turn_ref, same_ref)
    slots, kcount = turn_ref.shape
    chunk = 512

    def structure(first):
        filt = filt_ref[:, first : first + chunk]
        for at in (first, kcount + first):
            span = slice(at, at + chunk)
            total = part_ref[0:half, span] + dot(stack_ref[0:half, :], phase_ref[:, span], 1, 0)
            scaled_ref[:, span] = (total * filt).astype(BF)

    for first in range(0, kcount, chunk):
        if first:
            structure(first - chunk)
        for row in range(0, slots, 16):
            phase_tile(turn_ref, same_ref, phase_ref, slice(row, row + 16), first, chunk)
    structure(kcount - chunk)
    for phase, out in ((phase_own_ref, msg_own_ref), (phase_ref, msg_oth_ref)):
        out[...] = (scale_m * dot(scaled_ref[...], phase[...], 1, 1)).astype(BF)


def backward_kernel(
    own_ref, oth_ref, part_ref, phase_own_ref, phase_oth_ref, stack_ref, msg_own_ref, msg_oth_ref,
    filt_ref, grad_ref, scaled_ref, scale_m,
):
    half = msg_own_ref.shape[0]
    width = grad_ref.shape[1]
    kcount = filt_ref.shape[1]
    chunk = 512
    for at in range(0, 2 * kcount, chunk):
        span = slice(at, at + chunk)
        filt = filt_ref[:, at % kcount : at % kcount + chunk]
        total = part_ref[half:, span] + dot(stack_ref[half:, :], phase_oth_ref[:, span], 1, 0)
        scaled_ref[:, span] = (total * filt).astype(BF)
    total = dot(msg_own_ref[...], own_ref[:, width : 2 * width], 1, 0)
    total += dot(msg_oth_ref[...], oth_ref[:, width : 2 * width], 1, 0)
    grad_ref[0:half, :] = total.astype(BF)
    back_own = (scale_m * dot(scaled_ref[...], phase_own_ref[...], 1, 1)).astype(BF)
    back_oth = (scale_m * dot(scaled_ref[...], phase_oth_ref[...], 1, 1)).astype(BF)
    total = dot(back_own, own_ref[:, 0:width], 1, 0)
    total += dot(back_oth, oth_ref[:, 0:width], 1, 0)
    grad_ref[half:, :] = total.astype(BF)


def change_kernel(shard_ref, msg_ref, got_ref, w_out_ref, grad_ref, out_ref):
    half = msg_ref.shape[0]
    mine = pl.multiple_of(shard_ref[0] * half, half)
    other = pl.multiple_of((1 - shard_ref[0]) * half, half)
    change = dot(msg_ref[...], w_out_ref[pl.ds(mine, half), :], 0, 0)
    change += dot(got_ref[...], w_out_ref[pl.ds(other, half), :], 0, 0)
    change = change.astype(BF)
    step = half // PLANE
    for q in range(PLANE):
        out_ref[q, 0:step] = change[q * step : (q + 1) * step]
        out_ref[q, step : 2 * step] = grad_ref[q * step : (q + 1) * step]
        out_ref[q, 2 * step :] = grad_ref[half + q * step : half + (q + 1) * step]


def plane_sum_kernel(recv_ref, out_ref):
    planes, block = out_ref.shape[0], recv_ref.shape[1] // 3
    slots = PLANE * block
    change = jnp.concatenate([recv_ref[q, 0:block] for q in range(PLANE)], axis=0)
    to = lax.broadcasted_iota(jnp.int32, (slots, slots), 0)
    of = lax.broadcasted_iota(jnp.int32, (slots, slots), 1)
    width = 2 * PLANE
    source = ((to & 31) >> 1) * block + (to >> 5) * 2 + (to & 1)
    move = jnp.where(source == of, 1.0, 0.0).astype(BF)
    change = dot(move, change, 1, 0).astype(BF)
    total = recv_ref[0, block:].astype(F32)
    for q in range(1, PLANE):
        total += recv_ref[q, block:].astype(F32)
    total = total.astype(BF)
    for z in range(planes):
        out_ref[z, 0:width] = change[z * width : (z + 1) * width]
        out_ref[z, width:] = total


def column_sum_kernel(recv_ref, out_ref, norm_factor):
    first = recv_ref.shape[1] - out_ref.shape[1]
    total = recv_ref[0, first:].astype(F32)
    for z in range(1, recv_ref.shape[0]):
        total += recv_ref[z, first:].astype(F32)
    total = (total * norm_factor).astype(BF)
    for q in range(out_ref.shape[0]):
        out_ref[q] = total


def place_half(ref, member, grad_in_hbm, grad_out_hbm, in_ref, out_ref, sems):
    block = ref.shape[1] // 2
    half = PLANE * block
    start = pl.multiple_of(member * half, half)
    into = jnp.concatenate([ref[q, block:] for q in range(PLANE)], axis=0).astype(F32)
    in_ref[...] = into.T
    cols = pltpu.make_async_copy(in_ref, grad_in_hbm.at[:, pl.ds(start, half)], sems.at[0])
    cols.start()
    for q in range(PLANE):
        out_ref[q * block : (q + 1) * block, :] = ref[q, 0:block].astype(F32)
    rows = pltpu.make_async_copy(out_ref, grad_out_hbm.at[pl.ds(start, half), :], sems.at[1])
    rows.start()
    return cols, rows


def own_final_kernel(
    shard_ref, feat_ref, recv_ref, own_ref, half_ref,
    new_hbm, grad_in_hbm, grad_out_hbm,
    in_ref, out_ref, sems, new_ref, new_sem,
):
    copies = place_half(half_ref, shard_ref[0], grad_in_hbm, grad_out_hbm, in_ref, out_ref, sems)
    rows = feat_ref.shape[0]
    planes = recv_ref.shape[0]
    width = 2 * PLANE
    owner_row = own_ref[...].astype(F32)
    owner = as_column(owner_row)
    first = lax.broadcasted_iota(jnp.int32, (rows, rows), 0)
    second = lax.broadcasted_iota(jnp.int32, (rows, rows), 1)
    earlier = (owner == owner_row) & (second < first)
    rank = jnp.sum(jnp.where(earlier, 1.0, 0.0), axis=1, keepdims=True)
    first, second = place_of(owner.astype(jnp.int32), shard_ref[0])
    slot = (second * PLANE + first) * 2 + rank.astype(jnp.int32)
    pick = jnp.where(
        slot == lax.broadcasted_iota(jnp.int32, (rows, planes * width), 1), 1.0, 0.0
    ).astype(BF)
    change = jnp.concatenate([recv_ref[z, 0:width] for z in range(planes)], axis=0)
    new_ref[...] = (feat_ref[...].astype(F32) + dot(pick, change, 1, 0)).astype(BF)
    new = pltpu.make_async_copy(new_ref, new_hbm, new_sem)
    new.start()
    for copy in (*copies, new):
        copy.wait()


def other_final_kernel(
    shard_ref, half_ref, _grad_in, _grad_out, grad_in_hbm, grad_out_hbm, in_ref, out_ref, sems
):
    for copy in place_half(
        half_ref, 1 - shard_ref[0], grad_in_hbm, grad_out_hbm, in_ref, out_ref, sems
    ):
        copy.wait()


def local(
    features,
    norm_gain,
    w_in,
    w_out,
    cotangent,
    positions,
    crystal_of_atom,
    atom_owner,
    k_index,
    k_crystal,
    damping,
):
    rows, width = features.shape
    around, plane, column_set = hop_sets()
    groups = lax.axis_size("dp")
    planes = groups // PLANE
    members = lax.axis_size("shard")
    capacity = 2 * rows // groups
    slots = groups * capacity
    half = width // members
    kcount = k_index.shape[1]
    scale_s = (slots * members / CRY_DEV) ** (-0.5)
    scale_m = (kcount / CRY_DEV) ** (-0.5)
    norm_factor = (rows * groups * members) ** (-0.5)
    shard = lax.axis_index("shard").astype(jnp.int32).reshape(1)
    swap = [(0, 1), (1, 0)]

    owner_row = atom_owner.reshape(1, rows)
    packed = 2 * width + META
    operands = [
        shard,
        features,
        norm_gain.reshape(1, width),
        cotangent,
        positions,
        crystal_of_atom.reshape(1, rows),
        owner_row,
    ]
    send = call(
        prep_kernel,
        jax.ShapeDtypeStruct((groups, capacity, packed), BF),
        operands,
        scratch=[pltpu.VMEM(a.shape, a.dtype) for a in operands[1:]]
        + [
            pltpu.SemaphoreType.DMA((len(operands) - 1,)),
            pltpu.VMEM((groups, capacity, packed), BF),
            pltpu.SemaphoreType.DMA((3,)),
        ],
        specs=[SM] + [HB] * (len(operands) - 1),
        outs=HB,
        limit=FULL_VMEM,
    )
    recv = exchange(send, around)
    own = recv.reshape(slots, packed)
    kmat, kone, filt, w_in_t = call(
        functools.partial(static_kernel, scale_s=scale_s),
        (
            jax.ShapeDtypeStruct((META, kcount), BF),
            jax.ShapeDtypeStruct((META, kcount), BF),
            jax.ShapeDtypeStruct((half, kcount), F32),
            jax.ShapeDtypeStruct((half, width), BF),
        ),
        [shard, k_index, k_crystal.reshape(1, kcount), damping.reshape(width, 1), w_in],
        specs=[SM, VM, VM, VM, VM],
        flops=4_000_000_000,
    )
    own, kmat, kone, filt, w_in_t = lax.optimization_barrier((own, kmat, kone, filt, w_in_t))
    other = lax.ppermute(own, "shard", swap)
    phase_shape = jax.ShapeDtypeStruct((slots, 2 * kcount), BF)
    stack_shape = jax.ShapeDtypeStruct((2 * half, slots), BF)
    message_shape = jax.ShapeDtypeStruct((half, slots), BF)
    turn = pltpu.VMEM((slots, kcount), F32)
    scaled = pltpu.VMEM((half, 2 * kcount), BF)
    phase_own, _, part = call(
        own_kernel,
        (phase_shape, stack_shape, jax.ShapeDtypeStruct((2 * half, 2 * kcount), F32)),
        [shard, own, kmat, kone, w_in_t, w_out],
        scratch=[turn, turn],
        specs=[SM] + [VM] * 5,
        flops=4_000_000_000,
    )
    phase_oth, stack_oth, message, message_oth = call(
        functools.partial(forward_kernel, scale_m=scale_m),
        (phase_shape, stack_shape, message_shape, message_shape),
        [shard, other, part, phase_own, kmat, kone, filt, w_in_t, w_out],
        scratch=[turn, turn, scaled],
        specs=[SM] + [VM] * 8,
    )
    got = lax.ppermute(message_oth, "shard", swap)
    grads = call(
        functools.partial(backward_kernel, scale_m=scale_m),
        jax.ShapeDtypeStruct((2 * half, width), BF),
        [own, other, part, phase_own, phase_oth, stack_oth, message, message_oth, filt],
        scratch=[scaled],
        flops=4_000_000_000,
    )
    block = slots // PLANE
    back = call(
        change_kernel,
        jax.ShapeDtypeStruct((PLANE, 3 * block, width), BF),
        [shard, message, got, w_out, grads],
        specs=[SM] + [VM] * 4,
    )
    recv_plane = exchange(back, plane)
    column = call(
        plane_sum_kernel,
        jax.ShapeDtypeStruct((planes, slots // planes + 2 * block, width), BF),
        [recv_plane],
    )
    recv_column = exchange(column, column_set)
    share = call(
        functools.partial(column_sum_kernel, norm_factor=norm_factor),
        jax.ShapeDtypeStruct((PLANE, 2 * block, width), BF),
        [recv_column],
    )
    mine = exchange(share, plane)
    theirs = lax.ppermute(mine, "shard", swap)
    grads = (jax.ShapeDtypeStruct((width, width), F32),) * 2
    placing = [
        pltpu.VMEM((width, half), F32),
        pltpu.VMEM((half, width), F32),
        pltpu.SemaphoreType.DMA((2,)),
    ]
    updated, *first = call(
        own_final_kernel,
        (jax.ShapeDtypeStruct((rows, width), BF), *grads),
        [shard, features, recv_column, owner_row, mine],
        scratch=[*placing, pltpu.VMEM((rows, width), BF), pltpu.SemaphoreType.DMA],
        specs=[SM, VM, VM, VM, VM],
        outs=(HB, HB, HB),
        flops=4_000_000_000,
    )
    grad_w_in, grad_w_out = call(
        other_final_kernel,
        grads,
        [shard, theirs, *first],
        scratch=placing,
        specs=[SM, VM, HB, HB],
        outs=(HB, HB),
        aliases={2: 0, 3: 1},
    )
    return (updated, grad_w_in, grad_w_out)


def solution(mesh):
    every = ("dp", "shard")
    in_specs = (
        P(every, None),
        P(),
        P(),
        P(),
        P(every, None),
        P(None, every),
        P(every),
        P(every, None),
        P(None, "dp"),
        P("dp"),
        P(),
    )
    out_specs = (P(every, None), P(), P())
    return jax.shard_map(local, mesh=mesh, in_specs=in_specs, out_specs=out_specs, check_vma=False)
```

```python
import functools
import math

import jax
import jax.numpy as jnp
from jax import lax
from jax.experimental import pallas as pl
from jax.experimental.pallas import tpu as pltpu
from jax.sharding import PartitionSpec as P

CRY_DEV = 8
BF = jnp.bfloat16
F32 = jnp.float32
VMEM_LIMIT = 24 * 1024 * 1024
FULL_VMEM = 63 * 1024 * 1024
META = 128

COS_POLY = (
    1.4142135381698608,
    -6.978850841522217,
    5.739460468292236,
    -1.883557915687561,
    0.3106880187988281,
)
SIN_POLY = (
    4.442883014678955,
    -7.308245658874512,
    3.606354236602783,
    -0.8461116552352905,
    0.1098245158791542,
)

VM = pl.BlockSpec(memory_space=pltpu.VMEM)
SM = pl.BlockSpec(memory_space=pltpu.SMEM)
HB = pl.BlockSpec(memory_space=pltpu.MemorySpace.HBM)
PLANE = 16


def place_of(owner, shard):
    first = jnp.where(shard == 0, owner & 15, (owner >> 4) * 2 + (owner & 1))
    second = jnp.where(shard == 0, owner >> 4, (owner >> 1) & 7)
    return first, second


def hop_sets():
    every = [(z, x, y) for z in range(8) for x in range(4) for y in range(4)]

    def split(shard):
        if shard == 0:
            return {(x * 4 + y, z): (z, x, y) for z, x, y in every}
        return {(z * 2 + y % 2, x * 2 + y // 2): (z, x, y) for z, x, y in every}

    around, first, second = [], [], []
    for shard in range(2):
        at = {key: ((z * 4 + x) * 4 + y) * 2 + shard for key, (z, x, y) in split(shard).items()}
        around.append([at[i, j] for i in range(PLANE) for j in range(8)])
        first += [[at[i, j] for i in range(PLANE)] for j in range(8)]
        second += [[at[i, j] for j in range(8)] for i in range(PLANE)]
    return around, first, second


def exchange(array, sets):
    return lax.all_to_all(
        array,
        ("dp", "shard"),
        split_axis=0,
        concat_axis=0,
        axis_index_groups=sets,
        tiled=True,
    )


def call(body, out_shape, inputs, scratch=(), specs=None, outs=None, flops=1_000_000, aliases=None,
         limit=VMEM_LIMIT):
    return pl.pallas_call(
        body,
        out_shape=out_shape,
        in_specs=specs if specs is not None else [VM] * len(inputs),
        out_specs=outs if outs is not None else jax.tree.map(lambda _: VM, out_shape),
        scratch_shapes=list(scratch),
        input_output_aliases=aliases or {},
        compiler_params=pltpu.CompilerParams(vmem_limit_bytes=limit),
        cost_estimate=pl.CostEstimate(flops=flops, bytes_accessed=1_000_000, transcendentals=0),
    )(*inputs)


def dot(a, b, ca, cb):
    return lax.dot_general(a, b, (((ca,), (cb,)), ((), ())), preferred_element_type=F32)


def as_column(row):
    n = row.shape[1]
    diagonal = lax.broadcasted_iota(jnp.int32, (n, n), 0) == lax.broadcasted_iota(
        jnp.int32, (n, n), 1
    )
    return jnp.sum(jnp.where(diagonal, row, 0.0), axis=1, keepdims=True)


def prep_kernel(
    shard_ref, feat_hbm, gain_hbm, cot_hbm, pos_hbm, cry_hbm, own_hbm, out_hbm,
    feat_ref, gain_ref, cot_ref, pos_ref, cry_ref, own_ref, sems, stage_ref, out_sems,
):
    sources = (feat_hbm, gain_hbm, cot_hbm, pos_hbm, cry_hbm, own_hbm)
    targets = (feat_ref, gain_ref, cot_ref, pos_ref, cry_ref, own_ref)
    feat_in, gain_in, cot_in, pos_in, cry_in, own_in = copies = [
        pltpu.make_async_copy(src, dst, sems.at[i])
        for i, (src, dst) in enumerate(zip(sources, targets))
    ]
    for i in (5, 2, 0, 1, 3, 4):
        copies[i].start()
    rows, width = feat_ref.shape
    slots = out_hbm.shape[0] * out_hbm.shape[1]
    own_in.wait()
    owner = own_ref[...].astype(F32)
    first = lax.broadcasted_iota(jnp.int32, (rows, rows), 0)
    second = lax.broadcasted_iota(jnp.int32, (rows, rows), 1)
    earlier = (as_column(owner) == owner) & (first < second)
    rank = jnp.sum(jnp.where(earlier, 1.0, 0.0), axis=0, keepdims=True)
    first, second = place_of(own_ref[...], shard_ref[0])
    slot = (first * 8 + second) * 2 + rank.astype(jnp.int32)
    place = jnp.where(
        slot == lax.broadcasted_iota(jnp.int32, (slots, rows), 0), 1.0, 0.0
    ).astype(BF)
    sent = []

    def send(first, part):
        span = slice(first, first + part.shape[1])
        stage_ref[:, :, span] = part.astype(BF).reshape(slots // 2, 2, part.shape[1])
        copy = pltpu.make_async_copy(
            stage_ref.at[:, :, span], out_hbm.at[:, :, span], out_sems.at[len(sent)]
        )
        copy.start()
        sent.append(copy)

    cot_in.wait()
    send(width, dot(place, cot_ref[...], 1, 0))
    feat_in.wait()
    gain_in.wait()
    hidden = feat_ref[...].astype(F32)
    normed = (
        hidden
        * lax.rsqrt(jnp.mean(hidden * hidden, axis=-1, keepdims=True) + 1e-06)
        * gain_ref[...]
    ).astype(BF)
    send(0, dot(place, normed, 1, 0))
    pos_in.wait()
    cry_in.wait()
    meta = jnp.concatenate(
        [
            pos_ref[...].astype(F32),
            cry_ref[...].astype(F32),
            jnp.zeros((META - 4, rows), F32),
        ],
        axis=0,
    ).astype(BF)
    send(2 * width, dot(place, meta, 1, 1))
    for copy in sent:
        copy.wait()


def static_kernel(
    shard_ref, k_ref, kc_ref, damp_ref, w_in_ref, kmat_ref, kone_ref, filt_ref, w_in_t_ref, scale_s
):
    half = filt_ref.shape[0]
    start = pl.multiple_of(shard_ref[0] * half, half)
    kf = k_ref[...].astype(F32)
    kmat_ref[...] = jnp.zeros(kmat_ref.shape, BF)
    kmat_ref[0:16, :] = jnp.concatenate([kf, jnp.zeros((13, kf.shape[1]), F32)], axis=0).astype(BF)
    crystal = lax.broadcasted_iota(jnp.int32, kone_ref.shape, 0)
    kone_ref[...] = jnp.where(kc_ref[...] == crystal, 1.0, 0.0).astype(BF)
    ksq = kf[0:1] * kf[0:1] + kf[1:2] * kf[1:2] + kf[2:3] * kf[2:3]
    scale = scale_s / (1.0 + ksq)
    step = 32

    def rows(i, carry):
        at = pl.multiple_of(i * step, step)
        d = damp_ref[pl.ds(pl.multiple_of(start + at, step), step), :]
        filt_ref[pl.ds(at, step), :] = jnp.exp(-(d * ksq)) * scale
        return carry

    lax.fori_loop(0, half // step, rows, 0)
    w_in_t_ref[...] = w_in_ref[:, pl.ds(start, half)].T


def start_phase(rows_ref, kmat_ref, kone_ref, turn_ref, same_ref):
    first = rows_ref.shape[1] - META
    meta = rows_ref[:, first:]
    turn_ref[...] = dot(meta, kmat_ref[...], 1, 0)
    lane = lax.broadcasted_iota(jnp.int32, meta.shape, 1).astype(F32)
    one = jnp.where(meta.astype(F32)[:, 3:4] == lane, 1.0, 0.0).astype(BF)
    same_ref[...] = dot(one, kone_ref[...], 1, 0)


def phase_tile(turn_ref, same_ref, phase_ref, at, first, count):
    span = slice(first, first + count)
    kcount = turn_ref.shape[1]
    turn = turn_ref[at, span]
    same = same_ref[at, span]
    rest = turn - jnp.floor(turn + 0.5)
    square = rest * rest
    cosine = square * COS_POLY[-1] + COS_POLY[-2]
    for c in COS_POLY[-3::-1]:
        cosine = cosine * square + c
    sine = square * SIN_POLY[-1] + SIN_POLY[-2]
    for c in SIN_POLY[-3::-1]:
        sine = sine * square + c
    sine = sine * rest
    held = sine * same
    phase_ref[at, span] = (same - held * sine).astype(BF)
    phase_ref[at, kcount + first : kcount + first + count] = (held * cosine).astype(BF)


def fill_stack(rows_ref, w_in_t_ref, w_out_half, stack_ref):
    half = w_in_t_ref.shape[0]
    width = w_in_t_ref.shape[1]
    stack_ref[0:half, :] = dot(w_in_t_ref[...], rows_ref[:, 0:width], 1, 1).astype(BF)
    stack_ref[half:, :] = dot(w_out_half, rows_ref[:, width : 2 * width], 1, 1).astype(BF)


def half_of(ref, shard_ref, half):
    return ref[pl.ds(pl.multiple_of(shard_ref[0] * half, half), half), :]


def own_kernel(
    shard_ref, own_ref, kmat_ref, kone_ref, w_in_t_ref, w_out_ref, phase_ref, stack_ref, part_ref,
    turn_ref, same_ref,
):
    start_phase(own_ref, kmat_ref, kone_ref, turn_ref, same_ref)
    fill_stack(own_ref, w_in_t_ref, half_of(w_out_ref, shard_ref, w_in_t_ref.shape[0]), stack_ref)
    slots, kcount = turn_ref.shape
    chunk = 256

    def structure(first):
        for at in (first, kcount + first):
            span = slice(at, at + chunk)
            part_ref[:, span] = dot(stack_ref[...], phase_ref[:, span], 1, 0)

    for first in range(0, kcount, chunk):
        if first:
            structure(first - chunk)
        for row in range(0, slots, 16):
            phase_tile(turn_ref, same_ref, phase_ref, slice(row, row + 16), first, chunk)
    structure(kcount - chunk)


def forward_kernel(
    shard_ref, oth_ref, part_ref, phase_own_ref, kmat_ref, kone_ref, filt_ref, w_in_t_ref,
    w_out_ref,
    phase_ref, stack_ref, msg_own_ref, msg_oth_ref,
    turn_ref, same_ref, scaled_ref, scale_m,
):
    half = w_in_t_ref.shape[0]
    fill_stack(oth_ref, w_in_t_ref, half_of(w_out_ref, shard_ref, half), stack_ref)
    start_phase(oth_ref, kmat_ref, kone_ref, turn_ref, same_ref)
    slots, kcount = turn_ref.shape
    chunk = 512

    def structure(first):
        filt = filt_ref[:, first : first + chunk]
        for at in (first, kcount + first):
            span = slice(at, at + chunk)
            total = part_ref[0:half, span] + dot(stack_ref[0:half, :], phase_ref[:, span], 1, 0)
            scaled_ref[:, span] = (total * filt).astype(BF)

    for first in range(0, kcount, chunk):
        if first:
            structure(first - chunk)
        for row in range(0, slots, 16):
            phase_tile(turn_ref, same_ref, phase_ref, slice(row, row + 16), first, chunk)
    structure(kcount - chunk)
    for phase, out in ((phase_own_ref, msg_own_ref), (phase_ref, msg_oth_ref)):
        out[...] = (scale_m * dot(scaled_ref[...], phase[...], 1, 1)).astype(BF)


def backward_kernel(
    own_ref, oth_ref, part_ref, phase_own_ref, phase_oth_ref, stack_ref, msg_own_ref, msg_oth_ref,
    filt_ref, grad_ref, scaled_ref, scale_m,
):
    half = msg_own_ref.shape[0]
    width = grad_ref.shape[1]
    kcount = filt_ref.shape[1]
    chunk = 512
    for at in range(0, 2 * kcount, chunk):
        span = slice(at, at + chunk)
        filt = filt_ref[:, at % kcount : at % kcount + chunk]
        total = part_ref[half:, span] + dot(stack_ref[half:, :], phase_oth_ref[:, span], 1, 0)
        scaled_ref[:, span] = (total * filt).astype(BF)
    total = dot(msg_own_ref[...], own_ref[:, width : 2 * width], 1, 0)
    total += dot(msg_oth_ref[...], oth_ref[:, width : 2 * width], 1, 0)
    grad_ref[0:half, :] = total.astype(BF)
    back_own = (scale_m * dot(scaled_ref[...], phase_own_ref[...], 1, 1)).astype(BF)
    back_oth = (scale_m * dot(scaled_ref[...], phase_oth_ref[...], 1, 1)).astype(BF)
    total = dot(back_own, own_ref[:, 0:width], 1, 0)
    total += dot(back_oth, oth_ref[:, 0:width], 1, 0)
    grad_ref[half:, :] = total.astype(BF)


def change_kernel(shard_ref, msg_ref, got_ref, w_out_ref, grad_ref, out_ref):
    half = msg_ref.shape[0]
    mine = pl.multiple_of(shard_ref[0] * half, half)
    other = pl.multiple_of((1 - shard_ref[0]) * half, half)
    change = dot(msg_ref[...], w_out_ref[pl.ds(mine, half), :], 0, 0)
    change += dot(got_ref[...], w_out_ref[pl.ds(other, half), :], 0, 0)
    change = change.astype(BF)
    step = half // PLANE
    for q in range(PLANE):
        out_ref[q, 0:step] = change[q * step : (q + 1) * step]
        out_ref[q, step : 2 * step] = grad_ref[q * step : (q + 1) * step]
        out_ref[q, 2 * step :] = grad_ref[half + q * step : half + (q + 1) * step]


def plane_sum_kernel(recv_ref, out_ref):
    planes, block = out_ref.shape[0], recv_ref.shape[1] // 3
    slots = PLANE * block
    change = jnp.concatenate([recv_ref[q, 0:block] for q in range(PLANE)], axis=0)
    to = lax.broadcasted_iota(jnp.int32, (slots, slots), 0)
    of = lax.broadcasted_iota(jnp.int32, (slots, slots), 1)
    width = 2 * PLANE
    source = ((to & 31) >> 1) * block + (to >> 5) * 2 + (to & 1)
    move = jnp.where(source == of, 1.0, 0.0).astype(BF)
    change = dot(move, change, 1, 0).astype(BF)
    total = recv_ref[0, block:].astype(F32)
    for q in range(1, PLANE):
        total += recv_ref[q, block:].astype(F32)
    total = total.astype(BF)
    for z in range(planes):
        out_ref[z, 0:width] = change[z * width : (z + 1) * width]
        out_ref[z, width:] = total


def column_sum_kernel(recv_ref, out_ref, norm_factor):
    first = recv_ref.shape[1] - out_ref.shape[1]
    total = recv_ref[0, first:].astype(F32)
    for z in range(1, recv_ref.shape[0]):
        total += recv_ref[z, first:].astype(F32)
    total = (total * norm_factor).astype(BF)
    for q in range(out_ref.shape[0]):
        out_ref[q] = total


def place_half(ref, member, grad_in_hbm, grad_out_hbm, in_ref, out_ref, sems):
    block = ref.shape[1] // 2
    half = PLANE * block
    start = pl.multiple_of(member * half, half)
    copies = []

    def send(src, dst):
        copies.append(pltpu.make_async_copy(src, dst, sems.at[len(copies)]))
        copies[-1].start()

    for first in range(0, PLANE, 8):
        for q in range(first, first + 8):
            out_ref[q * block : (q + 1) * block, :] = ref[q, 0:block].astype(F32)
        at = pl.ds(pl.multiple_of(start + first * block, 8 * block), 8 * block)
        send(out_ref.at[first * block : (first + 8) * block, :], grad_out_hbm.at[at, :])
    into = jnp.concatenate([ref[q, block:] for q in range(PLANE)], axis=0)
    for first in range(0, into.shape[1], 128):
        span = slice(first, first + 128)
        in_ref[span, :] = into[:, span].astype(F32).T
        send(in_ref.at[span, :], grad_in_hbm.at[span, pl.ds(start, half)])
    return copies


def own_final_kernel(
    shard_ref, feat_ref, recv_ref, own_ref, half_ref,
    new_hbm, grad_in_hbm, grad_out_hbm,
    in_ref, out_ref, sems, new_ref, new_sem,
):
    copies = place_half(half_ref, shard_ref[0], grad_in_hbm, grad_out_hbm, in_ref, out_ref, sems)
    rows = feat_ref.shape[0]
    planes = recv_ref.shape[0]
    width = 2 * PLANE
    owner_row = own_ref[...].astype(F32)
    owner = as_column(owner_row)
    first = lax.broadcasted_iota(jnp.int32, (rows, rows), 0)
    second = lax.broadcasted_iota(jnp.int32, (rows, rows), 1)
    earlier = (owner == owner_row) & (second < first)
    rank = jnp.sum(jnp.where(earlier, 1.0, 0.0), axis=1, keepdims=True)
    first, second = place_of(owner.astype(jnp.int32), shard_ref[0])
    slot = (second * PLANE + first) * 2 + rank.astype(jnp.int32)
    pick = jnp.where(
        slot == lax.broadcasted_iota(jnp.int32, (rows, planes * width), 1), 1.0, 0.0
    ).astype(BF)
    change = jnp.concatenate([recv_ref[z, 0:width] for z in range(planes)], axis=0)
    new_ref[...] = (feat_ref[...].astype(F32) + dot(pick, change, 1, 0)).astype(BF)
    new = pltpu.make_async_copy(new_ref, new_hbm, new_sem)
    new.start()
    for copy in (*copies, new):
        copy.wait()


def other_final_kernel(
    shard_ref, half_ref, _grad_in, _grad_out, grad_in_hbm, grad_out_hbm, in_ref, out_ref, sems
):
    for copy in place_half(
        half_ref, 1 - shard_ref[0], grad_in_hbm, grad_out_hbm, in_ref, out_ref, sems
    ):
        copy.wait()


def local(
    features,
    norm_gain,
    w_in,
    w_out,
    cotangent,
    positions,
    crystal_of_atom,
    atom_owner,
    k_index,
    k_crystal,
    damping,
):
    rows, width = features.shape
    around, plane, column_set = hop_sets()
    groups = lax.axis_size("dp")
    planes = groups // PLANE
    members = lax.axis_size("shard")
    capacity = 2 * rows // groups
    slots = groups * capacity
    half = width // members
    kcount = k_index.shape[1]
    scale_s = (slots * members / CRY_DEV) ** (-0.5)
    scale_m = (kcount / CRY_DEV) ** (-0.5)
    norm_factor = (rows * groups * members) ** (-0.5)
    shard = lax.axis_index("shard").astype(jnp.int32).reshape(1)
    swap = [(0, 1), (1, 0)]

    owner_row = atom_owner.reshape(1, rows)
    packed = 2 * width + META
    operands = [
        shard,
        features,
        norm_gain.reshape(1, width),
        cotangent,
        positions,
        crystal_of_atom.reshape(1, rows),
        owner_row,
    ]
    send = call(
        prep_kernel,
        jax.ShapeDtypeStruct((groups, capacity, packed), BF),
        operands,
        scratch=[pltpu.VMEM(a.shape, a.dtype) for a in operands[1:]]
        + [
            pltpu.SemaphoreType.DMA((len(operands) - 1,)),
            pltpu.VMEM((groups, capacity, packed), BF),
            pltpu.SemaphoreType.DMA((3,)),
        ],
        specs=[SM] + [HB] * (len(operands) - 1),
        outs=HB,
        limit=FULL_VMEM,
    )
    recv = exchange(send, around)
    own = recv.reshape(slots, packed)
    kmat, kone, filt, w_in_t = call(
        functools.partial(static_kernel, scale_s=scale_s),
        (
            jax.ShapeDtypeStruct((META, kcount), BF),
            jax.ShapeDtypeStruct((META, kcount), BF),
            jax.ShapeDtypeStruct((half, kcount), F32),
            jax.ShapeDtypeStruct((half, width), BF),
        ),
        [shard, k_index, k_crystal.reshape(1, kcount), damping.reshape(width, 1), w_in],
        specs=[SM, VM, VM, VM, VM],
        flops=4_000_000_000,
    )
    own, kmat, kone, filt, w_in_t = lax.optimization_barrier((own, kmat, kone, filt, w_in_t))
    other = lax.ppermute(own, "shard", swap)
    phase_shape = jax.ShapeDtypeStruct((slots, 2 * kcount), BF)
    stack_shape = jax.ShapeDtypeStruct((2 * half, slots), BF)
    message_shape = jax.ShapeDtypeStruct((half, slots), BF)
    turn = pltpu.VMEM((slots, kcount), F32)
    scaled = pltpu.VMEM((half, 2 * kcount), BF)
    phase_own, _, part = call(
        own_kernel,
        (phase_shape, stack_shape, jax.ShapeDtypeStruct((2 * half, 2 * kcount), F32)),
        [shard, own, kmat, kone, w_in_t, w_out],
        scratch=[turn, turn],
        specs=[SM] + [VM] * 5,
        flops=4_000_000_000,
    )
    phase_oth, stack_oth, message, message_oth = call(
        functools.partial(forward_kernel, scale_m=scale_m),
        (phase_shape, stack_shape, message_shape, message_shape),
        [shard, other, part, phase_own, kmat, kone, filt, w_in_t, w_out],
        scratch=[turn, turn, scaled],
        specs=[SM] + [VM] * 8,
    )
    got = lax.ppermute(message_oth, "shard", swap)
    grads = call(
        functools.partial(backward_kernel, scale_m=scale_m),
        jax.ShapeDtypeStruct((2 * half, width), BF),
        [own, other, part, phase_own, phase_oth, stack_oth, message, message_oth, filt],
        scratch=[scaled],
        flops=4_000_000_000,
    )
    block = slots // PLANE
    back = call(
        change_kernel,
        jax.ShapeDtypeStruct((PLANE, 3 * block, width), BF),
        [shard, message, got, w_out, grads],
        specs=[SM] + [VM] * 4,
    )
    recv_plane = exchange(back, plane)
    column = call(
        plane_sum_kernel,
        jax.ShapeDtypeStruct((planes, slots // planes + 2 * block, width), BF),
        [recv_plane],
    )
    recv_column = exchange(column, column_set)
    share = call(
        functools.partial(column_sum_kernel, norm_factor=norm_factor),
        jax.ShapeDtypeStruct((PLANE, 2 * block, width), BF),
        [recv_column],
    )
    mine = exchange(share, plane)
    theirs = lax.ppermute(mine, "shard", swap)
    grads = (jax.ShapeDtypeStruct((width, width), F32),) * 2
    placing = [
        pltpu.VMEM((width, half), F32),
        pltpu.VMEM((half, width), F32),
        pltpu.SemaphoreType.DMA((6,)),
    ]
    updated, *first = call(
        own_final_kernel,
        (jax.ShapeDtypeStruct((rows, width), BF), *grads),
        [shard, features, recv_column, owner_row, mine],
        scratch=[*placing, pltpu.VMEM((rows, width), BF), pltpu.SemaphoreType.DMA],
        specs=[SM, VM, VM, VM, VM],
        outs=(HB, HB, HB),
        flops=4_000_000_000,
    )
    grad_w_in, grad_w_out = call(
        other_final_kernel,
        grads,
        [shard, theirs, *first],
        scratch=placing,
        specs=[SM, VM, HB, HB],
        outs=(HB, HB),
        aliases={2: 0, 3: 1},
    )
    return (updated, grad_w_in, grad_w_out)


def solution(mesh):
    every = ("dp", "shard")
    in_specs = (
        P(every, None),
        P(),
        P(),
        P(),
        P(every, None),
        P(None, every),
        P(every),
        P(every, None),
        P(None, "dp"),
        P("dp"),
        P(),
    )
    out_specs = (P(every, None), P(), P())
    return jax.shard_map(local, mesh=mesh, in_specs=in_specs, out_specs=out_specs, check_vma=False)
```

```python
import functools
import math

import jax
import jax.numpy as jnp
from jax import lax
from jax.experimental import pallas as pl
from jax.experimental.pallas import tpu as pltpu
from jax.sharding import PartitionSpec as P

CRY_DEV = 8
BF = jnp.bfloat16
F32 = jnp.float32
VMEM_LIMIT = 24 * 1024 * 1024
FULL_VMEM = 63 * 1024 * 1024
META = 128

COS_POLY = (
    1.4142135381698608,
    -6.978850841522217,
    5.739460468292236,
    -1.883557915687561,
    0.3106880187988281,
)
SIN_POLY = (
    4.442883014678955,
    -7.308245658874512,
    3.606354236602783,
    -0.8461116552352905,
    0.1098245158791542,
)

VM = pl.BlockSpec(memory_space=pltpu.VMEM)
SM = pl.BlockSpec(memory_space=pltpu.SMEM)
HB = pl.BlockSpec(memory_space=pltpu.MemorySpace.HBM)
PLANE = 16


def place_of(owner, shard):
    first = 15 - jnp.where(shard == 0, owner & 15, (owner >> 4) * 2 + (owner & 1))
    second = jnp.where(shard == 0, owner >> 4, 7 - ((owner >> 1) & 7))
    return first, second


def hop_sets():
    every = [(z, x, y) for z in range(8) for x in range(4) for y in range(4)]

    def split(shard):
        if shard == 0:
            return {(15 - (x * 4 + y), z): (z, x, y) for z, x, y in every}
        return {(15 - (z * 2 + y % 2), 7 - (x * 2 + y // 2)): (z, x, y) for z, x, y in every}

    around, first, second = [], [], []
    for shard in range(2):
        at = {key: ((z * 4 + x) * 4 + y) * 2 + shard for key, (z, x, y) in split(shard).items()}
        around.append([at[i, j] for i in range(PLANE) for j in range(8)])
        first += [[at[i, j] for i in range(PLANE)] for j in range(8)]
        second += [[at[i, j] for j in range(8)] for i in range(PLANE)]
    return around, first, second


def exchange(array, sets):
    return lax.all_to_all(
        array,
        ("dp", "shard"),
        split_axis=0,
        concat_axis=0,
        axis_index_groups=sets,
        tiled=True,
    )


def call(body, out_shape, inputs, scratch=(), specs=None, outs=None, flops=1_000_000, aliases=None,
         limit=VMEM_LIMIT):
    return pl.pallas_call(
        body,
        out_shape=out_shape,
        in_specs=specs if specs is not None else [VM] * len(inputs),
        out_specs=outs if outs is not None else jax.tree.map(lambda _: VM, out_shape),
        scratch_shapes=list(scratch),
        input_output_aliases=aliases or {},
        compiler_params=pltpu.CompilerParams(vmem_limit_bytes=limit),
        cost_estimate=pl.CostEstimate(flops=flops, bytes_accessed=1_000_000, transcendentals=0),
    )(*inputs)


def dot(a, b, ca, cb):
    return lax.dot_general(a, b, (((ca,), (cb,)), ((), ())), preferred_element_type=F32)


def as_column(row):
    n = row.shape[1]
    diagonal = lax.broadcasted_iota(jnp.int32, (n, n), 0) == lax.broadcasted_iota(
        jnp.int32, (n, n), 1
    )
    return jnp.sum(jnp.where(diagonal, row, 0.0), axis=1, keepdims=True)


def prep_kernel(
    shard_ref, feat_hbm, gain_hbm, cot_hbm, pos_hbm, cry_hbm, own_hbm, out_hbm,
    feat_ref, gain_ref, cot_ref, pos_ref, cry_ref, own_ref, sems, stage_ref, out_sems,
):
    sources = (feat_hbm, gain_hbm, cot_hbm, pos_hbm, cry_hbm, own_hbm)
    targets = (feat_ref, gain_ref, cot_ref, pos_ref, cry_ref, own_ref)
    feat_in, gain_in, cot_in, pos_in, cry_in, own_in = copies = [
        pltpu.make_async_copy(src, dst, sems.at[i])
        for i, (src, dst) in enumerate(zip(sources, targets))
    ]
    for i in (5, 2, 0, 1, 3, 4):
        copies[i].start()
    rows, width = feat_ref.shape
    slots = out_hbm.shape[0] * out_hbm.shape[1]
    own_in.wait()
    owner = own_ref[...].astype(F32)
    first = lax.broadcasted_iota(jnp.int32, (rows, rows), 0)
    second = lax.broadcasted_iota(jnp.int32, (rows, rows), 1)
    earlier = (as_column(owner) == owner) & (first < second)
    rank = jnp.sum(jnp.where(earlier, 1.0, 0.0), axis=0, keepdims=True)
    first, second = place_of(own_ref[...], shard_ref[0])
    slot = (first * 8 + second) * 2 + rank.astype(jnp.int32)
    place = jnp.where(
        slot == lax.broadcasted_iota(jnp.int32, (slots, rows), 0), 1.0, 0.0
    ).astype(BF)
    sent = []

    def send(first, part):
        span = slice(first, first + part.shape[1])
        stage_ref[:, :, span] = part.astype(BF).reshape(slots // 2, 2, part.shape[1])
        copy = pltpu.make_async_copy(
            stage_ref.at[:, :, span], out_hbm.at[:, :, span], out_sems.at[len(sent)]
        )
        copy.start()
        sent.append(copy)

    cot_in.wait()
    send(width, dot(place, cot_ref[...], 1, 0))
    feat_in.wait()
    gain_in.wait()
    hidden = feat_ref[...].astype(F32)
    normed = (
        hidden
        * lax.rsqrt(jnp.mean(hidden * hidden, axis=-1, keepdims=True) + 1e-06)
        * gain_ref[...]
    ).astype(BF)
    send(0, dot(place, normed, 1, 0))
    pos_in.wait()
    cry_in.wait()
    meta = jnp.concatenate(
        [
            pos_ref[...].astype(F32),
            cry_ref[...].astype(F32),
            jnp.zeros((META - 4, rows), F32),
        ],
        axis=0,
    ).astype(BF)
    send(2 * width, dot(place, meta, 1, 1))
    for copy in sent:
        copy.wait()


def static_kernel(
    shard_ref, k_ref, kc_ref, damp_ref, w_in_ref, kmat_ref, kone_ref, filt_ref, w_in_t_ref, scale_s
):
    half = filt_ref.shape[0]
    start = pl.multiple_of(shard_ref[0] * half, half)
    kf = k_ref[...].astype(F32)
    kmat_ref[...] = jnp.zeros(kmat_ref.shape, BF)
    kmat_ref[0:16, :] = jnp.concatenate([kf, jnp.zeros((13, kf.shape[1]), F32)], axis=0).astype(BF)
    crystal = lax.broadcasted_iota(jnp.int32, kone_ref.shape, 0)
    kone_ref[...] = jnp.where(kc_ref[...] == crystal, 1.0, 0.0).astype(BF)
    ksq = kf[0:1] * kf[0:1] + kf[1:2] * kf[1:2] + kf[2:3] * kf[2:3]
    scale = scale_s / (1.0 + ksq)
    step = 32

    def rows(i, carry):
        at = pl.multiple_of(i * step, step)
        d = damp_ref[pl.ds(pl.multiple_of(start + at, step), step), :]
        filt_ref[pl.ds(at, step), :] = jnp.exp(-(d * ksq)) * scale
        return carry

    lax.fori_loop(0, half // step, rows, 0)
    w_in_t_ref[...] = w_in_ref[:, pl.ds(start, half)].T


def start_phase(rows_ref, kmat_ref, kone_ref, turn_ref, same_ref):
    first = rows_ref.shape[1] - META
    meta = rows_ref[:, first:]
    turn_ref[...] = dot(meta, kmat_ref[...], 1, 0)
    lane = lax.broadcasted_iota(jnp.int32, meta.shape, 1).astype(F32)
    one = jnp.where(meta.astype(F32)[:, 3:4] == lane, 1.0, 0.0).astype(BF)
    same_ref[...] = dot(one, kone_ref[...], 1, 0)


def phase_tile(turn_ref, same_ref, phase_ref, at, first, count):
    span = slice(first, first + count)
    kcount = turn_ref.shape[1]
    turn = turn_ref[at, span]
    same = same_ref[at, span]
    rest = turn - jnp.floor(turn + 0.5)
    square = rest * rest
    cosine = square * COS_POLY[-1] + COS_POLY[-2]
    for c in COS_POLY[-3::-1]:
        cosine = cosine * square + c
    sine = square * SIN_POLY[-1] + SIN_POLY[-2]
    for c in SIN_POLY[-3::-1]:
        sine = sine * square + c
    sine = sine * rest
    held = sine * same
    phase_ref[at, span] = (same - held * sine).astype(BF)
    phase_ref[at, kcount + first : kcount + first + count] = (held * cosine).astype(BF)


def fill_stack(rows_ref, w_in_t_ref, w_out_half, stack_ref):
    half = w_in_t_ref.shape[0]
    width = w_in_t_ref.shape[1]
    stack_ref[0:half, :] = dot(w_in_t_ref[...], rows_ref[:, 0:width], 1, 1).astype(BF)
    stack_ref[half:, :] = dot(w_out_half, rows_ref[:, width : 2 * width], 1, 1).astype(BF)


def half_of(ref, shard_ref, half):
    return ref[pl.ds(pl.multiple_of(shard_ref[0] * half, half), half), :]


def own_kernel(
    shard_ref, own_ref, kmat_ref, kone_ref, w_in_t_ref, w_out_ref, phase_ref, stack_ref, part_ref,
    turn_ref, same_ref,
):
    start_phase(own_ref, kmat_ref, kone_ref, turn_ref, same_ref)
    fill_stack(own_ref, w_in_t_ref, half_of(w_out_ref, shard_ref, w_in_t_ref.shape[0]), stack_ref)
    slots, kcount = turn_ref.shape
    chunk = 256

    def structure(first):
        for at in (first, kcount + first):
            span = slice(at, at + chunk)
            part_ref[:, span] = dot(stack_ref[...], phase_ref[:, span], 1, 0)

    for first in range(0, kcount, chunk):
        if first:
            structure(first - chunk)
        for row in range(0, slots, 16):
            phase_tile(turn_ref, same_ref, phase_ref, slice(row, row + 16), first, chunk)
    structure(kcount - chunk)


def forward_kernel(
    shard_ref, oth_ref, part_ref, phase_own_ref, kmat_ref, kone_ref, filt_ref, w_in_t_ref,
    w_out_ref,
    phase_ref, stack_ref, msg_own_ref, msg_oth_ref,
    turn_ref, same_ref, scaled_ref, scale_m,
):
    half = w_in_t_ref.shape[0]
    fill_stack(oth_ref, w_in_t_ref, half_of(w_out_ref, shard_ref, half), stack_ref)
    start_phase(oth_ref, kmat_ref, kone_ref, turn_ref, same_ref)
    slots, kcount = turn_ref.shape
    chunk = 512

    def structure(first):
        filt = filt_ref[:, first : first + chunk]
        for at in (first, kcount + first):
            span = slice(at, at + chunk)
            total = part_ref[0:half, span] + dot(stack_ref[0:half, :], phase_ref[:, span], 1, 0)
            scaled_ref[:, span] = (total * filt).astype(BF)

    for first in range(0, kcount, chunk):
        if first:
            structure(first - chunk)
        for row in range(0, slots, 16):
            phase_tile(turn_ref, same_ref, phase_ref, slice(row, row + 16), first, chunk)
    structure(kcount - chunk)
    for phase, out in ((phase_own_ref, msg_own_ref), (phase_ref, msg_oth_ref)):
        out[...] = (scale_m * dot(scaled_ref[...], phase[...], 1, 1)).astype(BF)


def backward_kernel(
    own_ref, oth_ref, part_ref, phase_own_ref, phase_oth_ref, stack_ref, msg_own_ref, msg_oth_ref,
    filt_ref, grad_ref, scaled_ref, scale_m,
):
    half = msg_own_ref.shape[0]
    width = grad_ref.shape[1]
    kcount = filt_ref.shape[1]
    chunk = 512
    for at in range(0, 2 * kcount, chunk):
        span = slice(at, at + chunk)
        filt = filt_ref[:, at % kcount : at % kcount + chunk]
        total = part_ref[half:, span] + dot(stack_ref[half:, :], phase_oth_ref[:, span], 1, 0)
        scaled_ref[:, span] = (total * filt).astype(BF)
    total = dot(msg_own_ref[...], own_ref[:, width : 2 * width], 1, 0)
    total += dot(msg_oth_ref[...], oth_ref[:, width : 2 * width], 1, 0)
    grad_ref[0:half, :] = total.astype(BF)
    back_own = (scale_m * dot(scaled_ref[...], phase_own_ref[...], 1, 1)).astype(BF)
    back_oth = (scale_m * dot(scaled_ref[...], phase_oth_ref[...], 1, 1)).astype(BF)
    total = dot(back_own, own_ref[:, 0:width], 1, 0)
    total += dot(back_oth, oth_ref[:, 0:width], 1, 0)
    grad_ref[half:, :] = total.astype(BF)


def change_kernel(shard_ref, msg_ref, got_ref, w_out_ref, grad_ref, out_ref):
    half = msg_ref.shape[0]
    mine = pl.multiple_of(shard_ref[0] * half, half)
    other = pl.multiple_of((1 - shard_ref[0]) * half, half)
    change = dot(msg_ref[...], w_out_ref[pl.ds(mine, half), :], 0, 0)
    change += dot(got_ref[...], w_out_ref[pl.ds(other, half), :], 0, 0)
    change = change.astype(BF)
    step = half // PLANE
    for q in range(PLANE):
        out_ref[q, 0:step] = change[q * step : (q + 1) * step]
        out_ref[q, step : 2 * step] = grad_ref[q * step : (q + 1) * step]
        out_ref[q, 2 * step :] = grad_ref[half + q * step : half + (q + 1) * step]


def plane_sum_kernel(recv_ref, out_ref):
    planes, block = out_ref.shape[0], recv_ref.shape[1] // 3
    slots = PLANE * block
    change = jnp.concatenate([recv_ref[q, 0:block] for q in range(PLANE)], axis=0)
    to = lax.broadcasted_iota(jnp.int32, (slots, slots), 0)
    of = lax.broadcasted_iota(jnp.int32, (slots, slots), 1)
    width = 2 * PLANE
    source = ((to & 31) >> 1) * block + (to >> 5) * 2 + (to & 1)
    move = jnp.where(source == of, 1.0, 0.0).astype(BF)
    change = dot(move, change, 1, 0).astype(BF)
    total = recv_ref[0, block:].astype(F32)
    for q in range(1, PLANE):
        total += recv_ref[q, block:].astype(F32)
    total = total.astype(BF)
    for z in range(planes):
        out_ref[z, 0:width] = change[z * width : (z + 1) * width]
        out_ref[z, width:] = total


def column_sum_kernel(recv_ref, out_ref, norm_factor):
    first = recv_ref.shape[1] - out_ref.shape[1]
    total = recv_ref[0, first:].astype(F32)
    for z in range(1, recv_ref.shape[0]):
        total += recv_ref[z, first:].astype(F32)
    total = (total * norm_factor).astype(BF)
    for q in range(out_ref.shape[0]):
        out_ref[q] = total


def place_half(ref, member, grad_in_hbm, grad_out_hbm, in_ref, out_ref, sems):
    block = ref.shape[1] // 2
    half = PLANE * block
    start = pl.multiple_of(member * half, half)
    copies = []

    def send(src, dst):
        copies.append(pltpu.make_async_copy(src, dst, sems.at[len(copies)]))
        copies[-1].start()

    for first in range(0, PLANE, 8):
        for q in range(first, first + 8):
            out_ref[q * block : (q + 1) * block, :] = ref[q, 0:block].astype(F32)
        at = pl.ds(pl.multiple_of(start + first * block, 8 * block), 8 * block)
        send(out_ref.at[first * block : (first + 8) * block, :], grad_out_hbm.at[at, :])
    into = jnp.concatenate([ref[q, block:] for q in range(PLANE)], axis=0)
    for first in range(0, into.shape[1], 128):
        span = slice(first, first + 128)
        in_ref[span, :] = into[:, span].astype(F32).T
        send(in_ref.at[span, :], grad_in_hbm.at[span, pl.ds(start, half)])
    return copies


def own_final_kernel(
    shard_ref, feat_ref, recv_ref, own_ref, half_ref,
    new_hbm, grad_in_hbm, grad_out_hbm,
    in_ref, out_ref, sems, new_ref, new_sem,
):
    copies = place_half(half_ref, shard_ref[0], grad_in_hbm, grad_out_hbm, in_ref, out_ref, sems)
    rows = feat_ref.shape[0]
    planes = recv_ref.shape[0]
    width = 2 * PLANE
    owner_row = own_ref[...].astype(F32)
    owner = as_column(owner_row)
    first = lax.broadcasted_iota(jnp.int32, (rows, rows), 0)
    second = lax.broadcasted_iota(jnp.int32, (rows, rows), 1)
    earlier = (owner == owner_row) & (second < first)
    rank = jnp.sum(jnp.where(earlier, 1.0, 0.0), axis=1, keepdims=True)
    first, second = place_of(owner.astype(jnp.int32), shard_ref[0])
    slot = (second * PLANE + first) * 2 + rank.astype(jnp.int32)
    pick = jnp.where(
        slot == lax.broadcasted_iota(jnp.int32, (rows, planes * width), 1), 1.0, 0.0
    ).astype(BF)
    change = jnp.concatenate([recv_ref[z, 0:width] for z in range(planes)], axis=0)
    new_ref[...] = (feat_ref[...].astype(F32) + dot(pick, change, 1, 0)).astype(BF)
    new = pltpu.make_async_copy(new_ref, new_hbm, new_sem)
    new.start()
    for copy in (*copies, new):
        copy.wait()


def other_final_kernel(
    shard_ref, half_ref, _grad_in, _grad_out, grad_in_hbm, grad_out_hbm, in_ref, out_ref, sems
):
    for copy in place_half(
        half_ref, 1 - shard_ref[0], grad_in_hbm, grad_out_hbm, in_ref, out_ref, sems
    ):
        copy.wait()


def local(
    features,
    norm_gain,
    w_in,
    w_out,
    cotangent,
    positions,
    crystal_of_atom,
    atom_owner,
    k_index,
    k_crystal,
    damping,
):
    rows, width = features.shape
    around, plane, column_set = hop_sets()
    groups = lax.axis_size("dp")
    planes = groups // PLANE
    members = lax.axis_size("shard")
    capacity = 2 * rows // groups
    slots = groups * capacity
    half = width // members
    kcount = k_index.shape[1]
    scale_s = (slots * members / CRY_DEV) ** (-0.5)
    scale_m = (kcount / CRY_DEV) ** (-0.5)
    norm_factor = (rows * groups * members) ** (-0.5)
    shard = lax.axis_index("shard").astype(jnp.int32).reshape(1)
    swap = [(0, 1), (1, 0)]

    owner_row = atom_owner.reshape(1, rows)
    packed = 2 * width + META
    operands = [
        shard,
        features,
        norm_gain.reshape(1, width),
        cotangent,
        positions,
        crystal_of_atom.reshape(1, rows),
        owner_row,
    ]
    send = call(
        prep_kernel,
        jax.ShapeDtypeStruct((groups, capacity, packed), BF),
        operands,
        scratch=[pltpu.VMEM(a.shape, a.dtype) for a in operands[1:]]
        + [
            pltpu.SemaphoreType.DMA((len(operands) - 1,)),
            pltpu.VMEM((groups, capacity, packed), BF),
            pltpu.SemaphoreType.DMA((3,)),
        ],
        specs=[SM] + [HB] * (len(operands) - 1),
        outs=HB,
        limit=FULL_VMEM,
    )
    recv = exchange(send, around)
    own = recv.reshape(slots, packed)
    kmat, kone, filt, w_in_t = call(
        functools.partial(static_kernel, scale_s=scale_s),
        (
            jax.ShapeDtypeStruct((META, kcount), BF),
            jax.ShapeDtypeStruct((META, kcount), BF),
            jax.ShapeDtypeStruct((half, kcount), F32),
            jax.ShapeDtypeStruct((half, width), BF),
        ),
        [shard, k_index, k_crystal.reshape(1, kcount), damping.reshape(width, 1), w_in],
        specs=[SM, VM, VM, VM, VM],
        flops=4_000_000_000,
    )
    own, kmat, kone, filt, w_in_t = lax.optimization_barrier((own, kmat, kone, filt, w_in_t))
    other = lax.ppermute(own, "shard", swap)
    phase_shape = jax.ShapeDtypeStruct((slots, 2 * kcount), BF)
    stack_shape = jax.ShapeDtypeStruct((2 * half, slots), BF)
    message_shape = jax.ShapeDtypeStruct((half, slots), BF)
    turn = pltpu.VMEM((slots, kcount), F32)
    scaled = pltpu.VMEM((half, 2 * kcount), BF)
    phase_own, _, part = call(
        own_kernel,
        (phase_shape, stack_shape, jax.ShapeDtypeStruct((2 * half, 2 * kcount), F32)),
        [shard, own, kmat, kone, w_in_t, w_out],
        scratch=[turn, turn],
        specs=[SM] + [VM] * 5,
        flops=4_000_000_000,
    )
    phase_oth, stack_oth, message, message_oth = call(
        functools.partial(forward_kernel, scale_m=scale_m),
        (phase_shape, stack_shape, message_shape, message_shape),
        [shard, other, part, phase_own, kmat, kone, filt, w_in_t, w_out],
        scratch=[turn, turn, scaled],
        specs=[SM] + [VM] * 8,
    )
    got = lax.ppermute(message_oth, "shard", swap)
    grads = call(
        functools.partial(backward_kernel, scale_m=scale_m),
        jax.ShapeDtypeStruct((2 * half, width), BF),
        [own, other, part, phase_own, phase_oth, stack_oth, message, message_oth, filt],
        scratch=[scaled],
        flops=4_000_000_000,
    )
    block = slots // PLANE
    back = call(
        change_kernel,
        jax.ShapeDtypeStruct((PLANE, 3 * block, width), BF),
        [shard, message, got, w_out, grads],
        specs=[SM] + [VM] * 4,
    )
    recv_plane = exchange(back, plane)
    column = call(
        plane_sum_kernel,
        jax.ShapeDtypeStruct((planes, slots // planes + 2 * block, width), BF),
        [recv_plane],
    )
    recv_column = exchange(column, column_set)
    share = call(
        functools.partial(column_sum_kernel, norm_factor=norm_factor),
        jax.ShapeDtypeStruct((PLANE, 2 * block, width), BF),
        [recv_column],
    )
    mine = exchange(share, plane)
    theirs = lax.ppermute(mine, "shard", swap)
    grads = (jax.ShapeDtypeStruct((width, width), F32),) * 2
    placing = [
        pltpu.VMEM((width, half), F32),
        pltpu.VMEM((half, width), F32),
        pltpu.SemaphoreType.DMA((6,)),
    ]
    updated, *first = call(
        own_final_kernel,
        (jax.ShapeDtypeStruct((rows, width), BF), *grads),
        [shard, features, recv_column, owner_row, mine],
        scratch=[*placing, pltpu.VMEM((rows, width), BF), pltpu.SemaphoreType.DMA],
        specs=[SM, VM, VM, VM, VM],
        outs=(HB, HB, HB),
        flops=4_000_000_000,
    )
    grad_w_in, grad_w_out = call(
        other_final_kernel,
        grads,
        [shard, theirs, *first],
        scratch=placing,
        specs=[SM, VM, HB, HB],
        outs=(HB, HB),
        aliases={2: 0, 3: 1},
    )
    return (updated, grad_w_in, grad_w_out)


def solution(mesh):
    every = ("dp", "shard")
    in_specs = (
        P(every, None),
        P(),
        P(),
        P(),
        P(every, None),
        P(None, every),
        P(every),
        P(every, None),
        P(None, "dp"),
        P("dp"),
        P(),
    )
    out_specs = (P(every, None), P(), P())
    return jax.shard_map(local, mesh=mesh, in_specs=in_specs, out_specs=out_specs, check_vma=False)
```

```python
import functools
import math

import jax
import jax.numpy as jnp
from jax import lax
from jax.experimental import pallas as pl
from jax.experimental.pallas import tpu as pltpu
from jax.sharding import PartitionSpec as P

CRY_DEV = 8
BF = jnp.bfloat16
F32 = jnp.float32
VMEM_LIMIT = 24 * 1024 * 1024
FULL_VMEM = 63 * 1024 * 1024
META = 128

COS_POLY = (
    1.4142135381698608,
    -6.978850841522217,
    5.739460468292236,
    -1.883557915687561,
    0.3106880187988281,
)
SIN_POLY = (
    4.442883014678955,
    -7.308245658874512,
    3.606354236602783,
    -0.8461116552352905,
    0.1098245158791542,
)

VM = pl.BlockSpec(memory_space=pltpu.VMEM)
SM = pl.BlockSpec(memory_space=pltpu.SMEM)
HB = pl.BlockSpec(memory_space=pltpu.MemorySpace.HBM)
PLANE = 16


def place_of(owner, shard):
    first = jnp.where(shard == 0, 15 - (owner & 15), 15 - ((owner >> 4) * 2 + (owner & 1)))
    second = jnp.where(shard == 0, 7 - (owner >> 4), 7 - ((owner >> 1) & 7))
    return first, second


def hop_sets():
    every = [(z, x, y) for z in range(8) for x in range(4) for y in range(4)]

    def split(shard):
        if shard == 0:
            return {(15 - (x * 4 + y), 7 - (z)): (z, x, y) for z, x, y in every}
        return {(15 - (z * 2 + y % 2), 7 - (x * 2 + y // 2)): (z, x, y) for z, x, y in every}

    around, first, second = [], [], []
    for shard in range(2):
        at = {key: ((z * 4 + x) * 4 + y) * 2 + shard for key, (z, x, y) in split(shard).items()}
        around.append([at[i, j] for i in range(PLANE) for j in range(8)])
        first += [[at[i, j] for i in range(PLANE)] for j in range(8)]
        second += [[at[i, j] for j in range(8)] for i in range(PLANE)]
    return around, first, second


def exchange(array, sets):
    return lax.all_to_all(
        array,
        ("dp", "shard"),
        split_axis=0,
        concat_axis=0,
        axis_index_groups=sets,
        tiled=True,
    )


def call(body, out_shape, inputs, scratch=(), specs=None, outs=None, flops=1_000_000, aliases=None,
         limit=VMEM_LIMIT):
    return pl.pallas_call(
        body,
        out_shape=out_shape,
        in_specs=specs if specs is not None else [VM] * len(inputs),
        out_specs=outs if outs is not None else jax.tree.map(lambda _: VM, out_shape),
        scratch_shapes=list(scratch),
        input_output_aliases=aliases or {},
        compiler_params=pltpu.CompilerParams(vmem_limit_bytes=limit),
        cost_estimate=pl.CostEstimate(flops=flops, bytes_accessed=1_000_000, transcendentals=0),
    )(*inputs)


def dot(a, b, ca, cb):
    return lax.dot_general(a, b, (((ca,), (cb,)), ((), ())), preferred_element_type=F32)


def as_column(row):
    n = row.shape[1]
    diagonal = lax.broadcasted_iota(jnp.int32, (n, n), 0) == lax.broadcasted_iota(
        jnp.int32, (n, n), 1
    )
    return jnp.sum(jnp.where(diagonal, row, 0.0), axis=1, keepdims=True)


def prep_kernel(
    shard_ref, feat_hbm, gain_hbm, cot_hbm, pos_hbm, cry_hbm, own_hbm, out_hbm,
    feat_ref, gain_ref, cot_ref, pos_ref, cry_ref, own_ref, sems, stage_ref, out_sems,
):
    sources = (feat_hbm, gain_hbm, cot_hbm, pos_hbm, cry_hbm, own_hbm)
    targets = (feat_ref, gain_ref, cot_ref, pos_ref, cry_ref, own_ref)
    feat_in, gain_in, cot_in, pos_in, cry_in, own_in = copies = [
        pltpu.make_async_copy(src, dst, sems.at[i])
        for i, (src, dst) in enumerate(zip(sources, targets))
    ]
    for i in (5, 2, 0, 1, 3, 4):
        copies[i].start()
    rows, width = feat_ref.shape
    slots = out_hbm.shape[0] * out_hbm.shape[1]
    own_in.wait()
    owner = own_ref[...].astype(F32)
    first = lax.broadcasted_iota(jnp.int32, (rows, rows), 0)
    second = lax.broadcasted_iota(jnp.int32, (rows, rows), 1)
    earlier = (as_column(owner) == owner) & (first < second)
    rank = jnp.sum(jnp.where(earlier, 1.0, 0.0), axis=0, keepdims=True)
    first, second = place_of(own_ref[...], shard_ref[0])
    slot = (first * 8 + second) * 2 + rank.astype(jnp.int32)
    place = jnp.where(
        slot == lax.broadcasted_iota(jnp.int32, (slots, rows), 0), 1.0, 0.0
    ).astype(BF)
    sent = []

    def send(first, part):
        span = slice(first, first + part.shape[1])
        stage_ref[:, :, span] = part.astype(BF).reshape(slots // 2, 2, part.shape[1])
        copy = pltpu.make_async_copy(
            stage_ref.at[:, :, span], out_hbm.at[:, :, span], out_sems.at[len(sent)]
        )
        copy.start()
        sent.append(copy)

    cot_in.wait()
    send(width, dot(place, cot_ref[...], 1, 0))
    feat_in.wait()
    gain_in.wait()
    hidden = feat_ref[...].astype(F32)
    normed = (
        hidden
        * lax.rsqrt(jnp.mean(hidden * hidden, axis=-1, keepdims=True) + 1e-06)
        * gain_ref[...]
    ).astype(BF)
    send(0, dot(place, normed, 1, 0))
    pos_in.wait()
    cry_in.wait()
    meta = jnp.concatenate(
        [
            pos_ref[...].astype(F32),
            cry_ref[...].astype(F32),
            jnp.zeros((META - 4, rows), F32),
        ],
        axis=0,
    ).astype(BF)
    send(2 * width, dot(place, meta, 1, 1))
    for copy in sent:
        copy.wait()


def static_kernel(
    shard_ref, k_ref, kc_ref, damp_ref, w_in_ref, kmat_ref, kone_ref, filt_ref, w_in_t_ref, scale_s
):
    half = filt_ref.shape[0]
    start = pl.multiple_of(shard_ref[0] * half, half)
    kf = k_ref[...].astype(F32)
    kmat_ref[...] = jnp.zeros(kmat_ref.shape, BF)
    kmat_ref[0:16, :] = jnp.concatenate([kf, jnp.zeros((13, kf.shape[1]), F32)], axis=0).astype(BF)
    crystal = lax.broadcasted_iota(jnp.int32, kone_ref.shape, 0)
    kone_ref[...] = jnp.where(kc_ref[...] == crystal, 1.0, 0.0).astype(BF)
    ksq = kf[0:1] * kf[0:1] + kf[1:2] * kf[1:2] + kf[2:3] * kf[2:3]
    scale = scale_s / (1.0 + ksq)
    step = 32

    def rows(i, carry):
        at = pl.multiple_of(i * step, step)
        d = damp_ref[pl.ds(pl.multiple_of(start + at, step), step), :]
        filt_ref[pl.ds(at, step), :] = jnp.exp(-(d * ksq)) * scale
        return carry

    lax.fori_loop(0, half // step, rows, 0)
    w_in_t_ref[...] = w_in_ref[:, pl.ds(start, half)].T


def start_phase(rows_ref, kmat_ref, kone_ref, turn_ref, same_ref):
    first = rows_ref.shape[1] - META
    meta = rows_ref[:, first:]
    turn_ref[...] = dot(meta, kmat_ref[...], 1, 0)
    lane = lax.broadcasted_iota(jnp.int32, meta.shape, 1).astype(F32)
    one = jnp.where(meta.astype(F32)[:, 3:4] == lane, 1.0, 0.0).astype(BF)
    same_ref[...] = dot(one, kone_ref[...], 1, 0)


def phase_tile(turn_ref, same_ref, phase_ref, at, first, count):
    span = slice(first, first + count)
    kcount = turn_ref.shape[1]
    turn = turn_ref[at, span]
    same = same_ref[at, span]
    rest = turn - jnp.floor(turn + 0.5)
    square = rest * rest
    cosine = square * COS_POLY[-1] + COS_POLY[-2]
    for c in COS_POLY[-3::-1]:
        cosine = cosine * square + c
    sine = square * SIN_POLY[-1] + SIN_POLY[-2]
    for c in SIN_POLY[-3::-1]:
        sine = sine * square + c
    sine = sine * rest
    held = sine * same
    phase_ref[at, span] = (same - held * sine).astype(BF)
    phase_ref[at, kcount + first : kcount + first + count] = (held * cosine).astype(BF)


def fill_stack(rows_ref, w_in_t_ref, w_out_half, stack_ref):
    half = w_in_t_ref.shape[0]
    width = w_in_t_ref.shape[1]
    stack_ref[0:half, :] = dot(w_in_t_ref[...], rows_ref[:, 0:width], 1, 1).astype(BF)
    stack_ref[half:, :] = dot(w_out_half, rows_ref[:, width : 2 * width], 1, 1).astype(BF)


def half_of(ref, shard_ref, half):
    return ref[pl.ds(pl.multiple_of(shard_ref[0] * half, half), half), :]


def own_kernel(
    shard_ref, own_ref, kmat_ref, kone_ref, w_in_t_ref, w_out_ref, phase_ref, stack_ref, part_ref,
    turn_ref, same_ref,
):
    start_phase(own_ref, kmat_ref, kone_ref, turn_ref, same_ref)
    fill_stack(own_ref, w_in_t_ref, half_of(w_out_ref, shard_ref, w_in_t_ref.shape[0]), stack_ref)
    slots, kcount = turn_ref.shape
    chunk = 256

    def structure(first):
        for at in (first, kcount + first):
            span = slice(at, at + chunk)
            part_ref[:, span] = dot(stack_ref[...], phase_ref[:, span], 1, 0)

    for first in range(0, kcount, chunk):
        if first:
            structure(first - chunk)
        for row in range(0, slots, 16):
            phase_tile(turn_ref, same_ref, phase_ref, slice(row, row + 16), first, chunk)
    structure(kcount - chunk)


def forward_kernel(
    shard_ref, oth_ref, part_ref, phase_own_ref, kmat_ref, kone_ref, filt_ref, w_in_t_ref,
    w_out_ref,
    phase_ref, stack_ref, msg_own_ref, msg_oth_ref,
    turn_ref, same_ref, scaled_ref, scale_m,
):
    half = w_in_t_ref.shape[0]
    fill_stack(oth_ref, w_in_t_ref, half_of(w_out_ref, shard_ref, half), stack_ref)
    start_phase(oth_ref, kmat_ref, kone_ref, turn_ref, same_ref)
    slots, kcount = turn_ref.shape
    chunk = 512

    def structure(first):
        filt = filt_ref[:, first : first + chunk]
        for at in (first, kcount + first):
            span = slice(at, at + chunk)
            total = part_ref[0:half, span] + dot(stack_ref[0:half, :], phase_ref[:, span], 1, 0)
            scaled_ref[:, span] = (total * filt).astype(BF)

    for first in range(0, kcount, chunk):
        if first:
            structure(first - chunk)
        for row in range(0, slots, 16):
            phase_tile(turn_ref, same_ref, phase_ref, slice(row, row + 16), first, chunk)
    structure(kcount - chunk)
    for phase, out in ((phase_own_ref, msg_own_ref), (phase_ref, msg_oth_ref)):
        out[...] = (scale_m * dot(scaled_ref[...], phase[...], 1, 1)).astype(BF)


def backward_kernel(
    own_ref, oth_ref, part_ref, phase_own_ref, phase_oth_ref, stack_ref, msg_own_ref, msg_oth_ref,
    filt_ref, grad_ref, scaled_ref, scale_m,
):
    half = msg_own_ref.shape[0]
    width = grad_ref.shape[1]
    kcount = filt_ref.shape[1]
    chunk = 512
    for at in range(0, 2 * kcount, chunk):
        span = slice(at, at + chunk)
        filt = filt_ref[:, at % kcount : at % kcount + chunk]
        total = part_ref[half:, span] + dot(stack_ref[half:, :], phase_oth_ref[:, span], 1, 0)
        scaled_ref[:, span] = (total * filt).astype(BF)
    total = dot(msg_own_ref[...], own_ref[:, width : 2 * width], 1, 0)
    total += dot(msg_oth_ref[...], oth_ref[:, width : 2 * width], 1, 0)
    grad_ref[0:half, :] = total.astype(BF)
    back_own = (scale_m * dot(scaled_ref[...], phase_own_ref[...], 1, 1)).astype(BF)
    back_oth = (scale_m * dot(scaled_ref[...], phase_oth_ref[...], 1, 1)).astype(BF)
    total = dot(back_own, own_ref[:, 0:width], 1, 0)
    total += dot(back_oth, oth_ref[:, 0:width], 1, 0)
    grad_ref[half:, :] = total.astype(BF)


def change_kernel(shard_ref, msg_ref, got_ref, w_out_ref, grad_ref, out_ref):
    half = msg_ref.shape[0]
    mine = pl.multiple_of(shard_ref[0] * half, half)
    other = pl.multiple_of((1 - shard_ref[0]) * half, half)
    change = dot(msg_ref[...], w_out_ref[pl.ds(mine, half), :], 0, 0)
    change += dot(got_ref[...], w_out_ref[pl.ds(other, half), :], 0, 0)
    change = change.astype(BF)
    step = half // PLANE
    for q in range(PLANE):
        out_ref[q, 0:step] = change[q * step : (q + 1) * step]
        out_ref[q, step : 2 * step] = grad_ref[q * step : (q + 1) * step]
        out_ref[q, 2 * step :] = grad_ref[half + q * step : half + (q + 1) * step]


def plane_sum_kernel(recv_ref, out_ref):
    planes, block = out_ref.shape[0], recv_ref.shape[1] // 3
    slots = PLANE * block
    change = jnp.concatenate([recv_ref[q, 0:block] for q in range(PLANE)], axis=0)
    to = lax.broadcasted_iota(jnp.int32, (slots, slots), 0)
    of = lax.broadcasted_iota(jnp.int32, (slots, slots), 1)
    width = 2 * PLANE
    source = ((to & 31) >> 1) * block + (to >> 5) * 2 + (to & 1)
    move = jnp.where(source == of, 1.0, 0.0).astype(BF)
    change = dot(move, change, 1, 0).astype(BF)
    total = recv_ref[0, block:].astype(F32)
    for q in range(1, PLANE):
        total += recv_ref[q, block:].astype(F32)
    total = total.astype(BF)
    for z in range(planes):
        out_ref[z, 0:width] = change[z * width : (z + 1) * width]
        out_ref[z, width:] = total


def column_sum_kernel(recv_ref, out_ref, norm_factor):
    first = recv_ref.shape[1] - out_ref.shape[1]
    total = recv_ref[0, first:].astype(F32)
    for z in range(1, recv_ref.shape[0]):
        total += recv_ref[z, first:].astype(F32)
    total = (total * norm_factor).astype(BF)
    for q in range(out_ref.shape[0]):
        out_ref[q] = total


def place_half(ref, member, grad_in_hbm, grad_out_hbm, in_ref, out_ref, sems):
    block = ref.shape[1] // 2
    half = PLANE * block
    start = pl.multiple_of(member * half, half)
    copies = []

    def send(src, dst):
        copies.append(pltpu.make_async_copy(src, dst, sems.at[len(copies)]))
        copies[-1].start()

    for first in range(0, PLANE, 8):
        for q in range(first, first + 8):
            out_ref[q * block : (q + 1) * block, :] = ref[q, 0:block].astype(F32)
        at = pl.ds(pl.multiple_of(start + first * block, 8 * block), 8 * block)
        send(out_ref.at[first * block : (first + 8) * block, :], grad_out_hbm.at[at, :])
    into = jnp.concatenate([ref[q, block:] for q in range(PLANE)], axis=0)
    for first in range(0, into.shape[1], 128):
        span = slice(first, first + 128)
        in_ref[span, :] = into[:, span].astype(F32).T
        send(in_ref.at[span, :], grad_in_hbm.at[span, pl.ds(start, half)])
    return copies


def own_final_kernel(
    shard_ref, feat_ref, recv_ref, own_ref, half_ref,
    new_hbm, grad_in_hbm, grad_out_hbm,
    in_ref, out_ref, sems, new_ref, new_sem,
):
    copies = place_half(half_ref, shard_ref[0], grad_in_hbm, grad_out_hbm, in_ref, out_ref, sems)
    rows = feat_ref.shape[0]
    planes = recv_ref.shape[0]
    width = 2 * PLANE
    owner_row = own_ref[...].astype(F32)
    owner = as_column(owner_row)
    first = lax.broadcasted_iota(jnp.int32, (rows, rows), 0)
    second = lax.broadcasted_iota(jnp.int32, (rows, rows), 1)
    earlier = (owner == owner_row) & (second < first)
    rank = jnp.sum(jnp.where(earlier, 1.0, 0.0), axis=1, keepdims=True)
    first, second = place_of(owner.astype(jnp.int32), shard_ref[0])
    slot = (second * PLANE + first) * 2 + rank.astype(jnp.int32)
    pick = jnp.where(
        slot == lax.broadcasted_iota(jnp.int32, (rows, planes * width), 1), 1.0, 0.0
    ).astype(BF)
    change = jnp.concatenate([recv_ref[z, 0:width] for z in range(planes)], axis=0)
    new_ref[...] = (feat_ref[...].astype(F32) + dot(pick, change, 1, 0)).astype(BF)
    new = pltpu.make_async_copy(new_ref, new_hbm, new_sem)
    new.start()
    for copy in (*copies, new):
        copy.wait()


def other_final_kernel(
    shard_ref, half_ref, _grad_in, _grad_out, grad_in_hbm, grad_out_hbm, in_ref, out_ref, sems
):
    for copy in place_half(
        half_ref, 1 - shard_ref[0], grad_in_hbm, grad_out_hbm, in_ref, out_ref, sems
    ):
        copy.wait()


def local(
    features,
    norm_gain,
    w_in,
    w_out,
    cotangent,
    positions,
    crystal_of_atom,
    atom_owner,
    k_index,
    k_crystal,
    damping,
):
    rows, width = features.shape
    around, plane, column_set = hop_sets()
    groups = lax.axis_size("dp")
    planes = groups // PLANE
    members = lax.axis_size("shard")
    capacity = 2 * rows // groups
    slots = groups * capacity
    half = width // members
    kcount = k_index.shape[1]
    scale_s = (slots * members / CRY_DEV) ** (-0.5)
    scale_m = (kcount / CRY_DEV) ** (-0.5)
    norm_factor = (rows * groups * members) ** (-0.5)
    shard = lax.axis_index("shard").astype(jnp.int32).reshape(1)
    swap = [(0, 1), (1, 0)]

    owner_row = atom_owner.reshape(1, rows)
    packed = 2 * width + META
    operands = [
        shard,
        features,
        norm_gain.reshape(1, width),
        cotangent,
        positions,
        crystal_of_atom.reshape(1, rows),
        owner_row,
    ]
    send = call(
        prep_kernel,
        jax.ShapeDtypeStruct((groups, capacity, packed), BF),
        operands,
        scratch=[pltpu.VMEM(a.shape, a.dtype) for a in operands[1:]]
        + [
            pltpu.SemaphoreType.DMA((len(operands) - 1,)),
            pltpu.VMEM((groups, capacity, packed), BF),
            pltpu.SemaphoreType.DMA((3,)),
        ],
        specs=[SM] + [HB] * (len(operands) - 1),
        outs=HB,
        limit=FULL_VMEM,
    )
    recv = exchange(send, around)
    own = recv.reshape(slots, packed)
    kmat, kone, filt, w_in_t = call(
        functools.partial(static_kernel, scale_s=scale_s),
        (
            jax.ShapeDtypeStruct((META, kcount), BF),
            jax.ShapeDtypeStruct((META, kcount), BF),
            jax.ShapeDtypeStruct((half, kcount), F32),
            jax.ShapeDtypeStruct((half, width), BF),
        ),
        [shard, k_index, k_crystal.reshape(1, kcount), damping.reshape(width, 1), w_in],
        specs=[SM, VM, VM, VM, VM],
        flops=4_000_000_000,
    )
    own, kmat, kone, filt, w_in_t = lax.optimization_barrier((own, kmat, kone, filt, w_in_t))
    other = lax.ppermute(own, "shard", swap)
    phase_shape = jax.ShapeDtypeStruct((slots, 2 * kcount), BF)
    stack_shape = jax.ShapeDtypeStruct((2 * half, slots), BF)
    message_shape = jax.ShapeDtypeStruct((half, slots), BF)
    turn = pltpu.VMEM((slots, kcount), F32)
    scaled = pltpu.VMEM((half, 2 * kcount), BF)
    phase_own, _, part = call(
        own_kernel,
        (phase_shape, stack_shape, jax.ShapeDtypeStruct((2 * half, 2 * kcount), F32)),
        [shard, own, kmat, kone, w_in_t, w_out],
        scratch=[turn, turn],
        specs=[SM] + [VM] * 5,
        flops=4_000_000_000,
    )
    phase_oth, stack_oth, message, message_oth = call(
        functools.partial(forward_kernel, scale_m=scale_m),
        (phase_shape, stack_shape, message_shape, message_shape),
        [shard, other, part, phase_own, kmat, kone, filt, w_in_t, w_out],
        scratch=[turn, turn, scaled],
        specs=[SM] + [VM] * 8,
    )
    got = lax.ppermute(message_oth, "shard", swap)
    grads = call(
        functools.partial(backward_kernel, scale_m=scale_m),
        jax.ShapeDtypeStruct((2 * half, width), BF),
        [own, other, part, phase_own, phase_oth, stack_oth, message, message_oth, filt],
        scratch=[scaled],
        flops=4_000_000_000,
    )
    block = slots // PLANE
    back = call(
        change_kernel,
        jax.ShapeDtypeStruct((PLANE, 3 * block, width), BF),
        [shard, message, got, w_out, grads],
        specs=[SM] + [VM] * 4,
    )
    recv_plane = exchange(back, plane)
    column = call(
        plane_sum_kernel,
        jax.ShapeDtypeStruct((planes, slots // planes + 2 * block, width), BF),
        [recv_plane],
    )
    recv_column = exchange(column, column_set)
    share = call(
        functools.partial(column_sum_kernel, norm_factor=norm_factor),
        jax.ShapeDtypeStruct((PLANE, 2 * block, width), BF),
        [recv_column],
    )
    mine = exchange(share, plane)
    theirs = lax.ppermute(mine, "shard", swap)
    grads = (jax.ShapeDtypeStruct((width, width), F32),) * 2
    placing = [
        pltpu.VMEM((width, half), F32),
        pltpu.VMEM((half, width), F32),
        pltpu.SemaphoreType.DMA((6,)),
    ]
    updated, *first = call(
        own_final_kernel,
        (jax.ShapeDtypeStruct((rows, width), BF), *grads),
        [shard, features, recv_column, owner_row, mine],
        scratch=[*placing, pltpu.VMEM((rows, width), BF), pltpu.SemaphoreType.DMA],
        specs=[SM, VM, VM, VM, VM],
        outs=(HB, HB, HB),
        flops=4_000_000_000,
    )
    grad_w_in, grad_w_out = call(
        other_final_kernel,
        grads,
        [shard, theirs, *first],
        scratch=placing,
        specs=[SM, VM, HB, HB],
        outs=(HB, HB),
        aliases={2: 0, 3: 1},
    )
    return (updated, grad_w_in, grad_w_out)


def solution(mesh):
    every = ("dp", "shard")
    in_specs = (
        P(every, None),
        P(),
        P(),
        P(),
        P(every, None),
        P(None, every),
        P(every),
        P(every, None),
        P(None, "dp"),
        P("dp"),
        P(),
    )
    out_specs = (P(every, None), P(), P())
    return jax.shard_map(local, mesh=mesh, in_specs=in_specs, out_specs=out_specs, check_vma=False)
```

```python
import functools
import math

import jax
import jax.numpy as jnp
from jax import lax
from jax.experimental import pallas as pl
from jax.experimental.pallas import tpu as pltpu
from jax.sharding import PartitionSpec as P

CRY_DEV = 8
BF = jnp.bfloat16
F32 = jnp.float32
VMEM_LIMIT = 24 * 1024 * 1024
FULL_VMEM = 63 * 1024 * 1024
META = 128

COS_POLY = (
    1.4142135381698608,
    -6.978850841522217,
    5.739460468292236,
    -1.883557915687561,
    0.3106880187988281,
)
SIN_POLY = (
    4.442883014678955,
    -7.308245658874512,
    3.606354236602783,
    -0.8461116552352905,
    0.1098245158791542,
)

VM = pl.BlockSpec(memory_space=pltpu.VMEM)
SM = pl.BlockSpec(memory_space=pltpu.SMEM)
HB = pl.BlockSpec(memory_space=pltpu.MemorySpace.HBM)
PLANE = 16


def place_of(owner, shard):
    first = jnp.where(shard == 0, 15 - ((owner & 3) * 4 + ((owner >> 2) & 3)), 15 - ((owner >> 4) * 2 + (owner & 1)))
    second = jnp.where(shard == 0, 7 - (owner >> 4), 7 - ((owner >> 1) & 7))
    return first, second


def hop_sets():
    every = [(z, x, y) for z in range(8) for x in range(4) for y in range(4)]

    def split(shard):
        if shard == 0:
            return {(15 - (y * 4 + x), 7 - (z)): (z, x, y) for z, x, y in every}
        return {(15 - (z * 2 + y % 2), 7 - (x * 2 + y // 2)): (z, x, y) for z, x, y in every}

    around, first, second = [], [], []
    for shard in range(2):
        at = {key: ((z * 4 + x) * 4 + y) * 2 + shard for key, (z, x, y) in split(shard).items()}
        around.append([at[i, j] for i in range(PLANE) for j in range(8)])
        first += [[at[i, j] for i in range(PLANE)] for j in range(8)]
        second += [[at[i, j] for j in range(8)] for i in range(PLANE)]
    return around, first, second


def exchange(array, sets):
    return lax.all_to_all(
        array,
        ("dp", "shard"),
        split_axis=0,
        concat_axis=0,
        axis_index_groups=sets,
        tiled=True,
    )


def call(body, out_shape, inputs, scratch=(), specs=None, outs=None, flops=1_000_000, aliases=None,
         limit=VMEM_LIMIT):
    return pl.pallas_call(
        body,
        out_shape=out_shape,
        in_specs=specs if specs is not None else [VM] * len(inputs),
        out_specs=outs if outs is not None else jax.tree.map(lambda _: VM, out_shape),
        scratch_shapes=list(scratch),
        input_output_aliases=aliases or {},
        compiler_params=pltpu.CompilerParams(vmem_limit_bytes=limit),
        cost_estimate=pl.CostEstimate(flops=flops, bytes_accessed=1_000_000, transcendentals=0),
    )(*inputs)


def dot(a, b, ca, cb):
    return lax.dot_general(a, b, (((ca,), (cb,)), ((), ())), preferred_element_type=F32)


def as_column(row):
    n = row.shape[1]
    diagonal = lax.broadcasted_iota(jnp.int32, (n, n), 0) == lax.broadcasted_iota(
        jnp.int32, (n, n), 1
    )
    return jnp.sum(jnp.where(diagonal, row, 0.0), axis=1, keepdims=True)


def prep_kernel(
    shard_ref, feat_hbm, gain_hbm, cot_hbm, pos_hbm, cry_hbm, own_hbm, out_hbm,
    feat_ref, gain_ref, cot_ref, pos_ref, cry_ref, own_ref, sems, stage_ref, out_sems,
):
    sources = (feat_hbm, gain_hbm, cot_hbm, pos_hbm, cry_hbm, own_hbm)
    targets = (feat_ref, gain_ref, cot_ref, pos_ref, cry_ref, own_ref)
    feat_in, gain_in, cot_in, pos_in, cry_in, own_in = copies = [
        pltpu.make_async_copy(src, dst, sems.at[i])
        for i, (src, dst) in enumerate(zip(sources, targets))
    ]
    for i in (5, 2, 0, 1, 3, 4):
        copies[i].start()
    rows, width = feat_ref.shape
    slots = out_hbm.shape[0] * out_hbm.shape[1]
    own_in.wait()
    owner = own_ref[...].astype(F32)
    first = lax.broadcasted_iota(jnp.int32, (rows, rows), 0)
    second = lax.broadcasted_iota(jnp.int32, (rows, rows), 1)
    earlier = (as_column(owner) == owner) & (first < second)
    rank = jnp.sum(jnp.where(earlier, 1.0, 0.0), axis=0, keepdims=True)
    first, second = place_of(own_ref[...], shard_ref[0])
    slot = (first * 8 + second) * 2 + rank.astype(jnp.int32)
    place = jnp.where(
        slot == lax.broadcasted_iota(jnp.int32, (slots, rows), 0), 1.0, 0.0
    ).astype(BF)
    sent = []

    def send(first, part):
        span = slice(first, first + part.shape[1])
        stage_ref[:, :, span] = part.astype(BF).reshape(slots // 2, 2, part.shape[1])
        copy = pltpu.make_async_copy(
            stage_ref.at[:, :, span], out_hbm.at[:, :, span], out_sems.at[len(sent)]
        )
        copy.start()
        sent.append(copy)

    cot_in.wait()
    send(width, dot(place, cot_ref[...], 1, 0))
    feat_in.wait()
    gain_in.wait()
    hidden = feat_ref[...].astype(F32)
    normed = (
        hidden
        * lax.rsqrt(jnp.mean(hidden * hidden, axis=-1, keepdims=True) + 1e-06)
        * gain_ref[...]
    ).astype(BF)
    send(0, dot(place, normed, 1, 0))
    pos_in.wait()
    cry_in.wait()
    meta = jnp.concatenate(
        [
            pos_ref[...].astype(F32),
            cry_ref[...].astype(F32),
            jnp.zeros((META - 4, rows), F32),
        ],
        axis=0,
    ).astype(BF)
    send(2 * width, dot(place, meta, 1, 1))
    for copy in sent:
        copy.wait()


def static_kernel(
    shard_ref, k_ref, kc_ref, damp_ref, w_in_ref, kmat_ref, kone_ref, filt_ref, w_in_t_ref, scale_s
):
    half = filt_ref.shape[0]
    start = pl.multiple_of(shard_ref[0] * half, half)
    kf = k_ref[...].astype(F32)
    kmat_ref[...] = jnp.zeros(kmat_ref.shape, BF)
    kmat_ref[0:16, :] = jnp.concatenate([kf, jnp.zeros((13, kf.shape[1]), F32)], axis=0).astype(BF)
    crystal = lax.broadcasted_iota(jnp.int32, kone_ref.shape, 0)
    kone_ref[...] = jnp.where(kc_ref[...] == crystal, 1.0, 0.0).astype(BF)
    ksq = kf[0:1] * kf[0:1] + kf[1:2] * kf[1:2] + kf[2:3] * kf[2:3]
    scale = scale_s / (1.0 + ksq)
    step = 32

    def rows(i, carry):
        at = pl.multiple_of(i * step, step)
        d = damp_ref[pl.ds(pl.multiple_of(start + at, step), step), :]
        filt_ref[pl.ds(at, step), :] = jnp.exp(-(d * ksq)) * scale
        return carry

    lax.fori_loop(0, half // step, rows, 0)
    w_in_t_ref[...] = w_in_ref[:, pl.ds(start, half)].T


def start_phase(rows_ref, kmat_ref, kone_ref, turn_ref, same_ref):
    first = rows_ref.shape[1] - META
    meta = rows_ref[:, first:]
    turn_ref[...] = dot(meta, kmat_ref[...], 1, 0)
    lane = lax.broadcasted_iota(jnp.int32, meta.shape, 1).astype(F32)
    one = jnp.where(meta.astype(F32)[:, 3:4] == lane, 1.0, 0.0).astype(BF)
    same_ref[...] = dot(one, kone_ref[...], 1, 0)


def phase_tile(turn_ref, same_ref, phase_ref, at, first, count):
    span = slice(first, first + count)
    kcount = turn_ref.shape[1]
    turn = turn_ref[at, span]
    same = same_ref[at, span]
    rest = turn - jnp.floor(turn + 0.5)
    square = rest * rest
    cosine = square * COS_POLY[-1] + COS_POLY[-2]
    for c in COS_POLY[-3::-1]:
        cosine = cosine * square + c
    sine = square * SIN_POLY[-1] + SIN_POLY[-2]
    for c in SIN_POLY[-3::-1]:
        sine = sine * square + c
    sine = sine * rest
    held = sine * same
    phase_ref[at, span] = (same - held * sine).astype(BF)
    phase_ref[at, kcount + first : kcount + first + count] = (held * cosine).astype(BF)


def fill_stack(rows_ref, w_in_t_ref, w_out_half, stack_ref):
    half = w_in_t_ref.shape[0]
    width = w_in_t_ref.shape[1]
    stack_ref[0:half, :] = dot(w_in_t_ref[...], rows_ref[:, 0:width], 1, 1).astype(BF)
    stack_ref[half:, :] = dot(w_out_half, rows_ref[:, width : 2 * width], 1, 1).astype(BF)


def half_of(ref, shard_ref, half):
    return ref[pl.ds(pl.multiple_of(shard_ref[0] * half, half), half), :]


def own_kernel(
    shard_ref, own_ref, kmat_ref, kone_ref, w_in_t_ref, w_out_ref, phase_ref, stack_ref, part_ref,
    turn_ref, same_ref,
):
    start_phase(own_ref, kmat_ref, kone_ref, turn_ref, same_ref)
    fill_stack(own_ref, w_in_t_ref, half_of(w_out_ref, shard_ref, w_in_t_ref.shape[0]), stack_ref)
    slots, kcount = turn_ref.shape
    chunk = 256

    def structure(first):
        for at in (first, kcount + first):
            span = slice(at, at + chunk)
            part_ref[:, span] = dot(stack_ref[...], phase_ref[:, span], 1, 0)

    for first in range(0, kcount, chunk):
        if first:
            structure(first - chunk)
        for row in range(0, slots, 16):
            phase_tile(turn_ref, same_ref, phase_ref, slice(row, row + 16), first, chunk)
    structure(kcount - chunk)


def forward_kernel(
    shard_ref, oth_ref, part_ref, phase_own_ref, kmat_ref, kone_ref, filt_ref, w_in_t_ref,
    w_out_ref,
    phase_ref, stack_ref, msg_own_ref, msg_oth_ref,
    turn_ref, same_ref, scaled_ref, scale_m,
):
    half = w_in_t_ref.shape[0]
    fill_stack(oth_ref, w_in_t_ref, half_of(w_out_ref, shard_ref, half), stack_ref)
    start_phase(oth_ref, kmat_ref, kone_ref, turn_ref, same_ref)
    slots, kcount = turn_ref.shape
    chunk = 512

    def structure(first):
        filt = filt_ref[:, first : first + chunk]
        for at in (first, kcount + first):
            span = slice(at, at + chunk)
            total = part_ref[0:half, span] + dot(stack_ref[0:half, :], phase_ref[:, span], 1, 0)
            scaled_ref[:, span] = (total * filt).astype(BF)

    for first in range(0, kcount, chunk):
        if first:
            structure(first - chunk)
        for row in range(0, slots, 16):
            phase_tile(turn_ref, same_ref, phase_ref, slice(row, row + 16), first, chunk)
    structure(kcount - chunk)
    for phase, out in ((phase_own_ref, msg_own_ref), (phase_ref, msg_oth_ref)):
        out[...] = (scale_m * dot(scaled_ref[...], phase[...], 1, 1)).astype(BF)


def backward_kernel(
    own_ref, oth_ref, part_ref, phase_own_ref, phase_oth_ref, stack_ref, msg_own_ref, msg_oth_ref,
    filt_ref, grad_ref, scaled_ref, scale_m,
):
    half = msg_own_ref.shape[0]
    width = grad_ref.shape[1]
    kcount = filt_ref.shape[1]
    chunk = 512
    for at in range(0, 2 * kcount, chunk):
        span = slice(at, at + chunk)
        filt = filt_ref[:, at % kcount : at % kcount + chunk]
        total = part_ref[half:, span] + dot(stack_ref[half:, :], phase_oth_ref[:, span], 1, 0)
        scaled_ref[:, span] = (total * filt).astype(BF)
    total = dot(msg_own_ref[...], own_ref[:, width : 2 * width], 1, 0)
    total += dot(msg_oth_ref[...], oth_ref[:, width : 2 * width], 1, 0)
    grad_ref[0:half, :] = total.astype(BF)
    back_own = (scale_m * dot(scaled_ref[...], phase_own_ref[...], 1, 1)).astype(BF)
    back_oth = (scale_m * dot(scaled_ref[...], phase_oth_ref[...], 1, 1)).astype(BF)
    total = dot(back_own, own_ref[:, 0:width], 1, 0)
    total += dot(back_oth, oth_ref[:, 0:width], 1, 0)
    grad_ref[half:, :] = total.astype(BF)


def change_kernel(shard_ref, msg_ref, got_ref, w_out_ref, grad_ref, out_ref):
    half = msg_ref.shape[0]
    mine = pl.multiple_of(shard_ref[0] * half, half)
    other = pl.multiple_of((1 - shard_ref[0]) * half, half)
    change = dot(msg_ref[...], w_out_ref[pl.ds(mine, half), :], 0, 0)
    change += dot(got_ref[...], w_out_ref[pl.ds(other, half), :], 0, 0)
    change = change.astype(BF)
    step = half // PLANE
    for q in range(PLANE):
        out_ref[q, 0:step] = change[q * step : (q + 1) * step]
        out_ref[q, step : 2 * step] = grad_ref[q * step : (q + 1) * step]
        out_ref[q, 2 * step :] = grad_ref[half + q * step : half + (q + 1) * step]


def plane_sum_kernel(recv_ref, out_ref):
    planes, block = out_ref.shape[0], recv_ref.shape[1] // 3
    slots = PLANE * block
    change = jnp.concatenate([recv_ref[q, 0:block] for q in range(PLANE)], axis=0)
    to = lax.broadcasted_iota(jnp.int32, (slots, slots), 0)
    of = lax.broadcasted_iota(jnp.int32, (slots, slots), 1)
    width = 2 * PLANE
    source = ((to & 31) >> 1) * block + (to >> 5) * 2 + (to & 1)
    move = jnp.where(source == of, 1.0, 0.0).astype(BF)
    change = dot(move, change, 1, 0).astype(BF)
    total = recv_ref[0, block:].astype(F32)
    for q in range(1, PLANE):
        total += recv_ref[q, block:].astype(F32)
    total = total.astype(BF)
    for z in range(planes):
        out_ref[z, 0:width] = change[z * width : (z + 1) * width]
        out_ref[z, width:] = total


def column_sum_kernel(recv_ref, out_ref, norm_factor):
    first = recv_ref.shape[1] - out_ref.shape[1]
    total = recv_ref[0, first:].astype(F32)
    for z in range(1, recv_ref.shape[0]):
        total += recv_ref[z, first:].astype(F32)
    total = (total * norm_factor).astype(BF)
    for q in range(out_ref.shape[0]):
        out_ref[q] = total


def place_half(ref, member, grad_in_hbm, grad_out_hbm, in_ref, out_ref, sems):
    block = ref.shape[1] // 2
    half = PLANE * block
    start = pl.multiple_of(member * half, half)
    copies = []

    def send(src, dst):
        copies.append(pltpu.make_async_copy(src, dst, sems.at[len(copies)]))
        copies[-1].start()

    for first in range(0, PLANE, 8):
        for q in range(first, first + 8):
            out_ref[q * block : (q + 1) * block, :] = ref[q, 0:block].astype(F32)
        at = pl.ds(pl.multiple_of(start + first * block, 8 * block), 8 * block)
        send(out_ref.at[first * block : (first + 8) * block, :], grad_out_hbm.at[at, :])
    into = jnp.concatenate([ref[q, block:] for q in range(PLANE)], axis=0)
    for first in range(0, into.shape[1], 128):
        span = slice(first, first + 128)
        in_ref[span, :] = into[:, span].astype(F32).T
        send(in_ref.at[span, :], grad_in_hbm.at[span, pl.ds(start, half)])
    return copies


def own_final_kernel(
    shard_ref, feat_ref, recv_ref, own_ref, half_ref,
    new_hbm, grad_in_hbm, grad_out_hbm,
    in_ref, out_ref, sems, new_ref, new_sem,
):
    copies = place_half(half_ref, shard_ref[0], grad_in_hbm, grad_out_hbm, in_ref, out_ref, sems)
    rows = feat_ref.shape[0]
    planes = recv_ref.shape[0]
    width = 2 * PLANE
    owner_row = own_ref[...].astype(F32)
    owner = as_column(owner_row)
    first = lax.broadcasted_iota(jnp.int32, (rows, rows), 0)
    second = lax.broadcasted_iota(jnp.int32, (rows, rows), 1)
    earlier = (owner == owner_row) & (second < first)
    rank = jnp.sum(jnp.where(earlier, 1.0, 0.0), axis=1, keepdims=True)
    first, second = place_of(owner.astype(jnp.int32), shard_ref[0])
    slot = (second * PLANE + first) * 2 + rank.astype(jnp.int32)
    pick = jnp.where(
        slot == lax.broadcasted_iota(jnp.int32, (rows, planes * width), 1), 1.0, 0.0
    ).astype(BF)
    change = jnp.concatenate([recv_ref[z, 0:width] for z in range(planes)], axis=0)
    new_ref[...] = (feat_ref[...].astype(F32) + dot(pick, change, 1, 0)).astype(BF)
    new = pltpu.make_async_copy(new_ref, new_hbm, new_sem)
    new.start()
    for copy in (*copies, new):
        copy.wait()


def other_final_kernel(
    shard_ref, half_ref, _grad_in, _grad_out, grad_in_hbm, grad_out_hbm, in_ref, out_ref, sems
):
    for copy in place_half(
        half_ref, 1 - shard_ref[0], grad_in_hbm, grad_out_hbm, in_ref, out_ref, sems
    ):
        copy.wait()


def local(
    features,
    norm_gain,
    w_in,
    w_out,
    cotangent,
    positions,
    crystal_of_atom,
    atom_owner,
    k_index,
    k_crystal,
    damping,
):
    rows, width = features.shape
    around, plane, column_set = hop_sets()
    groups = lax.axis_size("dp")
    planes = groups // PLANE
    members = lax.axis_size("shard")
    capacity = 2 * rows // groups
    slots = groups * capacity
    half = width // members
    kcount = k_index.shape[1]
    scale_s = (slots * members / CRY_DEV) ** (-0.5)
    scale_m = (kcount / CRY_DEV) ** (-0.5)
    norm_factor = (rows * groups * members) ** (-0.5)
    shard = lax.axis_index("shard").astype(jnp.int32).reshape(1)
    swap = [(0, 1), (1, 0)]

    owner_row = atom_owner.reshape(1, rows)
    packed = 2 * width + META
    operands = [
        shard,
        features,
        norm_gain.reshape(1, width),
        cotangent,
        positions,
        crystal_of_atom.reshape(1, rows),
        owner_row,
    ]
    send = call(
        prep_kernel,
        jax.ShapeDtypeStruct((groups, capacity, packed), BF),
        operands,
        scratch=[pltpu.VMEM(a.shape, a.dtype) for a in operands[1:]]
        + [
            pltpu.SemaphoreType.DMA((len(operands) - 1,)),
            pltpu.VMEM((groups, capacity, packed), BF),
            pltpu.SemaphoreType.DMA((3,)),
        ],
        specs=[SM] + [HB] * (len(operands) - 1),
        outs=HB,
        limit=FULL_VMEM,
    )
    recv = exchange(send, around)
    own = recv.reshape(slots, packed)
    kmat, kone, filt, w_in_t = call(
        functools.partial(static_kernel, scale_s=scale_s),
        (
            jax.ShapeDtypeStruct((META, kcount), BF),
            jax.ShapeDtypeStruct((META, kcount), BF),
            jax.ShapeDtypeStruct((half, kcount), F32),
            jax.ShapeDtypeStruct((half, width), BF),
        ),
        [shard, k_index, k_crystal.reshape(1, kcount), damping.reshape(width, 1), w_in],
        specs=[SM, VM, VM, VM, VM],
        flops=4_000_000_000,
    )
    own, kmat, kone, filt, w_in_t = lax.optimization_barrier((own, kmat, kone, filt, w_in_t))
    other = lax.ppermute(own, "shard", swap)
    phase_shape = jax.ShapeDtypeStruct((slots, 2 * kcount), BF)
    stack_shape = jax.ShapeDtypeStruct((2 * half, slots), BF)
    message_shape = jax.ShapeDtypeStruct((half, slots), BF)
    turn = pltpu.VMEM((slots, kcount), F32)
    scaled = pltpu.VMEM((half, 2 * kcount), BF)
    phase_own, _, part = call(
        own_kernel,
        (phase_shape, stack_shape, jax.ShapeDtypeStruct((2 * half, 2 * kcount), F32)),
        [shard, own, kmat, kone, w_in_t, w_out],
        scratch=[turn, turn],
        specs=[SM] + [VM] * 5,
        flops=4_000_000_000,
    )
    phase_oth, stack_oth, message, message_oth = call(
        functools.partial(forward_kernel, scale_m=scale_m),
        (phase_shape, stack_shape, message_shape, message_shape),
        [shard, other, part, phase_own, kmat, kone, filt, w_in_t, w_out],
        scratch=[turn, turn, scaled],
        specs=[SM] + [VM] * 8,
    )
    got = lax.ppermute(message_oth, "shard", swap)
    grads = call(
        functools.partial(backward_kernel, scale_m=scale_m),
        jax.ShapeDtypeStruct((2 * half, width), BF),
        [own, other, part, phase_own, phase_oth, stack_oth, message, message_oth, filt],
        scratch=[scaled],
        flops=4_000_000_000,
    )
    block = slots // PLANE
    back = call(
        change_kernel,
        jax.ShapeDtypeStruct((PLANE, 3 * block, width), BF),
        [shard, message, got, w_out, grads],
        specs=[SM] + [VM] * 4,
    )
    recv_plane = exchange(back, plane)
    column = call(
        plane_sum_kernel,
        jax.ShapeDtypeStruct((planes, slots // planes + 2 * block, width), BF),
        [recv_plane],
    )
    recv_column = exchange(column, column_set)
    share = call(
        functools.partial(column_sum_kernel, norm_factor=norm_factor),
        jax.ShapeDtypeStruct((PLANE, 2 * block, width), BF),
        [recv_column],
    )
    mine = exchange(share, plane)
    theirs = lax.ppermute(mine, "shard", swap)
    grads = (jax.ShapeDtypeStruct((width, width), F32),) * 2
    placing = [
        pltpu.VMEM((width, half), F32),
        pltpu.VMEM((half, width), F32),
        pltpu.SemaphoreType.DMA((6,)),
    ]
    updated, *first = call(
        own_final_kernel,
        (jax.ShapeDtypeStruct((rows, width), BF), *grads),
        [shard, features, recv_column, owner_row, mine],
        scratch=[*placing, pltpu.VMEM((rows, width), BF), pltpu.SemaphoreType.DMA],
        specs=[SM, VM, VM, VM, VM],
        outs=(HB, HB, HB),
        flops=4_000_000_000,
    )
    grad_w_in, grad_w_out = call(
        other_final_kernel,
        grads,
        [shard, theirs, *first],
        scratch=placing,
        specs=[SM, VM, HB, HB],
        outs=(HB, HB),
        aliases={2: 0, 3: 1},
    )
    return (updated, grad_w_in, grad_w_out)


def solution(mesh):
    every = ("dp", "shard")
    in_specs = (
        P(every, None),
        P(),
        P(),
        P(),
        P(every, None),
        P(None, every),
        P(every),
        P(every, None),
        P(None, "dp"),
        P("dp"),
        P(),
    )
    out_specs = (P(every, None), P(), P())
    return jax.shard_map(local, mesh=mesh, in_specs=in_specs, out_specs=out_specs, check_vma=False)
```

```python
import functools
import math

import jax
import jax.numpy as jnp
from jax import lax
from jax.experimental import pallas as pl
from jax.experimental.pallas import tpu as pltpu
from jax.sharding import PartitionSpec as P

CRY_DEV = 8
BF = jnp.bfloat16
F32 = jnp.float32
VMEM_LIMIT = 24 * 1024 * 1024
FULL_VMEM = 63 * 1024 * 1024
META = 128

COS_POLY = (
    1.4142135381698608,
    -6.978850841522217,
    5.739460468292236,
    -1.883557915687561,
    0.3106880187988281,
)
SIN_POLY = (
    4.442883014678955,
    -7.308245658874512,
    3.606354236602783,
    -0.8461116552352905,
    0.1098245158791542,
)

VM = pl.BlockSpec(memory_space=pltpu.VMEM)
SM = pl.BlockSpec(memory_space=pltpu.SMEM)
HB = pl.BlockSpec(memory_space=pltpu.MemorySpace.HBM)
PLANE = 16


def place_of(owner, shard):
    first = jnp.where(shard == 0, 15 - ((owner & 3) * 4 + 3 - ((owner >> 2) & 3)), 15 - ((owner >> 4) * 2 + (owner & 1)))
    second = jnp.where(shard == 0, 7 - (owner >> 4), 7 - ((owner >> 1) & 7))
    return first, second


def hop_sets():
    every = [(z, x, y) for z in range(8) for x in range(4) for y in range(4)]

    def split(shard):
        if shard == 0:
            return {(15 - (y * 4 + 3 - x), 7 - (z)): (z, x, y) for z, x, y in every}
        return {(15 - (z * 2 + y % 2), 7 - (x * 2 + y // 2)): (z, x, y) for z, x, y in every}

    around, first, second = [], [], []
    for shard in range(2):
        at = {key: ((z * 4 + x) * 4 + y) * 2 + shard for key, (z, x, y) in split(shard).items()}
        around.append([at[i, j] for i in range(PLANE) for j in range(8)])
        first += [[at[i, j] for i in range(PLANE)] for j in range(8)]
        second += [[at[i, j] for j in range(8)] for i in range(PLANE)]
    return around, first, second


def exchange(array, sets):
    return lax.all_to_all(
        array,
        ("dp", "shard"),
        split_axis=0,
        concat_axis=0,
        axis_index_groups=sets,
        tiled=True,
    )


def call(body, out_shape, inputs, scratch=(), specs=None, outs=None, flops=1_000_000, aliases=None,
         limit=VMEM_LIMIT):
    return pl.pallas_call(
        body,
        out_shape=out_shape,
        in_specs=specs if specs is not None else [VM] * len(inputs),
        out_specs=outs if outs is not None else jax.tree.map(lambda _: VM, out_shape),
        scratch_shapes=list(scratch),
        input_output_aliases=aliases or {},
        compiler_params=pltpu.CompilerParams(vmem_limit_bytes=limit),
        cost_estimate=pl.CostEstimate(flops=flops, bytes_accessed=1_000_000, transcendentals=0),
    )(*inputs)


def dot(a, b, ca, cb):
    return lax.dot_general(a, b, (((ca,), (cb,)), ((), ())), preferred_element_type=F32)


def as_column(row):
    n = row.shape[1]
    diagonal = lax.broadcasted_iota(jnp.int32, (n, n), 0) == lax.broadcasted_iota(
        jnp.int32, (n, n), 1
    )
    return jnp.sum(jnp.where(diagonal, row, 0.0), axis=1, keepdims=True)


def prep_kernel(
    shard_ref, feat_hbm, gain_hbm, cot_hbm, pos_hbm, cry_hbm, own_hbm, out_hbm,
    feat_ref, gain_ref, cot_ref, pos_ref, cry_ref, own_ref, sems, stage_ref, out_sems,
):
    sources = (feat_hbm, gain_hbm, cot_hbm, pos_hbm, cry_hbm, own_hbm)
    targets = (feat_ref, gain_ref, cot_ref, pos_ref, cry_ref, own_ref)
    feat_in, gain_in, cot_in, pos_in, cry_in, own_in = copies = [
        pltpu.make_async_copy(src, dst, sems.at[i])
        for i, (src, dst) in enumerate(zip(sources, targets))
    ]
    for i in (5, 2, 0, 1, 3, 4):
        copies[i].start()
    rows, width = feat_ref.shape
    slots = out_hbm.shape[0] * out_hbm.shape[1]
    own_in.wait()
    owner = own_ref[...].astype(F32)
    first = lax.broadcasted_iota(jnp.int32, (rows, rows), 0)
    second = lax.broadcasted_iota(jnp.int32, (rows, rows), 1)
    earlier = (as_column(owner) == owner) & (first < second)
    rank = jnp.sum(jnp.where(earlier, 1.0, 0.0), axis=0, keepdims=True)
    first, second = place_of(own_ref[...], shard_ref[0])
    slot = (first * 8 + second) * 2 + rank.astype(jnp.int32)
    place = jnp.where(
        slot == lax.broadcasted_iota(jnp.int32, (slots, rows), 0), 1.0, 0.0
    ).astype(BF)
    sent = []

    def send(first, part):
        span = slice(first, first + part.shape[1])
        stage_ref[:, :, span] = part.astype(BF).reshape(slots // 2, 2, part.shape[1])
        copy = pltpu.make_async_copy(
            stage_ref.at[:, :, span], out_hbm.at[:, :, span], out_sems.at[len(sent)]
        )
        copy.start()
        sent.append(copy)

    cot_in.wait()
    send(width, dot(place, cot_ref[...], 1, 0))
    feat_in.wait()
    gain_in.wait()
    hidden = feat_ref[...].astype(F32)
    normed = (
        hidden
        * lax.rsqrt(jnp.mean(hidden * hidden, axis=-1, keepdims=True) + 1e-06)
        * gain_ref[...]
    ).astype(BF)
    send(0, dot(place, normed, 1, 0))
    pos_in.wait()
    cry_in.wait()
    meta = jnp.concatenate(
        [
            pos_ref[...].astype(F32),
            cry_ref[...].astype(F32),
            jnp.zeros((META - 4, rows), F32),
        ],
        axis=0,
    ).astype(BF)
    send(2 * width, dot(place, meta, 1, 1))
    for copy in sent:
        copy.wait()


def static_kernel(
    shard_ref, k_ref, kc_ref, damp_ref, w_in_ref, kmat_ref, kone_ref, filt_ref, w_in_t_ref, scale_s
):
    half = filt_ref.shape[0]
    start = pl.multiple_of(shard_ref[0] * half, half)
    kf = k_ref[...].astype(F32)
    kmat_ref[...] = jnp.zeros(kmat_ref.shape, BF)
    kmat_ref[0:16, :] = jnp.concatenate([kf, jnp.zeros((13, kf.shape[1]), F32)], axis=0).astype(BF)
    crystal = lax.broadcasted_iota(jnp.int32, kone_ref.shape, 0)
    kone_ref[...] = jnp.where(kc_ref[...] == crystal, 1.0, 0.0).astype(BF)
    ksq = kf[0:1] * kf[0:1] + kf[1:2] * kf[1:2] + kf[2:3] * kf[2:3]
    scale = scale_s / (1.0 + ksq)
    step = 32

    def rows(i, carry):
        at = pl.multiple_of(i * step, step)
        d = damp_ref[pl.ds(pl.multiple_of(start + at, step), step), :]
        filt_ref[pl.ds(at, step), :] = jnp.exp(-(d * ksq)) * scale
        return carry

    lax.fori_loop(0, half // step, rows, 0)
    w_in_t_ref[...] = w_in_ref[:, pl.ds(start, half)].T


def start_phase(rows_ref, kmat_ref, kone_ref, turn_ref, same_ref):
    first = rows_ref.shape[1] - META
    meta = rows_ref[:, first:]
    turn_ref[...] = dot(meta, kmat_ref[...], 1, 0)
    lane = lax.broadcasted_iota(jnp.int32, meta.shape, 1).astype(F32)
    one = jnp.where(meta.astype(F32)[:, 3:4] == lane, 1.0, 0.0).astype(BF)
    same_ref[...] = dot(one, kone_ref[...], 1, 0)


def phase_tile(turn_ref, same_ref, phase_ref, at, first, count):
    span = slice(first, first + count)
    kcount = turn_ref.shape[1]
    turn = turn_ref[at, span]
    same = same_ref[at, span]
    rest = turn - jnp.floor(turn + 0.5)
    square = rest * rest
    cosine = square * COS_POLY[-1] + COS_POLY[-2]
    for c in COS_POLY[-3::-1]:
        cosine = cosine * square + c
    sine = square * SIN_POLY[-1] + SIN_POLY[-2]
    for c in SIN_POLY[-3::-1]:
        sine = sine * square + c
    sine = sine * rest
    held = sine * same
    phase_ref[at, span] = (same - held * sine).astype(BF)
    phase_ref[at, kcount + first : kcount + first + count] = (held * cosine).astype(BF)


def fill_stack(rows_ref, w_in_t_ref, w_out_half, stack_ref):
    half = w_in_t_ref.shape[0]
    width = w_in_t_ref.shape[1]
    stack_ref[0:half, :] = dot(w_in_t_ref[...], rows_ref[:, 0:width], 1, 1).astype(BF)
    stack_ref[half:, :] = dot(w_out_half, rows_ref[:, width : 2 * width], 1, 1).astype(BF)


def half_of(ref, shard_ref, half):
    return ref[pl.ds(pl.multiple_of(shard_ref[0] * half, half), half), :]


def own_kernel(
    shard_ref, own_ref, kmat_ref, kone_ref, w_in_t_ref, w_out_ref, phase_ref, stack_ref, part_ref,
    turn_ref, same_ref,
):
    start_phase(own_ref, kmat_ref, kone_ref, turn_ref, same_ref)
    fill_stack(own_ref, w_in_t_ref, half_of(w_out_ref, shard_ref, w_in_t_ref.shape[0]), stack_ref)
    slots, kcount = turn_ref.shape
    chunk = 256

    def structure(first):
        for at in (first, kcount + first):
            span = slice(at, at + chunk)
            part_ref[:, span] = dot(stack_ref[...], phase_ref[:, span], 1, 0)

    for first in range(0, kcount, chunk):
        if first:
            structure(first - chunk)
        for row in range(0, slots, 16):
            phase_tile(turn_ref, same_ref, phase_ref, slice(row, row + 16), first, chunk)
    structure(kcount - chunk)


def forward_kernel(
    shard_ref, oth_ref, part_ref, phase_own_ref, kmat_ref, kone_ref, filt_ref, w_in_t_ref,
    w_out_ref,
    phase_ref, stack_ref, msg_own_ref, msg_oth_ref,
    turn_ref, same_ref, scaled_ref, scale_m,
):
    half = w_in_t_ref.shape[0]
    fill_stack(oth_ref, w_in_t_ref, half_of(w_out_ref, shard_ref, half), stack_ref)
    start_phase(oth_ref, kmat_ref, kone_ref, turn_ref, same_ref)
    slots, kcount = turn_ref.shape
    chunk = 512

    def structure(first):
        filt = filt_ref[:, first : first + chunk]
        for at in (first, kcount + first):
            span = slice(at, at + chunk)
            total = part_ref[0:half, span] + dot(stack_ref[0:half, :], phase_ref[:, span], 1, 0)
            scaled_ref[:, span] = (total * filt).astype(BF)

    for first in range(0, kcount, chunk):
        if first:
            structure(first - chunk)
        for row in range(0, slots, 16):
            phase_tile(turn_ref, same_ref, phase_ref, slice(row, row + 16), first, chunk)
    structure(kcount - chunk)
    for phase, out in ((phase_own_ref, msg_own_ref), (phase_ref, msg_oth_ref)):
        out[...] = (scale_m * dot(scaled_ref[...], phase[...], 1, 1)).astype(BF)


def backward_kernel(
    own_ref, oth_ref, part_ref, phase_own_ref, phase_oth_ref, stack_ref, msg_own_ref, msg_oth_ref,
    filt_ref, grad_ref, scaled_ref, scale_m,
):
    half = msg_own_ref.shape[0]
    width = grad_ref.shape[1]
    kcount = filt_ref.shape[1]
    chunk = 512
    for at in range(0, 2 * kcount, chunk):
        span = slice(at, at + chunk)
        filt = filt_ref[:, at % kcount : at % kcount + chunk]
        total = part_ref[half:, span] + dot(stack_ref[half:, :], phase_oth_ref[:, span], 1, 0)
        scaled_ref[:, span] = (total * filt).astype(BF)
    total = dot(msg_own_ref[...], own_ref[:, width : 2 * width], 1, 0)
    total += dot(msg_oth_ref[...], oth_ref[:, width : 2 * width], 1, 0)
    grad_ref[0:half, :] = total.astype(BF)
    back_own = (scale_m * dot(scaled_ref[...], phase_own_ref[...], 1, 1)).astype(BF)
    back_oth = (scale_m * dot(scaled_ref[...], phase_oth_ref[...], 1, 1)).astype(BF)
    total = dot(back_own, own_ref[:, 0:width], 1, 0)
    total += dot(back_oth, oth_ref[:, 0:width], 1, 0)
    grad_ref[half:, :] = total.astype(BF)


def change_kernel(shard_ref, msg_ref, got_ref, w_out_ref, grad_ref, out_ref):
    half = msg_ref.shape[0]
    mine = pl.multiple_of(shard_ref[0] * half, half)
    other = pl.multiple_of((1 - shard_ref[0]) * half, half)
    change = dot(msg_ref[...], w_out_ref[pl.ds(mine, half), :], 0, 0)
    change += dot(got_ref[...], w_out_ref[pl.ds(other, half), :], 0, 0)
    change = change.astype(BF)
    step = half // PLANE
    for q in range(PLANE):
        out_ref[q, 0:step] = change[q * step : (q + 1) * step]
        out_ref[q, step : 2 * step] = grad_ref[q * step : (q + 1) * step]
        out_ref[q, 2 * step :] = grad_ref[half + q * step : half + (q + 1) * step]


def plane_sum_kernel(recv_ref, out_ref):
    planes, block = out_ref.shape[0], recv_ref.shape[1] // 3
    slots = PLANE * block
    change = jnp.concatenate([recv_ref[q, 0:block] for q in range(PLANE)], axis=0)
    to = lax.broadcasted_iota(jnp.int32, (slots, slots), 0)
    of = lax.broadcasted_iota(jnp.int32, (slots, slots), 1)
    width = 2 * PLANE
    source = ((to & 31) >> 1) * block + (to >> 5) * 2 + (to & 1)
    move = jnp.where(source == of, 1.0, 0.0).astype(BF)
    change = dot(move, change, 1, 0).astype(BF)
    total = recv_ref[0, block:].astype(F32)
    for q in range(1, PLANE):
        total += recv_ref[q, block:].astype(F32)
    total = total.astype(BF)
    for z in range(planes):
        out_ref[z, 0:width] = change[z * width : (z + 1) * width]
        out_ref[z, width:] = total


def column_sum_kernel(recv_ref, out_ref, norm_factor):
    first = recv_ref.shape[1] - out_ref.shape[1]
    total = recv_ref[0, first:].astype(F32)
    for z in range(1, recv_ref.shape[0]):
        total += recv_ref[z, first:].astype(F32)
    total = (total * norm_factor).astype(BF)
    for q in range(out_ref.shape[0]):
        out_ref[q] = total


def place_half(ref, member, grad_in_hbm, grad_out_hbm, in_ref, out_ref, sems):
    block = ref.shape[1] // 2
    half = PLANE * block
    start = pl.multiple_of(member * half, half)
    copies = []

    def send(src, dst):
        copies.append(pltpu.make_async_copy(src, dst, sems.at[len(copies)]))
        copies[-1].start()

    for first in range(0, PLANE, 8):
        for q in range(first, first + 8):
            out_ref[q * block : (q + 1) * block, :] = ref[q, 0:block].astype(F32)
        at = pl.ds(pl.multiple_of(start + first * block, 8 * block), 8 * block)
        send(out_ref.at[first * block : (first + 8) * block, :], grad_out_hbm.at[at, :])
    into = jnp.concatenate([ref[q, block:] for q in range(PLANE)], axis=0)
    for first in range(0, into.shape[1], 128):
        span = slice(first, first + 128)
        in_ref[span, :] = into[:, span].astype(F32).T
        send(in_ref.at[span, :], grad_in_hbm.at[span, pl.ds(start, half)])
    return copies


def own_final_kernel(
    shard_ref, feat_ref, recv_ref, own_ref, half_ref,
    new_hbm, grad_in_hbm, grad_out_hbm,
    in_ref, out_ref, sems, new_ref, new_sem,
):
    copies = place_half(half_ref, shard_ref[0], grad_in_hbm, grad_out_hbm, in_ref, out_ref, sems)
    rows = feat_ref.shape[0]
    planes = recv_ref.shape[0]
    width = 2 * PLANE
    owner_row = own_ref[...].astype(F32)
    owner = as_column(owner_row)
    first = lax.broadcasted_iota(jnp.int32, (rows, rows), 0)
    second = lax.broadcasted_iota(jnp.int32, (rows, rows), 1)
    earlier = (owner == owner_row) & (second < first)
    rank = jnp.sum(jnp.where(earlier, 1.0, 0.0), axis=1, keepdims=True)
    first, second = place_of(owner.astype(jnp.int32), shard_ref[0])
    slot = (second * PLANE + first) * 2 + rank.astype(jnp.int32)
    pick = jnp.where(
        slot == lax.broadcasted_iota(jnp.int32, (rows, planes * width), 1), 1.0, 0.0
    ).astype(BF)
    change = jnp.concatenate([recv_ref[z, 0:width] for z in range(planes)], axis=0)
    new_ref[...] = (feat_ref[...].astype(F32) + dot(pick, change, 1, 0)).astype(BF)
    new = pltpu.make_async_copy(new_ref, new_hbm, new_sem)
    new.start()
    for copy in (*copies, new):
        copy.wait()


def other_final_kernel(
    shard_ref, half_ref, _grad_in, _grad_out, grad_in_hbm, grad_out_hbm, in_ref, out_ref, sems
):
    for copy in place_half(
        half_ref, 1 - shard_ref[0], grad_in_hbm, grad_out_hbm, in_ref, out_ref, sems
    ):
        copy.wait()


def local(
    features,
    norm_gain,
    w_in,
    w_out,
    cotangent,
    positions,
    crystal_of_atom,
    atom_owner,
    k_index,
    k_crystal,
    damping,
):
    rows, width = features.shape
    around, plane, column_set = hop_sets()
    groups = lax.axis_size("dp")
    planes = groups // PLANE
    members = lax.axis_size("shard")
    capacity = 2 * rows // groups
    slots = groups * capacity
    half = width // members
    kcount = k_index.shape[1]
    scale_s = (slots * members / CRY_DEV) ** (-0.5)
    scale_m = (kcount / CRY_DEV) ** (-0.5)
    norm_factor = (rows * groups * members) ** (-0.5)
    shard = lax.axis_index("shard").astype(jnp.int32).reshape(1)
    swap = [(0, 1), (1, 0)]

    owner_row = atom_owner.reshape(1, rows)
    packed = 2 * width + META
    operands = [
        shard,
        features,
        norm_gain.reshape(1, width),
        cotangent,
        positions,
        crystal_of_atom.reshape(1, rows),
        owner_row,
    ]
    send = call(
        prep_kernel,
        jax.ShapeDtypeStruct((groups, capacity, packed), BF),
        operands,
        scratch=[pltpu.VMEM(a.shape, a.dtype) for a in operands[1:]]
        + [
            pltpu.SemaphoreType.DMA((len(operands) - 1,)),
            pltpu.VMEM((groups, capacity, packed), BF),
            pltpu.SemaphoreType.DMA((3,)),
        ],
        specs=[SM] + [HB] * (len(operands) - 1),
        outs=HB,
        limit=FULL_VMEM,
    )
    recv = exchange(send, around)
    own = recv.reshape(slots, packed)
    kmat, kone, filt, w_in_t = call(
        functools.partial(static_kernel, scale_s=scale_s),
        (
            jax.ShapeDtypeStruct((META, kcount), BF),
            jax.ShapeDtypeStruct((META, kcount), BF),
            jax.ShapeDtypeStruct((half, kcount), F32),
            jax.ShapeDtypeStruct((half, width), BF),
        ),
        [shard, k_index, k_crystal.reshape(1, kcount), damping.reshape(width, 1), w_in],
        specs=[SM, VM, VM, VM, VM],
        flops=4_000_000_000,
    )
    own, kmat, kone, filt, w_in_t = lax.optimization_barrier((own, kmat, kone, filt, w_in_t))
    other = lax.ppermute(own, "shard", swap)
    phase_shape = jax.ShapeDtypeStruct((slots, 2 * kcount), BF)
    stack_shape = jax.ShapeDtypeStruct((2 * half, slots), BF)
    message_shape = jax.ShapeDtypeStruct((half, slots), BF)
    turn = pltpu.VMEM((slots, kcount), F32)
    scaled = pltpu.VMEM((half, 2 * kcount), BF)
    phase_own, _, part = call(
        own_kernel,
        (phase_shape, stack_shape, jax.ShapeDtypeStruct((2 * half, 2 * kcount), F32)),
        [shard, own, kmat, kone, w_in_t, w_out],
        scratch=[turn, turn],
        specs=[SM] + [VM] * 5,
        flops=4_000_000_000,
    )
    phase_oth, stack_oth, message, message_oth = call(
        functools.partial(forward_kernel, scale_m=scale_m),
        (phase_shape, stack_shape, message_shape, message_shape),
        [shard, other, part, phase_own, kmat, kone, filt, w_in_t, w_out],
        scratch=[turn, turn, scaled],
        specs=[SM] + [VM] * 8,
    )
    got = lax.ppermute(message_oth, "shard", swap)
    grads = call(
        functools.partial(backward_kernel, scale_m=scale_m),
        jax.ShapeDtypeStruct((2 * half, width), BF),
        [own, other, part, phase_own, phase_oth, stack_oth, message, message_oth, filt],
        scratch=[scaled],
        flops=4_000_000_000,
    )
    block = slots // PLANE
    back = call(
        change_kernel,
        jax.ShapeDtypeStruct((PLANE, 3 * block, width), BF),
        [shard, message, got, w_out, grads],
        specs=[SM] + [VM] * 4,
    )
    recv_plane = exchange(back, plane)
    column = call(
        plane_sum_kernel,
        jax.ShapeDtypeStruct((planes, slots // planes + 2 * block, width), BF),
        [recv_plane],
    )
    recv_column = exchange(column, column_set)
    share = call(
        functools.partial(column_sum_kernel, norm_factor=norm_factor),
        jax.ShapeDtypeStruct((PLANE, 2 * block, width), BF),
        [recv_column],
    )
    mine = exchange(share, plane)
    theirs = lax.ppermute(mine, "shard", swap)
    grads = (jax.ShapeDtypeStruct((width, width), F32),) * 2
    placing = [
        pltpu.VMEM((width, half), F32),
        pltpu.VMEM((half, width), F32),
        pltpu.SemaphoreType.DMA((6,)),
    ]
    updated, *first = call(
        own_final_kernel,
        (jax.ShapeDtypeStruct((rows, width), BF), *grads),
        [shard, features, recv_column, owner_row, mine],
        scratch=[*placing, pltpu.VMEM((rows, width), BF), pltpu.SemaphoreType.DMA],
        specs=[SM, VM, VM, VM, VM],
        outs=(HB, HB, HB),
        flops=4_000_000_000,
    )
    grad_w_in, grad_w_out = call(
        other_final_kernel,
        grads,
        [shard, theirs, *first],
        scratch=placing,
        specs=[SM, VM, HB, HB],
        outs=(HB, HB),
        aliases={2: 0, 3: 1},
    )
    return (updated, grad_w_in, grad_w_out)


def solution(mesh):
    every = ("dp", "shard")
    in_specs = (
        P(every, None),
        P(),
        P(),
        P(),
        P(every, None),
        P(None, every),
        P(every),
        P(every, None),
        P(None, "dp"),
        P("dp"),
        P(),
    )
    out_specs = (P(every, None), P(), P())
    return jax.shard_map(local, mesh=mesh, in_specs=in_specs, out_specs=out_specs, check_vma=False)
```
